32 devices in a mesh: groups: 2 (over y), blk: 4 (over z), side: 2 (over x), tp: 2 (over core).
Axes of the slice: x: 2, y: 2, z: 4, core: 2. Of those that a mesh axis runs over, the one named last changes fastest.
Arguments:
- queries: bfloat16 [4, 512, 4096], P(('groups', 'side'), 'blk', 'tp'), parts along dimension 0, may hold values from -8 to 8
- key_rows: bfloat16 [4, 512, 256], P(('groups', 'side'), 'blk', 'tp'), parts along dimension 0, may hold values from -8 to 8
- value_rows: bfloat16 [4, 512, 256], P(('groups', 'side'), 'blk', 'tp'), parts along dimension 0, may hold values from -6 to 6
- segments: int32 [4, 512], P(('groups', 'side'), 'blk'), parts along dimension 0, may hold values from 0 to 1, never falling along the last dimension, each value on 1 to 384 neighbouring positions
- hidden_entry_rows: bfloat16 [4, 512, 4096], P(('groups', 'side'), 'blk', 'tp'), parts along dimension 0, may hold values from -6 to 6
- expert_ids: int32 [4, 512, 8], P(('groups', 'side'), 'blk'), parts along dimension 0, may hold values from 0 to 127, all different within a row; in each aligned block of 128 rows (0 to 127, 128 to 255, ..., all dimensions but the last counted through in order) at most 10 rows name the same one
- route_weight: float32 [4, 512, 8], P(('groups', 'side'), 'blk'), parts along dimension 0, may hold values from 0.2 to 1
- w_gate: bfloat16 [4, 2048, 1536], P('blk', 'tp', 'side'), may hold values from -0.09375 to 0.09375
- w_up: bfloat16 [4, 2048, 1536], P('blk', 'tp', 'side'), may hold values from -0.09375 to 0.09375
- w_down: bfloat16 [4, 1536, 2048], P('blk', 'side', 'tp'), may hold values from -0.15625 to 0.15625
Outputs:
- attended: bfloat16 [4, 512, 4096], P(('groups', 'side'), 'blk', 'tp'), parts along dimension 0
- moe_out: bfloat16 [4, 512, 4096], P(('groups', 'side'), 'blk', 'tp'), parts along dimension 0
The draws below stay inside these ranges and needn't reach their ends.
There are 2 independent parts, one for each index of `groups`. The reference program is written for one: setup_inputs(seed, part) draws one part's arguments, and reference() takes and returns one part's arrays. A program takes and returns all parts, laid end to end along the dimension named above; an argument that names none is the same for every part. Nothing has to cross between parts.
Inputs may be any that keep to these rules, and one draw needn't show every extreme that they name: `expert_ids`: in the 128 rows of one device (aligned blocks of rows of a sequence) no expert is named by more than 10 rows, and in some such block one is named by exactly 10; a row names 8 different experts. `segments`: document numbers never fall along a sequence; a document spans at most 384 positions, and one spans exactly that many.
All inputs are finite; a program needn't handle non-finite values.
Results may differ from the reference program's by a relative error of at most 0.02.
Values may be sent and summed in bfloat16 or wider, within the bound.
No kernel may reach another device: no remote copies, remote signals or barrier semaphores. Data moves between devices by JAX's collectives and lax.ppermute only.
A program may use at most 64 MiB of HBM per device.

```python
import math
import jax
import jax.numpy as jnp
import numpy as np
from jax import lax

D = 4096
FF = 1536
ALL_EXPERTS = 128
TOPK = 8
HEAD_DIM = 128
HEADS = 32
KV_HEADS = 2
TOK_DEV = 128
SEQ_LEN = 512
SEQS = 2
EXPERTS = 2
D_QUARTER = 1024
FF_PART = 768
CAP = 10
DOCS = 2
LONGEST = 384
N_BLK = 4
N_SIDE = 2
N_TP = 2


def paired_draw(key):
    base = jax.random.fold_in(key, 7)
    first, second = jax.random.split(base, 2)
    query_all = jnp.clip(jax.random.normal(first, (SEQS, SEQ_LEN, HEADS, HEAD_DIM), jnp.float32), -6.0, 6.0)
    key_all = jnp.clip(jax.random.normal(second, (SEQS, SEQ_LEN, KV_HEADS, HEAD_DIM), jnp.float32), -6.0, 6.0)
    return (query_all.reshape(SEQS, SEQ_LEN, HEADS * HEAD_DIM), key_all.reshape(SEQS, SEQ_LEN, KV_HEADS * HEAD_DIM))


def draw_queries(key, part):
    return paired_draw(key)[0].astype(jnp.bfloat16)


def draw_key_rows(key, part):
    return paired_draw(key)[1].astype(jnp.bfloat16)


def block_scale(key, shape, shards, least, largest):
    gain = 1.0
    for axis_at, shards_of in shards:
        draws = jax.random.uniform(jax.random.fold_in(jax.random.fold_in(key, 6), axis_at), (shards_of,), jnp.float32, least / len(shards), largest / len(shards))
        gain = gain * jnp.repeat(jnp.exp(draws), shape[axis_at] // shards_of).reshape((-1,) + (1,) * (len(shape) - 1 - axis_at))
    return gain


def split_up(amount, total, limit, slope):
    weights = [(1 << 20) // math.isqrt(rank ** slope) + 1 for rank in range(2, amount + 1)]
    spare, given = total - limit - (amount - 1), [1] * (amount - 1)
    while spare > 0:
        candidates = [i for i in range(amount - 1) if given[i] < limit]
        whole, budget = sum([weights[i] for i in candidates]), spare
        for i in candidates:
            more = min(limit - given[i], max(1, budget * weights[i] // whole), spare)
            given[i] = given[i] + more
            spare = spare - more
    return np.array([limit] + given)


def uneven(stream_key, amount, total, limit, slope):
    if amount == 2:
        one = jax.random.randint(stream_key, (), max(1, total - limit), min(limit, total - 1) + 1)
        return jnp.stack([one, total - one])
    sizes = jnp.asarray(split_up(amount, total, limit, slope), jnp.int32)
    pairs = (amount - 1) // 2
    source_of, receiver = sizes[1:1 + 2 * pairs:2], sizes[2:2 + 2 * pairs:2]
    slack = jnp.minimum(source_of - 1, limit - receiver)
    passed = jax.random.randint(jax.random.fold_in(stream_key, 1), (pairs,), 0, 1 << 20) % (slack + 1)
    sizes = sizes.at[1:1 + 2 * pairs:2].set(source_of - passed).at[2:2 + 2 * pairs:2].set(receiver + passed)
    return sizes[jax.random.permutation(jax.random.fold_in(stream_key, 2), amount)]


def assign_block(key, own, number, rows, amount, top, most, slope):
    order = jax.random.permutation(key, amount)
    crowded, common = load_shares(amount, rows * top, most, slope, True), load_shares(amount, rows * top, most, slope, False)
    places = jnp.arange(amount)

    def named(lengths, offset_by):
        used = int((lengths > 0).sum())
        fixed = max(1, used // 4)
        shifted = fixed + (places - fixed + offset_by * (used - fixed)) % max(1, amount - fixed)
        return jnp.zeros((amount,), jnp.int32).at[order[jnp.where(places < fixed, places, shifted)]].set(jnp.asarray(lengths, jnp.int32))

    lengths = jnp.where(number % 4 == 0, named(crowded, number // 4), named(common, number - number // 4 - 1))
    mixed = jax.random.permutation(jax.random.fold_in(own, 3), amount)
    donor, receiver = mixed[0:amount // 2 * 2:2], mixed[1:amount // 2 * 2:2]
    slack = jnp.minimum(lengths[donor] - 1, most - lengths[receiver]) // 2
    slack = jnp.where((donor == order[0]) | (receiver == order[0]) | (lengths[receiver] == 0), 0, jnp.maximum(slack, 0))
    shifted = jax.random.randint(jax.random.fold_in(own, 4), (amount // 2,), 0, 1 << 20) % (slack + 1)
    lengths = lengths.at[donor].add(-shifted).at[receiver].add(shifted)
    items = jnp.searchsorted(jnp.cumsum(lengths), jnp.arange(rows * top), side="right").astype(jnp.int32)
    table = items.reshape(top, rows).T
    table = table[jax.random.permutation(jax.random.fold_in(own, 1), rows)]
    offset_by = jax.random.randint(jax.random.fold_in(own, 2), (rows, 1), 0, top)
    return jnp.take_along_axis(table, (jnp.arange(top)[None, :] + offset_by) % top, axis=1)


def load_shares(amount, total, most, lean, full):
    weights = [(1 << 20) // math.isqrt(rank ** lean) + 1 for rank in range(1, amount + 1)]
    largest = most if full else min(most, max(-(-total // amount), total * weights[0] // sum(weights)))
    least = 1 if total - largest >= amount - 1 else 0
    counts, spare = [largest] + [least] * (amount - 1), total - largest - least * (amount - 1)
    while spare > 0:
        movable = [i for i in range(1, amount) if counts[i] < largest] or [i for i in range(1, amount) if counts[i] < most]
        whole, left = sum([weights[i] for i in movable]), spare
        for i in movable:
            extra = min(most - counts[i], max(1, left * weights[i] // whole), spare)
            counts[i] = counts[i] + extra
            spare = spare - extra
    return np.array(counts)


def centred(key, extent, spread, most, cuts=(), kind=jnp.bfloat16):
    factor_of = block_scale(key, extent, cuts, -0.22, 0.18) if cuts else 1.0
    result = jax.random.normal(key, extent, jnp.float32) * spread * factor_of
    return jnp.minimum(jnp.maximum(result, -most), most).astype(kind)


def setup_inputs(seed: int = 0, part: int = 0) -> dict:
    splits = jax.random.split(jax.random.key(seed), 11)
    part_keys = jax.random.split(jax.random.fold_in(splits[10], part), 11)
    queries = draw_queries(jax.random.fold_in(jax.random.fold_in(splits[10], part), 71), part)
    key_rows = draw_key_rows(jax.random.fold_in(jax.random.fold_in(splits[10], part), 71), part)
    value_rows = centred(part_keys[2], (SEQS, SEQ_LEN, KV_HEADS * HEAD_DIM), 1.0, 6.0, ((0, 2), (1, 4), (2, 2)))
    segments = jax.vmap(lambda own: jnp.searchsorted(jnp.cumsum(uneven(own, DOCS, SEQ_LEN, LONGEST, 2)), jnp.arange(SEQ_LEN), side="right"))(jax.random.split(part_keys[3], SEQS)).reshape((SEQS, SEQ_LEN)).astype(jnp.int32)
    hidden_entry_rows = centred(part_keys[4], (SEQS, SEQ_LEN, D), 1.0, 6.0, ((0, 2), (1, 4), (2, 2)))
    expert_ids_keys = jax.random.split(jax.random.fold_in(part_keys[5], 1), SEQS * SEQ_LEN // TOK_DEV)
    expert_ids_turns = jax.random.permutation(jax.random.fold_in(part_keys[5], 3), SEQS * SEQ_LEN // TOK_DEV)
    expert_ids = jax.vmap(lambda own, number: assign_block(jax.random.fold_in(part_keys[5], 2), own, number, TOK_DEV, ALL_EXPERTS, TOPK, CAP, 1))(expert_ids_keys, expert_ids_turns).reshape((SEQS, SEQ_LEN, TOPK))
    route_weight = jnp.clip(0.2 + 0.8 * jax.random.uniform(part_keys[6], (SEQS, SEQ_LEN, TOPK), jnp.float32) ** block_scale(part_keys[6], (SEQS, SEQ_LEN, TOPK), ((0, 2), (1, 4)), -0.2, 0.2), 0.2, 1.0)
    w_gate = centred(splits[7], (2 * EXPERTS, D // 2, FF), D ** -0.5, 0.09375, ((0, 4), (1, 2), (2, 2)))
    w_up = centred(splits[8], (2 * EXPERTS, D // 2, FF), D ** -0.5, 0.09375, ((0, 4), (1, 2), (2, 2)))
    w_down = centred(splits[9], (2 * EXPERTS, FF, D // 2), FF ** -0.5, 0.15625, ((0, 4), (1, 2), (2, 2)))
    return {"queries": queries, "key_rows": key_rows, "value_rows": value_rows, "segments": segments, "hidden_entry_rows": hidden_entry_rows, "expert_ids": expert_ids, "route_weight": route_weight, "w_gate": w_gate, "w_up": w_up, "w_down": w_down}


def attend_sequence(operands):
    query_rows, key_rows, value_rows, segment_ids = operands
    length = query_rows.shape[0]
    group = HEADS // KV_HEADS
    query_portion = query_rows.reshape(length, HEADS, HEAD_DIM)
    key_split = key_rows.reshape(length, KV_HEADS, HEAD_DIM)
    value_split = value_rows.reshape(length, KV_HEADS, HEAD_DIM)
    positions = jnp.arange(length, dtype=jnp.int32)
    allowed = (positions[None, :] <= positions[:, None]) & (segment_ids[None, :] == segment_ids[:, None])
    factor = 1.0 / math.sqrt(HEAD_DIM)

    def one_head(head):
        query_head = lax.dynamic_index_in_dim(query_portion, head, 1, keepdims=False)
        key_head = lax.dynamic_index_in_dim(key_split, head // group, 1, keepdims=False)
        value_head = lax.dynamic_index_in_dim(value_split, head // group, 1, keepdims=False)
        scores = jnp.dot(query_head, key_head.T, preferred_element_type=jnp.float32) * factor
        scores = jnp.where(allowed, scores, -1e+30)
        row_max = lax.optimization_barrier(jnp.max(scores, axis=1, keepdims=True))
        weights = jnp.where(allowed, jnp.exp(scores - row_max), 0.0)
        totals = lax.optimization_barrier(jnp.sum(weights, axis=1, keepdims=True))
        mixed = jnp.dot(weights.astype(jnp.bfloat16), value_head, preferred_element_type=jnp.float32)
        return (mixed / totals).astype(jnp.bfloat16)
    heads_out = lax.map(one_head, jnp.arange(HEADS, dtype=jnp.int32))
    return jnp.transpose(heads_out, (1, 0, 2)).reshape(length, HEADS * HEAD_DIM)

def expert_pair(rows, gate_pair, up_pair, down_weight_couple):
    count = rows.shape[0]
    rows_split = rows.astype(jnp.float32).reshape(count, N_TP, 2, D_QUARTER)
    gate_split = gate_pair.astype(jnp.float32).reshape(2, N_TP, D_QUARTER, FF)
    up_split = up_pair.astype(jnp.float32).reshape(2, N_TP, D_QUARTER, FF)
    gate_terms = jnp.einsum('rtkq,ktqf->rtkf', rows_split, gate_split, precision=lax.Precision.HIGHEST).astype(jnp.bfloat16)
    up_terms = jnp.einsum('rtkq,ktqf->rtkf', rows_split, up_split, precision=lax.Precision.HIGHEST).astype(jnp.bfloat16)
    gate = lax.optimization_barrier(jnp.sum(gate_terms.astype(jnp.float32), axis=(1, 2)))
    up_sum = lax.optimization_barrier(jnp.sum(up_terms.astype(jnp.float32), axis=(1, 2)))
    hidden = (jax.nn.silu(gate) * up_sum).astype(jnp.bfloat16)
    down_split = down_weight_couple.astype(jnp.float32).reshape(2, N_SIDE, FF_PART, N_TP, D_QUARTER)
    hidden_split = hidden.astype(jnp.float32).reshape(count, N_SIDE, FF_PART)
    part_out = jnp.einsum('rjf,kjftq->rjtkq', hidden_split, down_split, precision=lax.Precision.HIGHEST).astype(jnp.bfloat16)
    slot_out = lax.optimization_barrier(jnp.sum(part_out.astype(jnp.float32), axis=1)).astype(jnp.bfloat16)
    return slot_out.reshape(count, D)

def reference(queries, key_rows, value_rows, segments, hidden_entry_rows, expert_ids, route_weight, w_gate, w_up, w_down):
    attended = lax.map(attend_sequence, (queries, key_rows, value_rows, segments))
    count = SEQS * SEQ_LEN
    flat_rows = hidden_entry_rows.reshape(count, D)
    flat_ids = expert_ids.reshape(count, TOPK)
    flat_weights = route_weight.reshape(count, TOPK)
    expert_iota = jnp.arange(EXPERTS, dtype=jnp.int32)
    named = flat_ids[:, :, None] == expert_iota[None, None, :]
    hits = lax.optimization_barrier(jnp.sum(named.astype(jnp.int32), axis=1))
    shares = lax.optimization_barrier(jnp.sum(jnp.where(named, flat_weights[:, :, None], 0.0), axis=1))
    blocked = hits.reshape(count // TOK_DEV, TOK_DEV, EXPERTS)
    ranks = (jnp.cumsum(blocked, axis=1) - blocked).reshape(count, EXPERTS)
    slots_all = SEQS * N_BLK * CAP
    owners = jnp.arange(count, dtype=jnp.int32) // TOK_DEV
    slot_of = jnp.where(hits > 0, owners[:, None] * CAP + ranks, slots_all).astype(jnp.int32)
    padded_rows = jnp.concatenate([flat_rows, jnp.zeros((1, D), flat_rows.dtype)], 0)
    token_iota = jnp.arange(count, dtype=jnp.int32)

    def one_expert(output, expert):
        slot_column = lax.dynamic_index_in_dim(slot_of, expert, 1, keepdims=False)
        share_column = lax.dynamic_index_in_dim(shares, expert, 1, keepdims=False)
        token_of_slot = jnp.full((slots_all + 1,), count, jnp.int32).at[slot_column].set(token_iota)[:slots_all]
        weight_of_slot = jnp.zeros((slots_all + 1,), jnp.float32).at[slot_column].set(share_column)[:slots_all]
        rows = padded_rows[token_of_slot]
        gate_pair = jnp.stack([w_gate[expert], w_gate[expert + EXPERTS]])
        up_pair = jnp.stack([w_up[expert], w_up[expert + EXPERTS]])
        down_weight_couple = jnp.stack([w_down[expert], w_down[expert + EXPERTS]])
        combined = expert_pair(rows, gate_pair, up_pair, down_weight_couple).astype(jnp.float32)
        output = output.at[token_of_slot].add(weight_of_slot[:, None] * combined)
        return (output, None)
    initial_running_sum = jnp.zeros((count + 1, D), jnp.float32)
    total_sum, _ = lax.scan(one_expert, initial_running_sum, expert_iota)
    moe_out = total_sum[:count].astype(jnp.bfloat16).reshape(SEQS, SEQ_LEN, D)
    return (attended, moe_out)
```

```python
import math

import jax
import jax.numpy as jnp
from jax import lax
from jax.experimental import pallas as pl
from jax.experimental.pallas import tpu as pltpu
from jax.sharding import PartitionSpec as P

HEAD_DIM = 128
CAP = 10
BF = jnp.bfloat16
F32 = jnp.float32
VMEM = pl.BlockSpec(memory_space=pltpu.VMEM)


def swapped(value, axis, bit):
    count = lax.axis_size(axis)
    return lax.ppermute(value, axis, [(i, i ^ bit) for i in range(count)])


def up_to(value, step):
    return -(-value // step) * step


def call(kernel, outs, *ins, scratch=(), flops=0, exps=0):
    moved = sum(math.prod(a.shape) * a.dtype.itemsize for a in (*ins, *outs))
    held = sum(math.prod(s.shape) * s.dtype.itemsize for s in scratch)
    return pl.pallas_call(
        kernel,
        out_shape=list(outs),
        in_specs=[VMEM] * len(ins),
        out_specs=[VMEM] * len(outs),
        scratch_shapes=list(scratch),
        compiler_params=pltpu.CompilerParams(vmem_limit_bytes=2 * moved + held + (2 << 20)),
        cost_estimate=pl.CostEstimate(flops=flops, bytes_accessed=moved, transcendentals=exps),
    )(*ins)


def shaped(rows, columns, dtype=BF):
    return jax.ShapeDtypeStruct((rows, columns), dtype)


def dot(a, b):
    return jnp.dot(a, b, preferred_element_type=F32)


def dot_rows(a, b):
    return lax.dot_general(a, b, (((0,), (0,)), ((), ())), preferred_element_type=F32)


def mover(rows_out, rows_in, pieces):
    i = lax.broadcasted_iota(jnp.int32, (rows_out, rows_in), 0)
    j = lax.broadcasted_iota(jnp.int32, (rows_out, rows_in), 1)
    hit = jnp.zeros((rows_out, rows_in), jnp.bool_)
    for to, start in pieces:
        hit = hit | ((j - i == start - to) & (i >= to) & (i < to + CAP))
    return jnp.where(hit, 1.0, 0.0).astype(BF)


class Plan:
    def __init__(self, count):
        self.count, self.experts = count, count // 2
        self.bits = [1 << i for i in range(count.bit_length() - 1)]
        keep = [(0, d) for d in range(count) if not d & self.bits[0]]
        send = [(0, d) for d in range(count) if d & self.bits[0]]
        self.first_keep, self.first_send = keep, send
        self.there = []
        for bit, later in zip(self.bits, self.bits[1:] + [None]):
            received = [(s ^ bit, d ^ bit) for s, d in send]
            pool = [(0, i, g) for i, g in enumerate(keep)] + [(1, i, g) for i, g in enumerate(received)]
            keep, send = [], []
            stage = ([], [])
            for which, place, group in pool:
                goes = later is not None and bool(group[1] & later)
                target = send if goes else keep
                stage[goes].append((which, len(target) * CAP, place * CAP))
                target.append(group)
            self.there.append(stage)
        self.sources = [s for s, _ in keep]
        self.back = []
        groups = [(s, 0) for s in self.sources]
        pool = [(0, i, g) for i, g in enumerate(groups)]
        for bit in reversed(self.bits):
            keep, send = [], []
            stage = ([], [])
            for which, place, group in pool:
                goes = bool(group[0] & bit)
                target = send if goes else keep
                stage[goes].append((which, len(target) * CAP, place * CAP))
                target.append(group)
            self.back.append(stage)
            received = [(s ^ bit, d ^ bit) for s, d in send]
            pool = [(0, i, g) for i, g in enumerate(keep)] + [(1, i, g) for i, g in enumerate(received)]
        self.last_keep, self.last_received = keep, received


def picked(ids, weight, groups, columns, here, experts):
    length = ids.shape[0]
    column = lax.broadcasted_iota(jnp.int32, (1, columns), 1)
    wanted = jnp.full((1, columns), -1, jnp.int32)
    level = jnp.zeros((1, columns), jnp.int32)
    for place, (_, target) in enumerate(groups):
        inside = (column >= place * CAP) & (column < (place + 1) * CAP)
        wanted = jnp.where(inside, (here ^ target) & (experts - 1), wanted)
        level = jnp.where(inside, column - place * CAP, level)
    hits = jnp.zeros((length, columns), F32)
    share = jnp.zeros((length, columns), F32)
    for pick in range(ids.shape[1]):
        named = ids[:, pick : pick + 1] == wanted
        hits = hits + jnp.where(named, 1.0, 0.0)
        if weight is not None:
            share = share + jnp.where(named, weight[:, pick : pick + 1], 0.0)
    i = lax.broadcasted_iota(jnp.int32, (length, length), 0)
    j = lax.broadcasted_iota(jnp.int32, (length, length), 1)
    ranks = dot(jnp.where(j < i, 1.0, 0.0).astype(BF), hits.astype(BF))
    chosen = (hits > 0.5) & (jnp.abs(ranks - level.astype(F32)) < 0.5)
    return jnp.where(chosen, 1.0 if weight is None else share, 0.0)


def run_mask(groups, columns, experts, run):
    column = lax.broadcasted_iota(jnp.int32, (1, columns), 1)
    inside = jnp.zeros((1, columns), jnp.bool_)
    for place, (_, target) in enumerate(groups):
        if (target >= experts) == bool(run):
            inside = inside | ((column >= place * CAP) & (column < (place + 1) * CAP))
    return inside


def body(queries, key_rows, value_rows, segments, hidden_entry_rows, expert_ids, route_weight, w_gate, w_up, w_down):
    length = queries.shape[1]
    blocks, sides, cores = lax.axis_size("blk"), lax.axis_size("side"), lax.axis_size("tp")
    plan = Plan(blocks)
    experts = plan.experts
    quarter, ff = w_gate.shape[1], w_gate.shape[2]
    ids, shares = expert_ids[0], route_weight[0]

    def columns_of(run):
        half = (lax.axis_index("blk") // experts) ^ run
        return pl.ds(pl.multiple_of(half * quarter, quarter), quarter)

    first_rows = up_to(max(len(plan.first_keep), len(plan.first_send)) * CAP, 8)

    def choose(ids_ref, x_ref, send_ref, keep_ref):
        here = lax.axis_index("blk")
        for groups, out in ((plan.first_send, send_ref), (plan.first_keep, keep_ref)):
            sel = picked(ids_ref[...], None, groups, first_rows, here, experts)
            total = 0.0
            for run in range(2):
                part = jnp.where(run_mask(groups, first_rows, experts, run), sel, 0.0).astype(BF)
                total = total + dot_rows(part, x_ref[:, columns_of(run)])
            out[...] = total.astype(BF)

    send, keep = call(
        choose,
        [shaped(first_rows, quarter)] * 2,
        ids,
        hidden_entry_rows[0],
        flops=8 * length * first_rows * quarter,
    )

    def sorter(stage, rows, outs):
        def kernel(keep_ref, received_ref, *out_refs):
            for pieces, out in zip(stage, out_refs):
                total = 0.0
                for which, ref in ((0, keep_ref), (1, received_ref)):
                    part = [(to, start) for w, to, start in pieces if w == which]
                    if part:
                        total = total + dot(mover(out.shape[0], ref.shape[0], part), ref[...])
                out[...] = total.astype(BF)

        return kernel

    def sort(stage, keep, received):
        sizes = [up_to(len(pieces) * CAP, 8) for pieces in stage if pieces]
        outs = call(
            sorter(stage, None, None),
            [shaped(size, keep.shape[1]) for size in sizes],
            keep,
            received,
            flops=4 * keep.shape[0] * keep.shape[1] * sum(sizes),
        )
        return outs if len(outs) == 2 else (outs[0], None)

    for bit, stage in zip(plan.bits, plan.there):
        received = swapped(send, "blk", bit)
        keep, send = sort(stage, keep, received)
    rows = keep
    side_rows = rows.shape[0]

    gathered = [rows]
    whole = rows
    bit = 1
    while bit < sides:
        received = swapped(whole, "side", bit)
        gathered.append(received)
        bit *= 2
        if bit < sides:
            whole = jnp.concatenate([whole, received], axis=0)
    if len(gathered) > 2:
        lower, upper = whole, gathered[-1]
    else:
        lower, upper = gathered[0], gathered[1]
    half = lower.shape[0]

    def project(lower_ref, upper_ref, gate_ref, up_ref, send_ref, keep_ref):
        mine = lax.axis_index("tp") == 0
        low, high = lower_ref[...], upper_ref[...]
        away, stay = jnp.where(mine, high, low), jnp.where(mine, low, high)
        both = jnp.concatenate([away, stay], axis=0)
        for at, weight in ((0, gate_ref), (ff, up_ref)):
            terms = dot(both, weight[...])
            send_ref[:, at : at + ff] = terms[:half].astype(BF)
            keep_ref[:, at : at + ff] = terms[half:]

    term_send, term_keep = call(
        project,
        [shaped(half, 2 * ff), shaped(half, 2 * ff, F32)],
        lower,
        upper,
        w_gate[0],
        w_up[0],
        flops=8 * half * quarter * ff,
    )
    term_received = swapped(term_send, "tp", 1)

    moves = []
    for block in range(half // side_rows):
        for place, source in enumerate(plan.sources):
            moves.append((block * side_rows + place * CAP, block * side_rows + plan.sources.index(source ^ experts) * CAP))

    def add_terms(keep_ref, received_ref, sum_ref, send_ref):
        total = keep_ref[...] + received_ref[...].astype(F32)
        sum_ref[...] = total
        send_ref[...] = dot(mover(half, half, moves), total.astype(BF)).astype(BF)

    sums, sums_send = call(
        add_terms,
        [shaped(half, 2 * ff, F32), shaped(half, 2 * ff)],
        term_keep,
        term_received,
        flops=4 * half * half * ff,
    )
    sums_received = swapped(sums_send, "blk", experts)

    def activate(sum_ref, received_ref, hidden_ref):
        gate = sum_ref[:, :ff] + received_ref[:, :ff].astype(F32)
        up = sum_ref[:, ff:] + received_ref[:, ff:].astype(F32)
        hidden_ref[...] = (gate / (1.0 + jnp.exp(-gate)) * up).astype(BF)

    (hidden,) = call(activate, [shaped(half, ff)], sums, sums_received, exps=half * ff)
    hidden_received = swapped(hidden, "tp", 1)

    def project_back(hidden_ref, received_ref, down_ref, low_ref, high_ref):
        mine = lax.axis_index("tp") == 0
        here, there = hidden_ref[...], received_ref[...]
        low, high = jnp.where(mine, here, there), jnp.where(mine, there, here)
        out = dot(jnp.concatenate([low, high], axis=0), down_ref[...])
        low_ref[...] = out[:half]
        high_ref[...] = out[half:].astype(BF)

    low, high = call(
        project_back,
        [shaped(half, quarter, F32), shaped(half, quarter)],
        hidden,
        hidden_received,
        w_down[0],
        flops=4 * half * ff * quarter,
    )

    bit = sides // 2
    received = swapped(high, "side", bit)
    while bit > 1:
        low = low + received.astype(F32)
        bit //= 2
        size = low.shape[0] // 2
        low, high = low[:size], low[size:].astype(BF)
        received = swapped(high, "side", bit)

    def summed_sorter(stage):
        def kernel(keep_ref, received_ref, *out_refs):
            total = (keep_ref[...] + received_ref[...].astype(F32)).astype(BF)
            for pieces, out in zip(stage, out_refs):
                part = [(to, start) for _, to, start in pieces]
                out[...] = dot(mover(out.shape[0], total.shape[0], part), total).astype(BF)

        return kernel

    stage = plan.back[0]
    sizes = [up_to(len(pieces) * CAP, 8) for pieces in stage]
    keep, send = call(
        summed_sorter(stage),
        [shaped(size, quarter) for size in sizes],
        low,
        received,
        flops=2 * side_rows * quarter * sum(sizes),
    )
    for bit, stage in zip(plan.bits[::-1], plan.back[1:]):
        received = swapped(send, "blk", bit)
        keep, send = sort(stage, keep, received)
    received = swapped(send, "blk", plan.bits[0])

    def share_out(ids_ref, weight_ref, keep_ref, received_ref):
        here = lax.axis_index("blk")
        for groups, out in ((plan.last_keep, keep_ref), (plan.last_received, received_ref)):
            out[...] = picked(ids_ref[...], weight_ref[...], groups, first_rows, here, experts)

    keep_share, received_share = call(share_out, [shaped(length, first_rows, F32)] * 2, ids, shares, flops=1000)

    def mix(keep_ref, received_ref, keep_share_ref, received_share_ref, out_ref):
        for run in range(2):
            total = 0.0
            for groups, rows_ref, share_ref in (
                (plan.last_keep, keep_ref, keep_share_ref),
                (plan.last_received, received_ref, received_share_ref),
            ):
                share = jnp.where(run_mask(groups, first_rows, experts, run), share_ref[...], 0.0)
                coarse = share.astype(BF)
                rest = (share - coarse.astype(F32)).astype(BF)
                total = total + dot(coarse, rows_ref[...]) + dot(rest, rows_ref[...])
            out_ref[:, columns_of(run)] = total.astype(BF)

    (moe_out,) = call(
        mix,
        [shaped(length, 2 * quarter)],
        keep,
        received,
        keep_share,
        received_share,
        flops=16 * length * first_rows * quarter,
    )

    labels = jnp.pad(segments.astype(BF), ((0, 15), (0, 0)))
    held = jnp.concatenate([key_rows[0], value_rows[0], labels], axis=0)[None]
    order = [0]
    for bit in plan.bits[::-1]:
        held = jnp.concatenate([held, swapped(held, "blk", bit)], axis=0)
        order = order + [place ^ bit for place in order]
    heads = queries.shape[2] // HEAD_DIM
    factor = 1.0 / math.sqrt(HEAD_DIM)
    span = blocks * length

    def attend(query_ref, held_ref, segment_ref, out_ref, keys, values, bias):
        here = lax.axis_index("blk")
        i = lax.broadcasted_iota(jnp.int32, (length, length), 0)
        j = lax.broadcasted_iota(jnp.int32, (length, length), 1)
        own = jnp.sum(jnp.where(i == j, segment_ref[...].astype(F32), 0.0), axis=1, keepdims=True)
        for place, other in enumerate(order):
            at = place * length
            keys[at : at + length, :] = held_ref[place, :length, :]
            values[at : at + length, :] = held_ref[place, length : 2 * length, :]
            label = held_ref[place, 2 * length : 2 * length + 16, :].astype(F32)[:1]
            same = own == label
            if other == 0:
                seen = same & (j <= i)
            else:
                seen = same & ((here ^ other) < here)
            bias[:, at : at + length] = jnp.where(seen, 0.0, -1e30)

        def one_head(head):
            columns = pl.ds(pl.multiple_of(head * HEAD_DIM, HEAD_DIM), HEAD_DIM)
            scores = lax.dot_general(
                query_ref[:, columns], keys[...], (((1,), (1,)), ((), ())), preferred_element_type=F32
            )
            scores = scores + bias[...]
            top = jnp.max(scores, axis=1, keepdims=True)
            weights = jnp.exp((scores - top) * factor)
            totals = jnp.sum(weights, axis=1, keepdims=True)
            out = dot(weights.astype(BF), values[...])
            out_ref[:, columns] = (out / totals).astype(BF)

        if span <= 1024:
            for head in range(heads):
                one_head(head)
        else:
            lax.fori_loop(0, heads, lambda head, _: (one_head(head), 0)[1], 0)

    (attended,) = call(
        attend,
        [shaped(length, heads * HEAD_DIM)],
        queries[0],
        held,
        segments,
        scratch=[pltpu.VMEM((span, HEAD_DIM), BF)] * 2 + [pltpu.VMEM((length, span), F32)],
        flops=4 * heads * length * span * HEAD_DIM,
        exps=heads * length * span,
    )
    return attended[None], moe_out[None]


def solution(mesh):
    rows = P(("groups", "side"), "blk", "tp")
    placed = (
        rows,
        rows,
        rows,
        P(("groups", "side"), "blk"),
        rows,
        P(("groups", "side"), "blk", None),
        P(("groups", "side"), "blk", None),
        P("blk", "tp", "side"),
        P("blk", "tp", "side"),
        P("blk", "side", "tp"),
    )
    return jax.shard_map(body, mesh=mesh, in_specs=placed, out_specs=(rows, rows), check_vma=False)
```

```python
import math

import jax
import jax.numpy as jnp
from jax import lax
from jax.experimental import pallas as pl
from jax.experimental.pallas import tpu as pltpu
from jax.sharding import PartitionSpec as P

HEAD_DIM = 128
CAP = 10
COST = 3_000_000_000
BF = jnp.bfloat16
F32 = jnp.float32
VMEM = pl.BlockSpec(memory_space=pltpu.VMEM)
HBM = pl.BlockSpec(memory_space=pltpu.HBM)


def swapped(value, axis, bit):
    count = lax.axis_size(axis)
    return lax.ppermute(value, axis, [(i, i ^ bit) for i in range(count)])


def up_to(value, step):
    return -(-value // step) * step


def call(kernel, outs, *ins, scratch=(), semaphores=0, far_in=(), far_out=(), aliases=None, flops=0, exps=0, grant=0):
    moved = sum(math.prod(a.shape) * a.dtype.itemsize for a in (*ins, *outs))
    held = sum(math.prod(s.shape) * s.dtype.itemsize for s in scratch)
    scratch = list(scratch) + ([pltpu.SemaphoreType.DMA((semaphores,))] if semaphores else [])
    return pl.pallas_call(
        kernel,
        out_shape=list(outs),
        in_specs=[HBM if i in far_in else VMEM for i in range(len(ins))],
        out_specs=[HBM if i in far_out else VMEM for i in range(len(outs))],
        scratch_shapes=scratch,
        input_output_aliases=aliases or {},
        compiler_params=pltpu.CompilerParams(vmem_limit_bytes=grant or 2 * moved + held + (2 << 20)),
        cost_estimate=pl.CostEstimate(flops=flops, bytes_accessed=moved, transcendentals=exps),
    )(*ins)


def shaped(rows, columns, dtype=BF):
    return jax.ShapeDtypeStruct((rows, columns), dtype)


def dot(a, b):
    return jnp.dot(a, b, preferred_element_type=F32)


def dot_rows(a, b):
    return lax.dot_general(a, b, (((0,), (0,)), ((), ())), preferred_element_type=F32)


def mover(rows_out, rows_in, pieces):
    i = lax.broadcasted_iota(jnp.int32, (rows_out, rows_in), 0)
    j = lax.broadcasted_iota(jnp.int32, (rows_out, rows_in), 1)
    hit = jnp.zeros((rows_out, rows_in), jnp.bool_)
    for to, start in pieces:
        hit = hit | ((j - i == start - to) & (i >= to) & (i < to + CAP))
    return jnp.where(hit, 1.0, 0.0).astype(BF)


class Plan:
    def __init__(self, count):
        self.count, self.experts = count, count // 2
        self.bits = [1 << i for i in reversed(range(1, count.bit_length() - 1))]
        keep = [(0, d) for d in range(self.experts)]
        send = [(0, d) for d in range(self.experts, count)]
        self.there = []
        for bit, later in zip(self.bits, self.bits[1:] + [1]):
            pool = self.pool(keep, send, bit)
            stage, keep, send = self.split(pool, lambda group: group[1] & later)
            self.there.append(stage)
        near = [s for s, _ in keep]
        self.sources = near + [s ^ 1 for s in near]
        self.back = []
        pool = [(i, j, (s, i)) for i in range(2) for j, s in enumerate(near)]
        for bit in reversed(self.bits):
            stage, keep, send = self.split(pool, lambda group: group[0] & bit)
            self.back.append(stage)
            pool = self.pool(keep, send, bit)
        self.ranked = [d for _, d in keep]

    def pool(self, keep, send, bit):
        received = [(s ^ bit, d ^ bit) for s, d in send]
        return [(0, i, g) for i, g in enumerate(keep)] + [(1, i, g) for i, g in enumerate(received)]

    def split(self, pool, goes):
        stage, groups = ([], []), ([], [])
        for which, place, group in pool:
            side = 1 if goes(group) else 0
            stage[side].append((which, len(groups[side]) * CAP, place * CAP))
            groups[side].append(group)
        return stage, groups[0], groups[1]


def sorted_rows(pieces, size, parts):
    total = 0.0
    for which, part in enumerate(parts):
        moves = [(to, start) for w, to, start in pieces if w == which]
        if moves:
            total = total + dot(mover(size, part.shape[0], moves), part)
    return total.astype(BF)


def ranked(ids, weight, earlier, rows, here, wanted):
    length = ids.shape[1]
    row = lax.broadcasted_iota(jnp.int32, (rows, 1), 0)
    expert = jnp.full((rows, 1), -1, jnp.int32)
    level = jnp.zeros((rows, 1), jnp.int32)
    for place, target in enumerate(wanted):
        inside = (row >= place * CAP) & (row < (place + 1) * CAP)
        expert = jnp.where(inside, here ^ target, expert)
        level = jnp.where(inside, row - place * CAP, level)
    hits = jnp.zeros((rows, length), F32)
    share = jnp.zeros((rows, length), F32)
    for pick in range(ids.shape[0]):
        named = ids[pick : pick + 1, :] == expert
        hits = hits + jnp.where(named, 1.0, 0.0)
        if weight is not None:
            share = share + jnp.where(named, weight[pick : pick + 1, :], 0.0)
    ranks = dot(hits.astype(BF), earlier)
    chosen = (hits > 0.5) & (jnp.abs(ranks - level.astype(F32)) < 0.5)
    return jnp.where(chosen, 1.0 if weight is None else share, 0.0)


def body(queries, key_rows, value_rows, segments, hidden_entry_rows, expert_ids, route_weight, w_gate, w_up, w_down):
    length = queries.shape[1]
    blocks, sides, cores = lax.axis_size("blk"), lax.axis_size("side"), lax.axis_size("tp")
    plan = Plan(blocks)
    experts = plan.experts
    quarter, ff = w_gate.shape[1], w_gate.shape[2]
    ids, shares = expert_ids[0].T, route_weight[0].T
    picks = ids.shape[0]

    def columns_of(run):
        half = (lax.axis_index("blk") // experts) ^ run
        return pl.ds(pl.multiple_of(half * quarter, quarter), quarter)

    def own_expert():
        return lax.axis_index("blk") % experts

    def over_side(value, offset, low):
        return swapped(value, ("blk", "side"), low * sides + offset)

    first_rows = up_to(experts * CAP, 8)
    wide = hidden_entry_rows.shape[2]

    def before(before_ref):
        i = lax.broadcasted_iota(jnp.int32, (length, length), 0)
        j = lax.broadcasted_iota(jnp.int32, (length, length), 1)
        before_ref[...] = jnp.where(i < j, 1.0, 0.0).astype(BF)

    (earlier,) = call(before, [shaped(length, length)], flops=COST)

    def choose(earlier_ref, ids_ref, x_ref, send_ref, keep_ref):
        chosen = ranked(ids_ref[...], None, earlier_ref[...], first_rows, own_expert(), range(experts)).astype(BF)
        send_ref[...] = dot(chosen, x_ref[:, columns_of(1)]).astype(BF)
        keep_ref[...] = dot(chosen, x_ref[:, columns_of(0)]).astype(BF)

    send, keep = call(
        choose, [shaped(first_rows, quarter)] * 2, earlier, ids, hidden_entry_rows[0], flops=COST
    )

    def share_out(earlier_ref, ids_ref, weight_ref, share_ref):
        share = ranked(ids_ref[...], weight_ref[...], earlier_ref[...], first_rows, own_expert(), plan.ranked)
        share_ref[...] = share.astype(BF)

    (share,) = call(share_out, [shaped(first_rows, length)], earlier, ids, shares)

    def pack(after_ref, key_ref, value_ref, segment_ref, held_ref, segment_here, sems):
        copies = [
            pltpu.make_async_copy(key_ref, held_ref.at[0, pl.ds(0, length)], sems.at[0]),
            pltpu.make_async_copy(value_ref, held_ref.at[0, pl.ds(length, length)], sems.at[1]),
            pltpu.make_async_copy(segment_ref, segment_here, sems.at[2]),
        ]
        for copy in copies:
            copy.start()
        copies[2].wait()
        labels = jnp.broadcast_to(segment_here[...].astype(F32), (16, length))
        held_ref[0, 2 * length : 2 * length + 16, :] = labels.astype(BF)
        copies[0].wait()
        copies[1].wait()

    (held,) = call(
        pack,
        [jax.ShapeDtypeStruct((1, 2 * length + 16, HEAD_DIM), BF)],
        send,
        key_rows[0],
        value_rows[0],
        segments,
        scratch=[pltpu.VMEM((1, length), jnp.int32)],
        semaphores=3,
        far_in=(1, 2, 3),
    )

    def sort(stage, *parts):
        sizes = [up_to(len(pieces) * CAP, 8) for pieces in stage]

        def kernel(*refs):
            values = [ref[...] for ref in refs[: len(parts)]]
            for pieces, size, out in zip(stage, sizes, refs[len(parts) :]):
                out[...] = sorted_rows(pieces, size, values)

        return call(
            kernel,
            [shaped(size, quarter) for size in sizes],
            *parts,
            flops=COST,
        )

    for bit, stage in zip(plan.bits, plan.there):
        received = swapped(send, "blk", bit)
        keep, send = sort(stage, keep, received)
    part_rows = len(plan.sources) // 2 * CAP
    padded = keep.shape[0]
    own = [keep] + [over_side(keep, offset, 0) for offset in range(1, sides)]
    other = [over_side(send, offset, 1) for offset in range(sides)]

    held, _ = lax.optimization_barrier((held, keep))
    order = [0]
    for bit in [1 << i for i in reversed(range(blocks.bit_length() - 1))]:
        held = jnp.concatenate([held, swapped(held, "blk", bit)], axis=0)
        order = order + [place ^ bit for place in order]
    side_rows = 2 * part_rows
    half = sides // 2 * side_rows

    def project(*refs):
        own_refs, other_refs, (gate_ref, up_ref, send_ref, keep_ref) = refs[:sides], refs[sides : 2 * sides], refs[2 * sides :]
        groups = range(part_rows // CAP)
        halves = []
        for first in (0, sides // 2):
            total = 0.0
            for at in range(sides // 2):
                for refs_of, shift in ((own_refs, 0), (other_refs, part_rows)):
                    moves = [(at * side_rows + shift + g * CAP, g * CAP) for g in groups]
                    total = total + dot(mover(half, padded, moves), refs_of[first + at][...])
            halves.append(total.astype(BF))
        low, high = halves
        mine = lax.axis_index("tp") == 0
        away, stay = jnp.where(mine, high, low), jnp.where(mine, low, high)
        both = jnp.concatenate([away, stay], axis=0)
        for at, weight in ((0, gate_ref), (ff, up_ref)):
            terms = dot(both, weight[...])
            send_ref[:, at : at + ff] = terms[:half].astype(BF)
            keep_ref[:, at : at + ff] = terms[half:]

    term_send, term_keep = call(
        project,
        [shaped(half, 2 * ff), shaped(half, 2 * ff, F32)],
        *own,
        *other,
        w_gate[0],
        w_up[0],
        flops=8 * half * quarter * ff,
    )
    term_received = swapped(term_send, "tp", 1)

    moves = []
    for block in range(half // side_rows):
        for place, source in enumerate(plan.sources):
            moves.append((block * side_rows + place * CAP, block * side_rows + plan.sources.index(source ^ experts) * CAP))

    def add_terms(keep_ref, received_ref, sum_ref, send_ref):
        total = keep_ref[...] + received_ref[...].astype(F32)
        sum_ref[...] = total
        send_ref[...] = dot(mover(half, half, moves), total.astype(BF)).astype(BF)

    sums, sums_send = call(
        add_terms,
        [shaped(half, 2 * ff, F32), shaped(half, 2 * ff)],
        term_keep,
        term_received,
        flops=4 * half * half * ff,
    )
    sums_received = swapped(sums_send, "blk", experts)

    heads = queries.shape[2] // HEAD_DIM
    factor = 1.0 / math.sqrt(HEAD_DIM)
    span = blocks * length

    def attend(query_ref, held_ref, segment_ref, out_ref, keys, values, bias):
        here = lax.axis_index("blk")
        i = lax.broadcasted_iota(jnp.int32, (length, length), 0)
        j = lax.broadcasted_iota(jnp.int32, (length, length), 1)
        label_here = jnp.sum(jnp.where(i == j, segment_ref[...].astype(F32), 0.0), axis=1, keepdims=True)
        for place, other_block in enumerate(order):
            at = place * length
            keys[at : at + length, :] = held_ref[place, :length, :]
            values[at : at + length, :] = held_ref[place, length : 2 * length, :]
            label = held_ref[place, 2 * length : 2 * length + 16, :].astype(F32)[:1]
            same = label_here == label
            if other_block == 0:
                seen = same & (j <= i)
            else:
                seen = same & ((here ^ other_block) < here)
            bias[:, at : at + length] = jnp.where(seen, 0.0, -1e30)

        def one_head(head):
            columns = pl.ds(pl.multiple_of(head * HEAD_DIM, HEAD_DIM), HEAD_DIM)
            scores = lax.dot_general(
                query_ref[:, columns], keys[...], (((1,), (1,)), ((), ())), preferred_element_type=F32
            )
            scores = scores + bias[...]
            top = jnp.max(scores, axis=1, keepdims=True)
            weights = jnp.exp((scores - top) * factor)
            totals = jnp.sum(weights, axis=1, keepdims=True)
            out = dot(weights.astype(BF), values[...])
            out_ref[:, columns] = (out / totals).astype(BF)

        if span <= 1024:
            for head in range(heads):
                one_head(head)
        else:
            lax.fori_loop(0, heads, lambda head, _: (one_head(head), 0)[1], 0)

    segments_then, _ = lax.optimization_barrier((segments, sums_send))
    (attended,) = call(
        attend,
        [shaped(length, heads * HEAD_DIM)],
        queries[0],
        held,
        segments_then,
        scratch=[pltpu.VMEM((span, HEAD_DIM), BF)] * 2 + [pltpu.VMEM((length, span), F32)],
        flops=4 * heads * length * span * HEAD_DIM,
        exps=heads * length * span,
    )
    sums_received, attended = lax.optimization_barrier((sums_received, attended))

    def activate(sum_ref, received_ref, hidden_ref):
        gate = sum_ref[:, :ff] + received_ref[:, :ff].astype(F32)
        up = sum_ref[:, ff:] + received_ref[:, ff:].astype(F32)
        hidden_ref[...] = (gate / (1.0 + jnp.exp(-gate)) * up).astype(BF)

    (hidden,) = call(activate, [shaped(half, ff)], sums, sums_received, exps=half * ff)
    hidden_received = swapped(hidden, "tp", 1)

    def project_back(hidden_ref, received_ref, down_ref, *out_refs):
        mine = lax.axis_index("tp") == 0
        here, there = hidden_ref[...], received_ref[...]
        low, high = jnp.where(mine, here, there), jnp.where(mine, there, here)
        groups = range(part_rows // CAP)
        total = 0.0
        for first, rows in ((0, low), (sides // 2, high)):
            moves = []
            for at in range(sides // 2):
                for part in range(2):
                    for g in groups:
                        to = (2 * (first + at) + part) * padded + g * CAP
                        moves.append((to, at * side_rows + part * part_rows + g * CAP))
            total = total + dot(mover(2 * sides * padded, half, moves), rows)
        out = dot(total.astype(BF), down_ref[...])
        for place, out_ref in enumerate(out_refs):
            out_ref[...] = out[place * padded : (place + 1) * padded].astype(out_ref.dtype)

    outs = call(
        project_back,
        [shaped(padded, quarter, BF if place else F32) for place in range(2 * sides)],
        hidden,
        hidden_received,
        w_down[0],
        flops=4 * half * ff * quarter,
    )
    own = [outs[0]] + [over_side(outs[2 * offset], offset, 0) for offset in range(1, sides)]
    other = [over_side(outs[2 * offset + 1], offset, 1) for offset in range(sides)]

    def add_parts(*refs):
        sums = []
        for part in (refs[:sides], refs[sides : 2 * sides]):
            total = part[0][...].astype(F32)
            for ref in part[1:]:
                total = total + ref[...].astype(F32)
            sums.append(total.astype(BF))
        for pieces, out in zip(plan.back[0], refs[2 * sides :]):
            out[...] = sorted_rows(pieces, out.shape[0], sums)

    keep, send = call(
        add_parts,
        [shaped(up_to(len(pieces) * CAP, 8), quarter) for pieces in plan.back[0]],
        *own,
        *other,
        flops=8 * padded * padded * quarter,
    )
    for bit, stage in zip(plan.bits[::-1], plan.back[1:]):
        keep, send = sort(stage, keep, swapped(send, "blk", bit))
    received = swapped(send, "blk", plan.bits[0])

    def mix(run):
        def kernel(share_ref, rows_ref, *refs):
            out_ref, here, sems = refs[-3:]
            piece = quarter // 4
            copies = []
            for at in range(4):
                columns = pl.ds(at * piece, piece)
                here[at] = dot_rows(share_ref[...], rows_ref[:, columns]).astype(BF)
                half_at = ((lax.axis_index("blk") // experts) ^ run) * 4 + at
                target = pl.ds(pl.multiple_of(half_at * piece, piece), piece)
                copies.append(pltpu.make_async_copy(here.at[at], out_ref.at[:, target], sems.at[at]))
                copies[-1].start()
            for copy in copies:
                copy.wait()

        return kernel

    moe_out = None
    for run, rows in ((0, keep), (1, received)):
        ins = [share, rows] + ([] if moe_out is None else [moe_out])
        (moe_out,) = call(
            mix(run),
            [shaped(length, wide)],
            *ins,
            scratch=[pltpu.VMEM((4, length, quarter // 4), BF)],
            semaphores=4,
            far_in=(2,),
            far_out=(0,),
            aliases={2: 0} if run else None,
            flops=4 * length * first_rows * quarter,
        )
    return attended[None], moe_out[None]


def solution(mesh):
    rows = P(("groups", "side"), "blk", "tp")
    placed = (
        rows,
        rows,
        rows,
        P(("groups", "side"), "blk"),
        rows,
        P(("groups", "side"), "blk", None),
        P(("groups", "side"), "blk", None),
        P("blk", "tp", "side"),
        P("blk", "tp", "side"),
        P("blk", "side", "tp"),
    )
    return jax.shard_map(body, mesh=mesh, in_specs=placed, out_specs=(rows, rows), check_vma=False)
```

```python
import math

import jax
import jax.numpy as jnp
from jax import lax
from jax.experimental import pallas as pl
from jax.experimental.pallas import tpu as pltpu
from jax.sharding import PartitionSpec as P

HEAD_DIM = 128
CAP = 10
COST = 3_000_000_000
BF = jnp.bfloat16
F32 = jnp.float32
VMEM = pl.BlockSpec(memory_space=pltpu.VMEM)
HBM = pl.BlockSpec(memory_space=pltpu.HBM)


def swapped(value, axis, bit):
    count = lax.axis_size(axis)
    return lax.ppermute(value, axis, [(i, i ^ bit) for i in range(count)])


def up_to(value, step):
    return -(-value // step) * step


def call(kernel, outs, *ins, scratch=(), semaphores=0, far_in=(), far_out=(), aliases=None, flops=0, exps=0, grant=0):
    moved = sum(math.prod(a.shape) * a.dtype.itemsize for a in (*ins, *outs))
    held = sum(math.prod(s.shape) * s.dtype.itemsize for s in scratch)
    scratch = list(scratch) + ([pltpu.SemaphoreType.DMA((semaphores,))] if semaphores else [])
    return pl.pallas_call(
        kernel,
        out_shape=list(outs),
        in_specs=[HBM if i in far_in else VMEM for i in range(len(ins))],
        out_specs=[HBM if i in far_out else VMEM for i in range(len(outs))],
        scratch_shapes=scratch,
        input_output_aliases=aliases or {},
        compiler_params=pltpu.CompilerParams(vmem_limit_bytes=grant or 2 * moved + held + (2 << 20)),
        cost_estimate=pl.CostEstimate(flops=flops, bytes_accessed=0 if flops == 0 else moved, transcendentals=exps),
    )(*ins)


def shaped(rows, columns, dtype=BF):
    return jax.ShapeDtypeStruct((rows, columns), dtype)


def dot(a, b):
    return jnp.dot(a, b, preferred_element_type=F32)


def dot_rows(a, b):
    return lax.dot_general(a, b, (((0,), (0,)), ((), ())), preferred_element_type=F32)


def mover(rows_out, rows_in, pieces):
    i = lax.broadcasted_iota(jnp.int32, (rows_out, rows_in), 0)
    j = lax.broadcasted_iota(jnp.int32, (rows_out, rows_in), 1)
    hit = jnp.zeros((rows_out, rows_in), jnp.bool_)
    for to, start in pieces:
        hit = hit | ((j - i == start - to) & (i >= to) & (i < to + CAP))
    return jnp.where(hit, 1.0, 0.0).astype(BF)


class Plan:
    def __init__(self, count):
        self.count, self.experts = count, count // 2
        self.bits = [1 << i for i in reversed(range(1, count.bit_length() - 1))]
        keep = [(0, d) for d in range(self.experts)]
        send = [(0, d) for d in range(self.experts, count)]
        self.there = []
        for bit, later in zip(self.bits, self.bits[1:] + [1]):
            pool = self.pool(keep, send, bit)
            stage, keep, send = self.split(pool, lambda group: group[1] & later)
            self.there.append(stage)
        near = [s for s, _ in keep]
        self.sources = near + [s ^ 1 for s in near]
        self.back = []
        pool = [(i, j, (s, i)) for i in range(2) for j, s in enumerate(near)]
        for bit in reversed(self.bits):
            stage, keep, send = self.split(pool, lambda group: group[0] & bit)
            self.back.append(stage)
            pool = self.pool(keep, send, bit)
        self.ranked = [d for _, d in keep]

    def pool(self, keep, send, bit):
        received = [(s ^ bit, d ^ bit) for s, d in send]
        return [(0, i, g) for i, g in enumerate(keep)] + [(1, i, g) for i, g in enumerate(received)]

    def split(self, pool, goes):
        stage, groups = ([], []), ([], [])
        for which, place, group in pool:
            side = 1 if goes(group) else 0
            stage[side].append((which, len(groups[side]) * CAP, place * CAP))
            groups[side].append(group)
        return stage, groups[0], groups[1]


def sorted_rows(pieces, size, parts):
    total = 0.0
    for which, part in enumerate(parts):
        moves = [(to, start) for w, to, start in pieces if w == which]
        if moves:
            total = total + dot(mover(size, part.shape[0], moves), part)
    return total.astype(BF)


def ranked(ids, weight, earlier, rows, here, wanted):
    length = ids.shape[1]
    row = lax.broadcasted_iota(jnp.int32, (rows, 1), 0)
    expert = jnp.full((rows, 1), -1, jnp.int32)
    level = jnp.zeros((rows, 1), jnp.int32)
    for place, target in enumerate(wanted):
        inside = (row >= place * CAP) & (row < (place + 1) * CAP)
        expert = jnp.where(inside, here ^ target, expert)
        level = jnp.where(inside, row - place * CAP, level)
    hits = jnp.zeros((rows, length), F32)
    share = jnp.zeros((rows, length), F32)
    for pick in range(ids.shape[0]):
        named = ids[pick : pick + 1, :] == expert
        hits = hits + jnp.where(named, 1.0, 0.0)
        if weight is not None:
            share = share + jnp.where(named, weight[pick : pick + 1, :], 0.0)
    ranks = dot(hits.astype(BF), earlier)
    chosen = (hits > 0.5) & (jnp.abs(ranks - level.astype(F32)) < 0.5)
    return jnp.where(chosen, 1.0 if weight is None else share, 0.0)


def body(queries, key_rows, value_rows, segments, hidden_entry_rows, expert_ids, route_weight, w_gate, w_up, w_down):
    length = queries.shape[1]
    blocks, sides, cores = lax.axis_size("blk"), lax.axis_size("side"), lax.axis_size("tp")
    plan = Plan(blocks)
    experts = plan.experts
    quarter, ff = w_gate.shape[1], w_gate.shape[2]
    ids, shares = expert_ids[0].T, route_weight[0].T
    picks = ids.shape[0]

    def columns_of(run):
        half = (lax.axis_index("blk") // experts) ^ run
        return pl.ds(pl.multiple_of(half * quarter, quarter), quarter)

    def own_expert():
        return lax.axis_index("blk") % experts

    def over_side(value, offset, low):
        return swapped(value, ("blk", "side"), low * sides + offset)

    first_rows = up_to(experts * CAP, 8)
    wide = hidden_entry_rows.shape[2]

    def before(before_ref):
        i = lax.broadcasted_iota(jnp.int32, (length, length), 0)
        j = lax.broadcasted_iota(jnp.int32, (length, length), 1)
        before_ref[...] = jnp.where(i < j, 1.0, 0.0).astype(BF)

    (earlier,) = call(before, [shaped(length, length)], flops=COST)

    def choose(earlier_ref, ids_ref, x_ref, send_ref, keep_ref):
        chosen = ranked(ids_ref[...], None, earlier_ref[...], first_rows, own_expert(), range(experts)).astype(BF)
        send_ref[...] = dot(chosen, x_ref[:, columns_of(1)]).astype(BF)
        keep_ref[...] = dot(chosen, x_ref[:, columns_of(0)]).astype(BF)

    send, keep = call(
        choose, [shaped(first_rows, quarter)] * 2, earlier, ids, hidden_entry_rows[0], flops=COST
    )

    def share_out(earlier_ref, ids_ref, weight_ref, share_ref):
        share = ranked(ids_ref[...], weight_ref[...], earlier_ref[...], first_rows, own_expert(), plan.ranked)
        share_ref[...] = share.astype(BF)

    (share,) = call(share_out, [shaped(first_rows, length)], earlier, ids, shares)

    def pack(after_ref, key_ref, value_ref, segment_ref, held_ref, segment_here, sems):
        copies = [
            pltpu.make_async_copy(key_ref, held_ref.at[0, pl.ds(0, length)], sems.at[0]),
            pltpu.make_async_copy(value_ref, held_ref.at[0, pl.ds(length, length)], sems.at[1]),
            pltpu.make_async_copy(segment_ref, segment_here, sems.at[2]),
        ]
        for copy in copies:
            copy.start()
        copies[2].wait()
        labels = jnp.broadcast_to(segment_here[...].astype(F32), (16, length))
        held_ref[0, 2 * length : 2 * length + 16, :] = labels.astype(BF)
        copies[0].wait()
        copies[1].wait()

    (held,) = call(
        pack,
        [jax.ShapeDtypeStruct((1, 2 * length + 16, HEAD_DIM), BF)],
        send,
        key_rows[0],
        value_rows[0],
        segments,
        scratch=[pltpu.VMEM((1, length), jnp.int32)],
        semaphores=3,
        far_in=(1, 2, 3),
    )

    def sort(stage, *parts):
        sizes = [up_to(len(pieces) * CAP, 8) for pieces in stage]

        def kernel(*refs):
            values = [ref[...] for ref in refs[: len(parts)]]
            for pieces, size, out in zip(stage, sizes, refs[len(parts) :]):
                out[...] = sorted_rows(pieces, size, values)

        return call(
            kernel,
            [shaped(size, quarter) for size in sizes],
            *parts,
            flops=COST,
        )

    for bit, stage in zip(plan.bits, plan.there):
        received, held = lax.optimization_barrier((swapped(send, "blk", bit), held))
        keep, send = sort(stage, keep, received)
    part_rows = len(plan.sources) // 2 * CAP
    padded = keep.shape[0]
    own = [keep] + [over_side(keep, offset, 0) for offset in range(1, sides)]
    other = [over_side(send, offset, 1) for offset in range(sides)]

    held, _ = lax.optimization_barrier((held, keep))
    nearby = [1 << i for i in reversed(range(blocks.bit_length() - 1))]
    order = [0]
    received_held = swapped(held, "blk", nearby[0])

    def join(after_ref, held_ref, received_ref, both_ref):
        both_ref[: held_ref.shape[0]] = held_ref[...]
        both_ref[held_ref.shape[0] :] = received_ref[...]

    def joined(after, held, received_held, flops):
        both = jax.ShapeDtypeStruct((2 * held.shape[0], *held.shape[1:]), BF)
        return call(join, [both], after, held, received_held, flops=flops)[0]

    side_rows = 2 * part_rows
    half = sides // 2 * side_rows

    def project(*refs):
        own_refs, other_refs, (gate_ref, up_ref, *out_refs) = refs[:sides], refs[sides : 2 * sides], refs[2 * sides :]
        groups = range(part_rows // CAP)
        halves = []
        for first in (0, sides // 2):
            total = 0.0
            for at in range(sides // 2):
                for refs_of, shift in ((own_refs, 0), (other_refs, part_rows)):
                    moves = [(at * side_rows + shift + g * CAP, g * CAP) for g in groups]
                    total = total + dot(mover(half, padded, moves), refs_of[first + at][...])
            halves.append(total.astype(BF))
        low, high = halves
        mine = lax.axis_index("tp") == 0
        away, stay = jnp.where(mine, high, low), jnp.where(mine, low, high)
        both = jnp.concatenate([away, stay], axis=0)
        for weight, send_ref, keep_ref in ((gate_ref, *out_refs[:2]), (up_ref, *out_refs[2:])):
            terms = dot(both, weight[...])
            send_ref[...] = terms[:half].astype(BF)
            keep_ref[...] = terms[half:]

    gate_send, gate_keep, up_send, up_keep = call(
        project,
        [shaped(half, ff), shaped(half, ff, F32)] * 2,
        *own,
        *other,
        w_gate[0],
        w_up[0],
    )
    gate_received, up_received = swapped(gate_send, "tp", 1), swapped(up_send, "tp", 1)

    moves = []
    for block in range(half // side_rows):
        for place, source in enumerate(plan.sources):
            moves.append((block * side_rows + place * CAP, block * side_rows + plan.sources.index(source ^ experts) * CAP))

    def add_terms(gate_keep_ref, gate_received_ref, up_keep_ref, up_received_ref, sum_ref, send_ref):
        for at, keep_ref, received_ref in ((0, gate_keep_ref, gate_received_ref), (ff, up_keep_ref, up_received_ref)):
            total = keep_ref[...] + received_ref[...].astype(F32)
            sum_ref[:, at : at + ff] = total
            send_ref[:, at : at + ff] = dot(mover(half, half, moves), total.astype(BF)).astype(BF)

    sums, sums_send = call(
        add_terms,
        [shaped(half, 2 * ff, F32), shaped(half, 2 * ff)],
        gate_keep,
        gate_received,
        up_keep,
        up_received,
    )
    sums_received = swapped(sums_send, "blk", experts)
    for bit in nearby[1:]:
        held = joined(sums_send, held, received_held, COST)
        received_held = swapped(held, "blk", bit)
    held = joined(sums_send, held, received_held, 0)
    for bit in nearby:
        order = order + [place ^ bit for place in order]

    def activate(sum_ref, received_ref, hidden_ref):
        gate = sum_ref[:, :ff] + received_ref[:, :ff].astype(F32)
        up = sum_ref[:, ff:] + received_ref[:, ff:].astype(F32)
        hidden_ref[...] = (gate / (1.0 + jnp.exp(-gate)) * up).astype(BF)

    (hidden,) = call(activate, [shaped(half, ff)], sums, sums_received, exps=half * ff)
    hidden_received = swapped(hidden, "tp", 1)

    def project_back(hidden_ref, received_ref, down_ref, *out_refs):
        mine = lax.axis_index("tp") == 0
        here, there = hidden_ref[...], received_ref[...]
        low, high = jnp.where(mine, here, there), jnp.where(mine, there, here)
        groups = range(part_rows // CAP)
        total = 0.0
        for first, rows in ((0, low), (sides // 2, high)):
            moves = []
            for at in range(sides // 2):
                for part in range(2):
                    for g in groups:
                        to = (2 * (first + at) + part) * padded + g * CAP
                        moves.append((to, at * side_rows + part * part_rows + g * CAP))
            total = total + dot(mover(2 * sides * padded, half, moves), rows)
        out = dot(total.astype(BF), down_ref[...])
        for place, out_ref in enumerate(out_refs):
            out_ref[...] = out[place * padded : (place + 1) * padded].astype(out_ref.dtype)

    outs = call(
        project_back,
        [shaped(padded, quarter, BF if place else F32) for place in range(2 * sides)],
        hidden,
        hidden_received,
        w_down[0],
        flops=4 * half * ff * quarter,
    )
    own = [outs[0]] + [over_side(outs[2 * offset], offset, 0) for offset in range(1, sides)]
    other = [over_side(outs[2 * offset + 1], offset, 1) for offset in range(sides)]

    heads = queries.shape[2] // HEAD_DIM
    factor = 1.0 / math.sqrt(HEAD_DIM)
    span = blocks * length
    batch = math.gcd(heads, max(1, 2048 // span))

    def attend(query_ref, held_ref, segment_ref, out_ref, keys, values, bias):
        here = lax.axis_index("blk")
        i = lax.broadcasted_iota(jnp.int32, (length, length), 0)
        j = lax.broadcasted_iota(jnp.int32, (length, length), 1)
        label_here = jnp.sum(jnp.where(i == j, segment_ref[...].astype(F32), 0.0), axis=1, keepdims=True)
        for place, other_block in enumerate(order):
            at = place * length
            keys[at : at + length, :] = held_ref[place, :length, :]
            values[at : at + length, :] = held_ref[place, length : 2 * length, :]
            label = held_ref[place, 2 * length : 2 * length + 16, :].astype(F32)[:1]
            same = label_here == label
            if other_block == 0:
                seen = same & (j <= i)
            else:
                seen = same & ((here ^ other_block) < here)
            bias[:, at : at + length] = jnp.where(seen, 0.0, -1e30)

        def some_heads(first):
            columns = [pl.ds(pl.multiple_of((first + h) * HEAD_DIM, HEAD_DIM), HEAD_DIM) for h in range(batch)]
            query = jnp.concatenate([query_ref[:, c] for c in columns], axis=0)
            scores = lax.dot_general(query, keys[...], (((1,), (1,)), ((), ())), preferred_element_type=F32)
            scores = (scores.reshape(batch, length, span) + bias[...][None]).reshape(batch * length, span)
            top = jnp.max(scores, axis=1, keepdims=True)
            weights = jnp.exp((scores - top) * factor)
            totals = jnp.sum(weights, axis=1, keepdims=True)
            out = (dot(weights.astype(BF), values[...]) / totals).astype(BF)
            for h, c in enumerate(columns):
                out_ref[:, c] = out[h * length : (h + 1) * length]

        if span <= 1024:
            for first in range(0, heads, batch):
                some_heads(first)
        else:
            lax.fori_loop(0, heads // batch, lambda step, _: (some_heads(step * batch), 0)[1], 0)

    segments_then, _ = lax.optimization_barrier((segments, outs[1]))
    (attended,) = call(
        attend,
        [shaped(length, heads * HEAD_DIM)],
        queries[0],
        held,
        segments_then,
        scratch=[pltpu.VMEM((span, HEAD_DIM), BF)] * 2 + [pltpu.VMEM((length, span), F32)],
        flops=4 * heads * length * span * HEAD_DIM,
        exps=heads * length * span,
    )
    other[-1], attended = lax.optimization_barrier((other[-1], attended))

    def add_parts(*refs):
        sums = []
        for part in (refs[:sides], refs[sides : 2 * sides]):
            total = part[0][...].astype(F32)
            for ref in part[1:]:
                total = total + ref[...].astype(F32)
            sums.append(total.astype(BF))
        for pieces, out in zip(plan.back[0], refs[2 * sides :]):
            out[...] = sorted_rows(pieces, out.shape[0], sums)

    keep, send = call(
        add_parts,
        [shaped(up_to(len(pieces) * CAP, 8), quarter) for pieces in plan.back[0]],
        *own,
        *other,
        flops=8 * padded * padded * quarter,
    )
    for bit, stage in zip(plan.bits[::-1], plan.back[1:]):
        keep, send = sort(stage, keep, swapped(send, "blk", bit))
    received = swapped(send, "blk", plan.bits[0])

    def mix(run):
        def kernel(share_ref, rows_ref, *refs):
            out_ref, here, sems = refs[-3:]
            piece = quarter // 4
            copies = []
            for at in range(4):
                columns = pl.ds(at * piece, piece)
                here[at] = dot_rows(share_ref[...], rows_ref[:, columns]).astype(BF)
                half_at = ((lax.axis_index("blk") // experts) ^ run) * 4 + at
                target = pl.ds(pl.multiple_of(half_at * piece, piece), piece)
                copies.append(pltpu.make_async_copy(here.at[at], out_ref.at[:, target], sems.at[at]))
                copies[-1].start()
            for copy in copies:
                copy.wait()

        return kernel

    moe_out = None
    for run, rows in ((0, keep), (1, received)):
        ins = [share, rows] + ([] if moe_out is None else [moe_out])
        (moe_out,) = call(
            mix(run),
            [shaped(length, wide)],
            *ins,
            scratch=[pltpu.VMEM((4, length, quarter // 4), BF)],
            semaphores=4,
            far_in=(2,),
            far_out=(0,),
            aliases={2: 0} if run else None,
            flops=4 * length * first_rows * quarter,
        )
    return attended[None], moe_out[None]


def solution(mesh):
    rows = P(("groups", "side"), "blk", "tp")
    placed = (
        rows,
        rows,
        rows,
        P(("groups", "side"), "blk"),
        rows,
        P(("groups", "side"), "blk", None),
        P(("groups", "side"), "blk", None),
        P("blk", "tp", "side"),
        P("blk", "tp", "side"),
        P("blk", "side", "tp"),
    )
    return jax.shard_map(body, mesh=mesh, in_specs=placed, out_specs=(rows, rows), check_vma=False)
```

```python
import math

import jax
import jax.numpy as jnp
from jax import lax
from jax.experimental import pallas as pl
from jax.experimental.pallas import tpu as pltpu
from jax.sharding import PartitionSpec as P

HEAD_DIM = 128
CAP = 10
COST = 3_000_000_000
BF = jnp.bfloat16
F32 = jnp.float32
VMEM = pl.BlockSpec(memory_space=pltpu.VMEM)
HBM = pl.BlockSpec(memory_space=pltpu.HBM)


def swapped(value, axis, bit):
    count = lax.axis_size(axis)
    return lax.ppermute(value, axis, [(i, i ^ bit) for i in range(count)])


def up_to(value, step):
    return -(-value // step) * step


def call(kernel, outs, *ins, scratch=(), semaphores=0, far_in=(), far_out=(), aliases=None, flops=0, exps=0, grant=0):
    moved = sum(math.prod(a.shape) * a.dtype.itemsize for a in (*ins, *outs))
    held = sum(math.prod(s.shape) * s.dtype.itemsize for s in scratch)
    scratch = list(scratch) + ([pltpu.SemaphoreType.DMA((semaphores,))] if semaphores else [])
    return pl.pallas_call(
        kernel,
        out_shape=list(outs),
        in_specs=[HBM if i in far_in else VMEM for i in range(len(ins))],
        out_specs=[HBM if i in far_out else VMEM for i in range(len(outs))],
        scratch_shapes=scratch,
        input_output_aliases=aliases or {},
        compiler_params=pltpu.CompilerParams(vmem_limit_bytes=grant or 2 * moved + held + (2 << 20)),
        cost_estimate=pl.CostEstimate(flops=flops, bytes_accessed=0 if flops == 0 else moved, transcendentals=exps),
    )(*ins)


def shaped(rows, columns, dtype=BF):
    return jax.ShapeDtypeStruct((rows, columns), dtype)


def dot(a, b):
    return jnp.dot(a, b, preferred_element_type=F32)


def dot_rows(a, b):
    return lax.dot_general(a, b, (((0,), (0,)), ((), ())), preferred_element_type=F32)


def mover(rows_out, rows_in, pieces):
    i = lax.broadcasted_iota(jnp.int32, (rows_out, rows_in), 0)
    j = lax.broadcasted_iota(jnp.int32, (rows_out, rows_in), 1)
    hit = jnp.zeros((rows_out, rows_in), jnp.bool_)
    for to, start in pieces:
        hit = hit | ((j - i == start - to) & (i >= to) & (i < to + CAP))
    return jnp.where(hit, 1.0, 0.0).astype(BF)


class Plan:
    def __init__(self, count, cuts):
        self.experts = count // 2
        self.bits = [1 << i for i in reversed(range(1, count.bit_length() - 1))]
        self.first = keep = [(0, d, c) for c in range(cuts) for d in range(self.experts)]
        send = [(0, d + self.experts, c) for _, d, c in keep]
        self.there = []
        for bit, later in zip(self.bits, self.bits[1:] + [1]):
            stage, keep, send = self.split(self.pool(keep, send, bit), lambda group: group[1] & later)
            self.there.append(stage)
        self.arrived = [(s, c) for s, _, c in keep]
        near = [s for s, c in self.arrived if c == 0]
        self.near, self.sources = near, near + [s ^ 1 for s in near]
        self.leaving = [(s, c) for c in range(cuts) for s in near]
        self.back = []
        pool = [(i, j, (s, i, c)) for i in range(2) for j, (s, c) in enumerate(self.leaving)]
        for bit in reversed(self.bits):
            stage, keep, send = self.split(pool, lambda group: group[0] & bit)
            self.back.append(stage)
            pool = self.pool(keep, send, bit)
        self.last = keep

    def pool(self, keep, send, bit):
        received = [(s ^ bit, d ^ bit, c) for s, d, c in send]
        return [(0, i, g) for i, g in enumerate(keep)] + [(1, i, g) for i, g in enumerate(received)]

    def split(self, pool, goes):
        stage, groups = ([], []), ([], [])
        for which, place, group in pool:
            side = 1 if goes(group) else 0
            stage[side].append((which, len(groups[side]) * CAP, place * CAP))
            groups[side].append(group)
        return stage, groups[0], groups[1]


def sorted_rows(pieces, size, parts):
    total = 0.0
    for which, part in enumerate(parts):
        moves = [(to, start) for w, to, start in pieces if w == which]
        if moves:
            total = total + dot(mover(size, part.shape[0], moves), part)
    return total.astype(BF)


def ranked(ids, weight, earlier, rows, here, groups):
    length = ids.shape[1]
    row = lax.broadcasted_iota(jnp.int32, (rows, 1), 0)
    expert = jnp.full((rows, 1), -1, jnp.int32)
    level = jnp.zeros((rows, 1), jnp.int32)
    for place, (_, target, _) in enumerate(groups):
        inside = (row >= place * CAP) & (row < (place + 1) * CAP)
        expert = jnp.where(inside, here ^ target, expert)
        level = jnp.where(inside, row - place * CAP, level)
    hits = jnp.zeros((rows, length), F32)
    share = jnp.zeros((rows, length), F32)
    for pick in range(ids.shape[0]):
        named = ids[pick : pick + 1, :] == expert
        hits = hits + jnp.where(named, 1.0, 0.0)
        if weight is not None:
            share = share + jnp.where(named, weight[pick : pick + 1, :], 0.0)
    ranks = dot(hits.astype(BF), earlier)
    chosen = (hits > 0.5) & (jnp.abs(ranks - level.astype(F32)) < 0.5)
    return jnp.where(chosen, 1.0 if weight is None else share, 0.0)


def cut_rows(matrix, groups, cut):
    row = lax.broadcasted_iota(jnp.int32, (matrix.shape[0], 1), 0)
    inside = jnp.zeros(row.shape, jnp.bool_)
    for place, (_, _, c) in enumerate(groups):
        if c == cut:
            inside = inside | ((row >= place * CAP) & (row < (place + 1) * CAP))
    return jnp.where(inside, matrix, 0.0).astype(BF)


def body(queries, key_rows, value_rows, segments, hidden_entry_rows, expert_ids, route_weight, w_gate, w_up, w_down):
    length = queries.shape[1]
    blocks, sides, cores = lax.axis_size("blk"), lax.axis_size("side"), lax.axis_size("tp")
    quarter, ff = w_gate.shape[1], w_gate.shape[2]
    cuts = next((c for c in (1, 2, 4) if blocks // 2 * CAP * c % 8 == 0 and quarter % (c * 128) == 0), 1)
    plan = Plan(blocks, cuts)
    experts, narrow = plan.experts, quarter // cuts
    ids, shares = expert_ids[0].T, route_weight[0].T
    picks = ids.shape[0]

    def columns_of(run, piece, pieces):
        place = ((lax.axis_index("blk") // experts) ^ run) * pieces + piece
        width = quarter // pieces
        return pl.ds(pl.multiple_of(place * width, width), width)

    def own_expert():
        return lax.axis_index("blk") % experts

    def over_side(value, offset, low):
        return swapped(value, ("blk", "side"), low * sides + offset)

    first_rows = up_to(len(plan.first) * CAP, 8)
    wide = hidden_entry_rows.shape[2]

    def before(before_ref):
        i = lax.broadcasted_iota(jnp.int32, (length, length), 0)
        j = lax.broadcasted_iota(jnp.int32, (length, length), 1)
        before_ref[...] = jnp.where(i < j, 1.0, 0.0).astype(BF)

    (earlier,) = call(before, [shaped(length, length)], flops=COST)

    def rank(earlier_ref, ids_ref, out_ref):
        chosen = ranked(ids_ref[...], None, earlier_ref[...], first_rows, own_expert(), plan.first)
        for cut in range(cuts):
            out_ref[cut] = cut_rows(chosen, plan.first, cut)

    (chosen,) = call(rank, [jax.ShapeDtypeStruct((cuts, first_rows, length), BF)], earlier, ids)

    def choose(run):
        def kernel(chosen_ref, x_ref, out_ref):
            total = 0.0
            for cut in range(cuts):
                total = total + dot(chosen_ref[cut], x_ref[:, columns_of(run, cut, cuts)])
            out_ref[...] = total.astype(BF)

        return call(kernel, [shaped(first_rows, narrow)], chosen, hidden_entry_rows[0], flops=COST)[0]

    send, keep = choose(1), choose(0)

    def share_out(earlier_ref, ids_ref, weight_ref, share_ref):
        share = ranked(ids_ref[...], weight_ref[...], earlier_ref[...], first_rows, own_expert(), plan.last)
        share_ref[...] = share.astype(BF)

    (share,) = call(share_out, [shaped(first_rows, length)], earlier, ids, shares)

    def pack(after_ref, key_ref, value_ref, segment_ref, held_ref, segment_here, sems):
        copies = [
            pltpu.make_async_copy(key_ref, held_ref.at[0, pl.ds(0, length)], sems.at[0]),
            pltpu.make_async_copy(value_ref, held_ref.at[0, pl.ds(length, length)], sems.at[1]),
            pltpu.make_async_copy(segment_ref, segment_here, sems.at[2]),
        ]
        for copy in copies:
            copy.start()
        copies[2].wait()
        labels = jnp.broadcast_to(segment_here[...].astype(F32), (16, length))
        held_ref[0, 2 * length : 2 * length + 16, :] = labels.astype(BF)
        copies[0].wait()
        copies[1].wait()

    (held,) = call(
        pack,
        [jax.ShapeDtypeStruct((1, 2 * length + 16, HEAD_DIM), BF)],
        send,
        key_rows[0],
        value_rows[0],
        segments,
        scratch=[pltpu.VMEM((1, length), jnp.int32)],
        semaphores=3,
        far_in=(1, 2, 3),
    )

    def sort(stage, *parts):
        sizes = [up_to(len(pieces) * CAP, 8) for pieces in stage]

        def kernel(*refs):
            values = [ref[...] for ref in refs[: len(parts)]]
            for pieces, size, out in zip(stage, sizes, refs[len(parts) :]):
                out[...] = sorted_rows(pieces, size, values)

        return call(
            kernel,
            [shaped(size, narrow) for size in sizes],
            *parts,
            flops=COST,
        )

    for bit, stage in zip(plan.bits, plan.there):
        received, held = lax.optimization_barrier((swapped(send, "blk", bit), held))
        keep, send = sort(stage, keep, received)
    part_rows = len(plan.near) * CAP
    padded = keep.shape[0]
    own = [keep] + [over_side(keep, offset, 0) for offset in range(1, sides)]
    other = [over_side(send, offset, 1) for offset in range(sides)]

    held, _ = lax.optimization_barrier((held, keep))
    nearby = [1 << i for i in reversed(range(blocks.bit_length() - 1))]
    order = [0]
    received_held = swapped(held, "blk", nearby[0])

    def join(after_ref, held_ref, received_ref, both_ref):
        both_ref[: held_ref.shape[0]] = held_ref[...]
        both_ref[held_ref.shape[0] :] = received_ref[...]

    def joined(after, held, received_held, flops):
        both = jax.ShapeDtypeStruct((2 * held.shape[0], *held.shape[1:]), BF)
        return call(join, [both], after, held, received_held, flops=flops)[0]

    side_rows = 2 * part_rows
    half = sides // 2 * side_rows

    def project(*refs):
        own_refs, other_refs, (gate_ref, up_ref, *out_refs) = refs[:sides], refs[sides : 2 * sides], refs[2 * sides :]
        mine = lax.axis_index("tp") == 0
        away, stay = [], []
        for refs_of in (own_refs, other_refs):
            for at in range(sides // 2):
                low, high = refs_of[at][...], refs_of[sides // 2 + at][...]
                away.append(jnp.where(mine, high, low))
                stay.append(jnp.where(mine, low, high))
        stacked = jnp.concatenate([jnp.concatenate(away, axis=0), jnp.concatenate(stay, axis=0)], axis=1)
        columns = []
        for cut in range(cuts):
            moves = []
            for part in range(2):
                for at in range(sides // 2):
                    for place, (source, c) in enumerate(plan.arrived):
                        if c == cut:
                            to = at * side_rows + part * part_rows + plan.near.index(source) * CAP
                            moves.append((to, (part * (sides // 2) + at) * padded + place * CAP))
            columns.append(dot(mover(half, stacked.shape[0], moves), stacked).astype(BF))
        both = jnp.concatenate(
            [jnp.concatenate([c[:, at : at + narrow] for c in columns], axis=1) for at in (0, narrow)], axis=0
        )
        for weight, send_ref, keep_ref in ((gate_ref, *out_refs[:2]), (up_ref, *out_refs[2:])):
            terms = dot(both, weight[...])
            send_ref[...] = terms[:half].astype(BF)
            keep_ref[...] = terms[half:]

    gate_send, gate_keep, up_send, up_keep = call(
        project,
        [shaped(half, ff), shaped(half, ff, F32)] * 2,
        *own,
        *other,
        w_gate[0],
        w_up[0],
    )
    gate_received, up_received = swapped(gate_send, "tp", 1), swapped(up_send, "tp", 1)

    moves = []
    for block in range(half // side_rows):
        for place, source in enumerate(plan.sources):
            moves.append((block * side_rows + place * CAP, block * side_rows + plan.sources.index(source ^ experts) * CAP))

    def add_terms(gate_keep_ref, gate_received_ref, up_keep_ref, up_received_ref, sum_ref, send_ref):
        for at, keep_ref, received_ref in ((0, gate_keep_ref, gate_received_ref), (ff, up_keep_ref, up_received_ref)):
            total = keep_ref[...] + received_ref[...].astype(F32)
            sum_ref[:, at : at + ff] = total
            send_ref[:, at : at + ff] = dot(mover(half, half, moves), total.astype(BF)).astype(BF)

    sums, sums_send = call(
        add_terms,
        [shaped(half, 2 * ff, F32), shaped(half, 2 * ff)],
        gate_keep,
        gate_received,
        up_keep,
        up_received,
    )
    sums_received = swapped(sums_send, "blk", experts)
    for bit in nearby[1:]:
        held = joined(sums_send, held, received_held, COST)
        received_held = swapped(held, "blk", bit)
    held = joined(sums_send, held, received_held, 0)
    for bit in nearby:
        order = order + [place ^ bit for place in order]

    def activate(sum_ref, received_ref, hidden_ref):
        gate = sum_ref[:, :ff] + received_ref[:, :ff].astype(F32)
        up = sum_ref[:, ff:] + received_ref[:, ff:].astype(F32)
        hidden_ref[...] = (gate / (1.0 + jnp.exp(-gate)) * up).astype(BF)

    (hidden,) = call(activate, [shaped(half, ff)], sums, sums_received, exps=half * ff)
    hidden_received = swapped(hidden, "tp", 1)

    def project_back(hidden_ref, received_ref, down_ref, *out_refs):
        mine = lax.axis_index("tp") == 0
        here, there = hidden_ref[...], received_ref[...]
        low, high = jnp.where(mine, here, there), jnp.where(mine, there, here)
        spaced = up_to(part_rows, 8)
        total = 0.0
        for first, rows in ((0, low), (sides // 2, high)):
            moves = []
            for at in range(sides // 2):
                for part in range(2):
                    for place in range(part_rows // CAP):
                        to = (2 * (first + at) + part) * spaced + place * CAP
                        moves.append((to, at * side_rows + part * part_rows + place * CAP))
            total = total + dot(mover(2 * sides * spaced, half, moves), rows)
        out = dot(total.astype(BF), down_ref[...])
        for place, out_ref in enumerate(out_refs):
            rows = out[place * spaced : place * spaced + part_rows]
            pieces = [rows[:, cut * narrow : (cut + 1) * narrow] for cut in range(cuts)]
            out_ref[...] = jnp.concatenate(pieces, axis=0).astype(out_ref.dtype)

    outs = call(
        project_back,
        [shaped(padded, narrow, BF if place else F32) for place in range(2 * sides)],
        hidden,
        hidden_received,
        w_down[0],
        flops=4 * half * ff * quarter,
    )
    own = [outs[0]] + [over_side(outs[2 * offset], offset, 0) for offset in range(1, sides)]
    other = [over_side(outs[2 * offset + 1], offset, 1) for offset in range(sides)]

    heads = queries.shape[2] // HEAD_DIM
    factor = 1.0 / math.sqrt(HEAD_DIM)
    span = blocks * length
    batch = math.gcd(heads, max(1, 2048 // span))

    def attend(query_ref, held_ref, segment_ref, out_ref, keys, values, bias):
        here = lax.axis_index("blk")
        i = lax.broadcasted_iota(jnp.int32, (length, length), 0)
        j = lax.broadcasted_iota(jnp.int32, (length, length), 1)
        label_here = jnp.sum(jnp.where(i == j, segment_ref[...].astype(F32), 0.0), axis=1, keepdims=True)
        for place, other_block in enumerate(order):
            at = place * length
            keys[at : at + length, :] = held_ref[place, :length, :]
            values[at : at + length, :] = held_ref[place, length : 2 * length, :]
            label = held_ref[place, 2 * length : 2 * length + 16, :].astype(F32)[:1]
            same = label_here == label
            if other_block == 0:
                seen = same & (j <= i)
            else:
                seen = same & ((here ^ other_block) < here)
            bias[:, at : at + length] = jnp.where(seen, 0.0, -1e30)

        def some_heads(first):
            columns = [pl.ds(pl.multiple_of((first + h) * HEAD_DIM, HEAD_DIM), HEAD_DIM) for h in range(batch)]
            query = jnp.concatenate([query_ref[:, c] for c in columns], axis=0)
            scores = lax.dot_general(query, keys[...], (((1,), (1,)), ((), ())), preferred_element_type=F32)
            scores = (scores.reshape(batch, length, span) + bias[...][None]).reshape(batch * length, span)
            top = jnp.max(scores, axis=1, keepdims=True)
            weights = jnp.exp((scores - top) * factor)
            totals = jnp.sum(weights, axis=1, keepdims=True)
            out = (dot(weights.astype(BF), values[...]) / totals).astype(BF)
            for h, c in enumerate(columns):
                out_ref[:, c] = out[h * length : (h + 1) * length]

        if span <= 1024:
            for first in range(0, heads, batch):
                some_heads(first)
        else:
            lax.fori_loop(0, heads // batch, lambda step, _: (some_heads(step * batch), 0)[1], 0)

    segments_then, _ = lax.optimization_barrier((segments, outs[1]))
    (attended,) = call(
        attend,
        [shaped(length, heads * HEAD_DIM)],
        queries[0],
        held,
        segments_then,
        scratch=[pltpu.VMEM((span, HEAD_DIM), BF)] * 2 + [pltpu.VMEM((length, span), F32)],
        flops=4 * heads * length * span * HEAD_DIM,
        exps=heads * length * span,
    )
    other[-1], attended = lax.optimization_barrier((other[-1], attended))

    def add_parts(*refs):
        sums = []
        for part in (refs[:sides], refs[sides : 2 * sides]):
            total = part[0][...].astype(F32)
            for ref in part[1:]:
                total = total + ref[...].astype(F32)
            sums.append(total.astype(BF))
        for pieces, out in zip(plan.back[0], refs[2 * sides :]):
            out[...] = sorted_rows(pieces, out.shape[0], sums)

    keep, send = call(
        add_parts,
        [shaped(up_to(len(pieces) * CAP, 8), narrow) for pieces in plan.back[0]],
        *own,
        *other,
        flops=8 * padded * padded * quarter,
    )
    for bit, stage in zip(plan.bits[::-1], plan.back[1:]):
        keep, send = sort(stage, keep, swapped(send, "blk", bit))
    received = swapped(send, "blk", plan.bits[0])

    def mix(run):
        def kernel(share_ref, rows_ref, *refs):
            out_ref, here, sems = refs[-3:]
            copies = []
            for at in range(4):
                cut, within = at * cuts // 4, at % (4 // cuts)
                rows = rows_ref[:, within * (quarter // 4) : (within + 1) * (quarter // 4)]
                here[at] = dot_rows(cut_rows(share_ref[...].astype(F32), plan.last, cut), rows).astype(BF)
                target = out_ref.at[:, columns_of(run, at, 4)]
                copies.append(pltpu.make_async_copy(here.at[at], target, sems.at[at]))
                copies[-1].start()
            for copy in copies:
                copy.wait()

        return kernel

    moe_out = None
    for run, rows in ((0, keep), (1, received)):
        ins = [share, rows] + ([] if moe_out is None else [moe_out])
        (moe_out,) = call(
            mix(run),
            [shaped(length, wide)],
            *ins,
            scratch=[pltpu.VMEM((4, length, quarter // 4), BF)],
            semaphores=4,
            far_in=(2,),
            far_out=(0,),
            aliases={2: 0} if run else None,
            flops=4 * length * first_rows * quarter,
        )
    return attended[None], moe_out[None]


def solution(mesh):
    rows = P(("groups", "side"), "blk", "tp")
    placed = (
        rows,
        rows,
        rows,
        P(("groups", "side"), "blk"),
        rows,
        P(("groups", "side"), "blk", None),
        P(("groups", "side"), "blk", None),
        P("blk", "tp", "side"),
        P("blk", "tp", "side"),
        P("blk", "side", "tp"),
    )
    return jax.shard_map(body, mesh=mesh, in_specs=placed, out_specs=(rows, rows), check_vma=False)
```

```python
import math

import jax
import jax.numpy as jnp
from jax import lax
from jax.experimental import pallas as pl
from jax.experimental.pallas import tpu as pltpu
from jax.sharding import PartitionSpec as P

HEAD_DIM = 128
CAP = 10
COST = 3_000_000_000
BF = jnp.bfloat16
F32 = jnp.float32
VMEM = pl.BlockSpec(memory_space=pltpu.VMEM)
HBM = pl.BlockSpec(memory_space=pltpu.HBM)


def swapped(value, axis, bit):
    count = lax.axis_size(axis)
    return lax.ppermute(value, axis, [(i, i ^ bit) for i in range(count)])


def up_to(value, step):
    return -(-value // step) * step


def call(kernel, outs, *ins, scratch=(), semaphores=0, far_in=(), far_out=(), aliases=None, flops=0, exps=0, grant=0):
    moved = sum(math.prod(a.shape) * a.dtype.itemsize for a in (*ins, *outs))
    held = sum(math.prod(s.shape) * s.dtype.itemsize for s in scratch)
    scratch = list(scratch) + ([pltpu.SemaphoreType.DMA((semaphores,))] if semaphores else [])
    return pl.pallas_call(
        kernel,
        out_shape=list(outs),
        in_specs=[HBM if i in far_in else VMEM for i in range(len(ins))],
        out_specs=[HBM if i in far_out else VMEM for i in range(len(outs))],
        scratch_shapes=scratch,
        input_output_aliases=aliases or {},
        compiler_params=pltpu.CompilerParams(vmem_limit_bytes=grant or 2 * moved + held + (2 << 20)),
        cost_estimate=pl.CostEstimate(flops=flops, bytes_accessed=0 if flops == 0 else moved, transcendentals=exps),
    )(*ins)


def shaped(rows, columns, dtype=BF):
    return jax.ShapeDtypeStruct((rows, columns), dtype)


def dot(a, b):
    return jnp.dot(a, b, preferred_element_type=F32)


def arranged(parts, pieces, rows):
    runs = []
    for which, to, start in sorted(pieces, key=lambda piece: piece[1]):
        if runs and runs[-1][0] == which and runs[-1][1] + runs[-1][3] == to and runs[-1][2] + runs[-1][3] == start:
            runs[-1][3] += CAP
        else:
            runs.append([which, to, start, CAP])
    out, at, width = [], 0, parts[0].shape[1]
    for which, to, start, count in runs + [[None, rows, 0, 0]]:
        if to > at:
            out.append(jnp.zeros((to - at, width), F32))
        if count:
            out.append(parts[which][start : start + count])
        at = to + count
    return jnp.concatenate(out, axis=0) if len(out) > 1 else out[0]


class Plan:
    def __init__(self, count, cuts):
        self.experts = count // 2
        self.bits = [1 << i for i in reversed(range(1, count.bit_length() - 1))]
        self.first = keep = [(0, d, c) for c in range(cuts) for d in range(self.experts)]
        send = [(0, d + self.experts, c) for _, d, c in keep]
        self.there = []
        for bit, later in zip(self.bits, self.bits[1:] + [1]):
            stage, keep, send = self.split(self.pool(keep, send, bit), lambda group: group[1] & later)
            self.there.append(stage)
        self.arrived = [(s, c) for s, _, c in keep]
        near = [s for s, c in self.arrived if c == 0]
        self.near, self.sources = near, near + [s ^ 1 for s in near]
        self.leaving = [(s, c) for c in range(cuts) for s in near]
        self.back = []
        pool = [(i, j, (s, i, c)) for i in range(2) for j, (s, c) in enumerate(self.leaving)]
        for bit in reversed(self.bits):
            stage, keep, send = self.split(pool, lambda group: group[0] & bit)
            self.back.append(stage)
            pool = self.pool(keep, send, bit)
        self.last = keep

    def pool(self, keep, send, bit):
        received = [(s ^ bit, d ^ bit, c) for s, d, c in send]
        return [(0, i, g) for i, g in enumerate(keep)] + [(1, i, g) for i, g in enumerate(received)]

    def split(self, pool, goes):
        stage, groups = ([], []), ([], [])
        for which, place, group in pool:
            side = 1 if goes(group) else 0
            stage[side].append((which, len(groups[side]) * CAP, place * CAP))
            groups[side].append(group)
        return stage, groups[0], groups[1]


def ranked(ids, weight, earlier, rows, here, groups):
    length = ids.shape[1]
    row = lax.broadcasted_iota(jnp.int32, (rows, 1), 0)
    expert = jnp.full((rows, 1), -1, jnp.int32)
    level = jnp.zeros((rows, 1), jnp.int32)
    for place, (_, target, _) in enumerate(groups):
        inside = (row >= place * CAP) & (row < (place + 1) * CAP)
        expert = jnp.where(inside, here ^ target, expert)
        level = jnp.where(inside, row - place * CAP, level)
    hits = jnp.zeros((rows, length), F32)
    share = jnp.zeros((rows, length), F32)
    for pick in range(ids.shape[0]):
        named = ids[pick : pick + 1, :] == expert
        hits = hits + jnp.where(named, 1.0, 0.0)
        if weight is not None:
            share = share + jnp.where(named, weight[pick : pick + 1, :], 0.0)
    ranks = dot(hits.astype(BF), earlier)
    chosen = (hits > 0.5) & (jnp.abs(ranks - level.astype(F32)) < 0.5)
    return jnp.where(chosen, 1.0 if weight is None else share, 0.0)


def cut_rows(matrix, groups, cut):
    row = lax.broadcasted_iota(jnp.int32, (matrix.shape[0], 1), 0)
    inside = jnp.zeros(row.shape, jnp.bool_)
    for place, (_, _, c) in enumerate(groups):
        if c == cut:
            inside = inside | ((row >= place * CAP) & (row < (place + 1) * CAP))
    return jnp.where(inside, matrix, 0.0).astype(BF)


def body(queries, key_rows, value_rows, segments, hidden_entry_rows, expert_ids, route_weight, w_gate, w_up, w_down):
    length = queries.shape[1]
    blocks, sides, cores = lax.axis_size("blk"), lax.axis_size("side"), lax.axis_size("tp")
    quarter, ff = w_gate.shape[1], w_gate.shape[2]
    cuts = next((c for c in (1, 2, 4) if blocks // 2 * CAP * c % 8 == 0 and quarter % (c * 128) == 0), 1)
    plan = Plan(blocks, cuts)
    experts, narrow = plan.experts, quarter // cuts
    ids, shares = expert_ids[0].T, route_weight[0].T
    picks = ids.shape[0]

    def columns_of(run, piece, pieces):
        place = ((lax.axis_index("blk") // experts) ^ run) * pieces + piece
        width = quarter // pieces
        return pl.ds(pl.multiple_of(place * width, width), width)

    def own_expert():
        return lax.axis_index("blk") % experts

    def over_side(value, offset, low):
        return swapped(value, ("blk", "side"), low * sides + offset)

    first_rows = up_to(len(plan.first) * CAP, 8)
    wide = hidden_entry_rows.shape[2]

    def before(before_ref):
        i = lax.broadcasted_iota(jnp.int32, (length, length), 0)
        j = lax.broadcasted_iota(jnp.int32, (length, length), 1)
        before_ref[...] = jnp.where(i < j, 1.0, 0.0).astype(BF)

    (earlier,) = call(before, [shaped(length, length)], flops=COST)

    def rank(earlier_ref, ids_ref, out_ref):
        chosen = ranked(ids_ref[...], None, earlier_ref[...], first_rows, own_expert(), plan.first)
        for cut in range(cuts):
            out_ref[cut] = cut_rows(chosen, plan.first, cut)

    (chosen,) = call(rank, [jax.ShapeDtypeStruct((cuts, first_rows, length), BF)], earlier, ids)

    def choose(run):
        def kernel(chosen_ref, x_ref, out_ref):
            total = 0.0
            for cut in range(cuts):
                total = total + dot(chosen_ref[cut], x_ref[:, columns_of(run, cut, cuts)])
            out_ref[...] = total.astype(BF)

        return call(kernel, [shaped(first_rows, narrow)], chosen, hidden_entry_rows[0], flops=COST)[0]

    send, keep = choose(1), choose(0)

    def share_out(earlier_ref, ids_ref, weight_ref, share_ref):
        share = ranked(ids_ref[...], weight_ref[...], earlier_ref[...], first_rows, own_expert(), plan.last)
        for cut in range(cuts):
            share_ref[cut] = cut_rows(share, plan.last, cut).astype(F32).T.astype(BF)

    (share,) = call(share_out, [jax.ShapeDtypeStruct((cuts, length, first_rows), BF)], earlier, ids, shares)

    def pack(after_ref, key_ref, value_ref, segment_ref, held_ref, segment_here, sems):
        copies = [
            pltpu.make_async_copy(key_ref, held_ref.at[0, pl.ds(0, length)], sems.at[0]),
            pltpu.make_async_copy(value_ref, held_ref.at[0, pl.ds(length, length)], sems.at[1]),
            pltpu.make_async_copy(segment_ref, segment_here, sems.at[2]),
        ]
        for copy in copies:
            copy.start()
        copies[2].wait()
        labels = jnp.broadcast_to(segment_here[...].astype(F32), (16, length))
        held_ref[0, 2 * length : 2 * length + 16, :] = labels.astype(BF)
        copies[0].wait()
        copies[1].wait()

    (held,) = call(
        pack,
        [jax.ShapeDtypeStruct((1, 2 * length + 16, HEAD_DIM), BF)],
        send,
        key_rows[0],
        value_rows[0],
        segments,
        scratch=[pltpu.VMEM((1, length), jnp.int32)],
        semaphores=3,
        far_in=(1, 2, 3),
    )

    def sort(stage, *parts):
        sizes = [up_to(len(pieces) * CAP, 8) for pieces in stage]

        def kernel(*refs):
            values = [ref[...].astype(F32) for ref in refs[: len(parts)]]
            for pieces, size, out in zip(stage, sizes, refs[len(parts) :]):
                out[...] = arranged(values, pieces, size).astype(BF)

        return call(
            kernel,
            [shaped(size, narrow) for size in sizes],
            *parts,
            flops=COST,
        )

    for bit, stage in zip(plan.bits, plan.there):
        received, held = lax.optimization_barrier((swapped(send, "blk", bit), held))
        keep, send = sort(stage, keep, received)
    part_rows = len(plan.near) * CAP
    padded = keep.shape[0]
    own = [keep] + [over_side(keep, offset, 0) for offset in range(1, sides)]
    other = [over_side(send, offset, 1) for offset in range(sides)]

    held, _ = lax.optimization_barrier((held, keep))
    nearby = [1 << i for i in reversed(range(blocks.bit_length() - 1))]
    order = [0]
    received_held = swapped(held, "blk", nearby[0])

    def join(after_ref, held_ref, received_ref, both_ref):
        both_ref[: held_ref.shape[0]] = held_ref[...]
        both_ref[held_ref.shape[0] :] = received_ref[...]

    def joined(after, held, received_held, flops):
        both = jax.ShapeDtypeStruct((2 * held.shape[0], *held.shape[1:]), BF)
        return call(join, [both], after, held, received_held, flops=flops)[0]

    side_rows = 2 * part_rows

    half = sides // 2 * side_rows

    def by_source(build):
        here = build(lambda source: plan.near.index(source) * CAP)
        there = build(lambda source: plan.near.index(source ^ experts) * CAP)
        return jnp.where(lax.axis_index("blk") >= experts, there, here)

    def project(*refs):
        own_refs, other_refs, (gate_ref, up_ref, *out_refs) = refs[:sides], refs[sides : 2 * sides], refs[2 * sides :]
        mine = lax.axis_index("tp") == 0
        away, stay = [], []
        for refs_of in (own_refs, other_refs):
            for at in range(sides // 2):
                low, high = refs_of[at][...].astype(F32), refs_of[sides // 2 + at][...].astype(F32)
                away.append(jnp.where(mine, high, low))
                stay.append(jnp.where(mine, low, high))

        def build(row_of, rows, cut):
            pieces = []
            for part in range(2):
                for at in range(sides // 2):
                    for place, (source, c) in enumerate(plan.arrived):
                        if c == cut:
                            to = at * side_rows + part * part_rows + row_of(source)
                            pieces.append((part * (sides // 2) + at, to, place * CAP))
            return arranged(rows, pieces, half)

        both = jnp.concatenate(
            [
                jnp.concatenate([by_source(lambda row_of: build(row_of, rows, cut)) for cut in range(cuts)], axis=1)
                for rows in (away, stay)
            ],
            axis=0,
        ).astype(BF)
        for weight, send_ref, keep_ref in ((gate_ref, *out_refs[:2]), (up_ref, *out_refs[2:])):
            terms = dot(both, weight[...])
            send_ref[...] = terms[:half].astype(BF)
            keep_ref[...] = terms[half:]

    gate_send, gate_keep, up_send, up_keep = call(
        project,
        [shaped(half, ff), shaped(half, ff, F32)] * 2,
        *own,
        *other,
        w_gate[0],
        w_up[0],
    )
    gate_received, up_received = swapped(gate_send, "tp", 1), swapped(up_send, "tp", 1)

    def add_terms(gate_keep_ref, gate_received_ref, up_keep_ref, up_received_ref, sum_ref, send_ref):
        for at, keep_ref, received_ref in ((0, gate_keep_ref, gate_received_ref), (ff, up_keep_ref, up_received_ref)):
            total = keep_ref[...] + received_ref[...].astype(F32)
            sum_ref[:, at : at + ff] = total
            send_ref[:, at : at + ff] = total.astype(BF)

    sums, sums_send = call(
        add_terms,
        [shaped(half, 2 * ff, F32), shaped(half, 2 * ff)],
        gate_keep,
        gate_received,
        up_keep,
        up_received,
    )
    sums_received = swapped(sums_send, "blk", experts)
    for bit in nearby[1:]:
        held = joined(sums_send, held, received_held, COST)
        received_held = swapped(held, "blk", bit)
    held = joined(sums_send, held, received_held, 0)
    for bit in nearby:
        order = order + [place ^ bit for place in order]

    def activate(sum_ref, received_ref, hidden_ref):
        gate = sum_ref[:, :ff] + received_ref[:, :ff].astype(F32)
        up = sum_ref[:, ff:] + received_ref[:, ff:].astype(F32)
        hidden_ref[...] = (gate / (1.0 + jnp.exp(-gate)) * up).astype(BF)

    (hidden,) = call(activate, [shaped(half, ff)], sums, sums_received, exps=half * ff)
    hidden_received = swapped(hidden, "tp", 1)

    def project_back(hidden_ref, received_ref, down_ref, *out_refs):
        mine = lax.axis_index("tp") == 0
        here, there = hidden_ref[...].astype(F32), received_ref[...].astype(F32)
        ordered = [jnp.where(mine, here, there), jnp.where(mine, there, here)]
        spaced = up_to(part_rows, 8)

        def build(row_of):
            pieces = []
            for at in range(sides):
                for part in range(2):
                    for place, source in enumerate(plan.near):
                        to = (2 * at + part) * spaced + place * CAP
                        start = at % (sides // 2) * side_rows + part * part_rows + row_of(source)
                        pieces.append((at // (sides // 2), to, start))
            return arranged(ordered, pieces, 2 * sides * spaced)

        total = by_source(build)
        out = dot(total.astype(BF), down_ref[...])
        for place, out_ref in enumerate(out_refs):
            rows = out[place * spaced : place * spaced + part_rows]
            pieces = [rows[:, cut * narrow : (cut + 1) * narrow] for cut in range(cuts)]
            out_ref[...] = jnp.concatenate(pieces, axis=0).astype(out_ref.dtype)

    outs = call(
        project_back,
        [shaped(padded, narrow, BF if place else F32) for place in range(2 * sides)],
        hidden,
        hidden_received,
        w_down[0],
        flops=4 * half * ff * quarter,
    )
    own = [outs[0]] + [over_side(outs[2 * offset], offset, 0) for offset in range(1, sides)]
    other = [over_side(outs[2 * offset + 1], offset, 1) for offset in range(sides)]

    heads = queries.shape[2] // HEAD_DIM
    factor = 1.0 / math.sqrt(HEAD_DIM)
    span = blocks * length
    batch = math.gcd(heads, max(1, 2048 // span))

    def attend(query_ref, held_ref, segment_ref, out_ref, keys, values, bias):
        here = lax.axis_index("blk")
        i = lax.broadcasted_iota(jnp.int32, (length, length), 0)
        j = lax.broadcasted_iota(jnp.int32, (length, length), 1)
        label_here = jnp.sum(jnp.where(i == j, segment_ref[...].astype(F32), 0.0), axis=1, keepdims=True)
        for place, other_block in enumerate(order):
            at = place * length
            keys[at : at + length, :] = held_ref[place, :length, :]
            values[at : at + length, :] = held_ref[place, length : 2 * length, :]
            label = held_ref[place, 2 * length : 2 * length + 16, :].astype(F32)[:1]
            same = label_here == label
            if other_block == 0:
                seen = same & (j <= i)
            else:
                seen = same & ((here ^ other_block) < here)
            bias[:, at : at + length] = jnp.where(seen, 0.0, -1e30)

        def some_heads(first):
            columns = [pl.ds(pl.multiple_of((first + h) * HEAD_DIM, HEAD_DIM), HEAD_DIM) for h in range(batch)]
            query = jnp.concatenate([query_ref[:, c] for c in columns], axis=0)
            scores = lax.dot_general(query, keys[...], (((1,), (1,)), ((), ())), preferred_element_type=F32)
            scores = (scores.reshape(batch, length, span) + bias[...][None]).reshape(batch * length, span)
            top = jnp.max(scores, axis=1, keepdims=True)
            weights = jnp.exp((scores - top) * factor)
            totals = jnp.sum(weights, axis=1, keepdims=True)
            out = (dot(weights.astype(BF), values[...]) / totals).astype(BF)
            for h, c in enumerate(columns):
                out_ref[:, c] = out[h * length : (h + 1) * length]

        if span <= 1024:
            for first in range(0, heads, batch):
                some_heads(first)
        else:
            lax.fori_loop(0, heads // batch, lambda step, _: (some_heads(step * batch), 0)[1], 0)

    segments_then, _ = lax.optimization_barrier((segments, outs[1]))
    (attended,) = call(
        attend,
        [shaped(length, heads * HEAD_DIM)],
        queries[0],
        held,
        segments_then,
        scratch=[pltpu.VMEM((span, HEAD_DIM), BF)] * 2 + [pltpu.VMEM((length, span), F32)],
        flops=4 * heads * length * span * HEAD_DIM,
        exps=heads * length * span,
    )
    other[-1], attended = lax.optimization_barrier((other[-1], attended))

    def add_parts(*refs):
        sums = []
        for part in (refs[:sides], refs[sides : 2 * sides]):
            total = part[0][...].astype(F32)
            for ref in part[1:]:
                total = total + ref[...].astype(F32)
            sums.append(total)
        for pieces, out in zip(plan.back[0], refs[2 * sides :]):
            out[...] = arranged(sums, pieces, out.shape[0]).astype(BF)

    keep, send = call(
        add_parts,
        [shaped(up_to(len(pieces) * CAP, 8), narrow) for pieces in plan.back[0]],
        *own,
        *other,
        flops=8 * padded * padded * quarter,
    )
    for bit, stage in zip(plan.bits[::-1], plan.back[1:]):
        keep, send = sort(stage, keep, swapped(send, "blk", bit))
    received = swapped(send, "blk", plan.bits[0])

    def mix(run):
        def kernel(share_ref, rows_ref, *refs):
            out_ref, here, sems = refs[-3:]
            copies = []
            for at in range(4):
                cut, within = at * cuts // 4, at % (4 // cuts)
                rows = rows_ref[:, within * (quarter // 4) : (within + 1) * (quarter // 4)]
                here[at] = dot(share_ref[cut], rows).astype(BF)
                target = out_ref.at[:, columns_of(run, at, 4)]
                copies.append(pltpu.make_async_copy(here.at[at], target, sems.at[at]))
                copies[-1].start()
            for copy in copies:
                copy.wait()

        return kernel

    moe_out = None
    for run, rows in ((0, keep), (1, received)):
        ins = [share, rows] + ([] if moe_out is None else [moe_out])
        (moe_out,) = call(
            mix(run),
            [shaped(length, wide)],
            *ins,
            scratch=[pltpu.VMEM((4, length, quarter // 4), BF)],
            semaphores=4,
            far_in=(2,),
            far_out=(0,),
            aliases={2: 0} if run else None,
            flops=4 * length * first_rows * quarter,
        )
    return attended[None], moe_out[None]


def solution(mesh):
    rows = P(("groups", "side"), "blk", "tp")
    placed = (
        rows,
        rows,
        rows,
        P(("groups", "side"), "blk"),
        rows,
        P(("groups", "side"), "blk", None),
        P(("groups", "side"), "blk", None),
        P("blk", "tp", "side"),
        P("blk", "tp", "side"),
        P("blk", "side", "tp"),
    )
    return jax.shard_map(body, mesh=mesh, in_specs=placed, out_specs=(rows, rows), check_vma=False)
```

```python
import math

import jax
import jax.numpy as jnp
from jax import lax
from jax.experimental import pallas as pl
from jax.experimental.pallas import tpu as pltpu
from jax.sharding import PartitionSpec as P

HEAD_DIM = 128
CAP = 10
COST = 3_000_000_000
BF = jnp.bfloat16
F32 = jnp.float32
VMEM = pl.BlockSpec(memory_space=pltpu.VMEM)
HBM = pl.BlockSpec(memory_space=pltpu.HBM)


def swapped(value, axis, bit):
    count = lax.axis_size(axis)
    return lax.ppermute(value, axis, [(i, i ^ bit) for i in range(count)])


def up_to(value, step):
    return -(-value // step) * step


def call(kernel, outs, *ins, scratch=(), semaphores=0, far_in=(), far_out=(), aliases=None, flops=0, exps=0, grant=0):
    moved = sum(math.prod(a.shape) * a.dtype.itemsize for a in (*ins, *outs))
    held = sum(math.prod(s.shape) * s.dtype.itemsize for s in scratch)
    scratch = list(scratch) + ([pltpu.SemaphoreType.DMA((semaphores,))] if semaphores else [])
    return pl.pallas_call(
        kernel,
        out_shape=list(outs),
        in_specs=[HBM if i in far_in else VMEM for i in range(len(ins))],
        out_specs=[HBM if i in far_out else VMEM for i in range(len(outs))],
        scratch_shapes=scratch,
        input_output_aliases=aliases or {},
        compiler_params=pltpu.CompilerParams(vmem_limit_bytes=grant or 2 * moved + held + (2 << 20)),
        cost_estimate=pl.CostEstimate(flops=flops, bytes_accessed=0 if flops == 0 else moved, transcendentals=exps),
    )(*ins)


def shaped(rows, columns, dtype=BF):
    return jax.ShapeDtypeStruct((rows, columns), dtype)


def dot(a, b):
    return jnp.dot(a, b, preferred_element_type=F32)


def arranged(parts, pieces, rows):
    runs = []
    for which, to, start in sorted(pieces, key=lambda piece: piece[1]):
        if runs and runs[-1][0] == which and runs[-1][1] + runs[-1][3] == to and runs[-1][2] + runs[-1][3] == start:
            runs[-1][3] += CAP
        else:
            runs.append([which, to, start, CAP])
    out, at, width = [], 0, parts[0].shape[1]
    for which, to, start, count in runs + [[None, rows, 0, 0]]:
        if to > at:
            out.append(jnp.zeros((to - at, width), F32))
        if count:
            out.append(parts[which][start : start + count])
        at = to + count
    return jnp.concatenate(out, axis=0) if len(out) > 1 else out[0]


class Plan:
    def __init__(self, count, cuts):
        self.experts = count // 2
        self.bits = [1 << i for i in reversed(range(1, count.bit_length() - 1))]
        self.first = keep = [(0, d, c) for c in range(cuts) for d in range(self.experts)]
        send = [(0, d + self.experts, c) for _, d, c in keep]
        self.there = []
        for bit, later in zip(self.bits, self.bits[1:] + [1]):
            stage, keep, send = self.split(self.pool(keep, send, bit), lambda group: group[1] & later)
            self.there.append(stage)
        self.arrived = [(s, c) for s, _, c in keep]
        near = [s for s, c in self.arrived if c == 0]
        self.near, self.sources = near, near + [s ^ 1 for s in near]
        self.leaving = [(s, c) for c in range(cuts) for s in near]
        self.back = []
        pool = [(i, j, (s, i, c)) for i in range(2) for j, (s, c) in enumerate(self.leaving)]
        for bit in reversed(self.bits):
            stage, keep, send = self.split(pool, lambda group: group[0] & bit)
            self.back.append(stage)
            pool = self.pool(keep, send, bit)
        self.last = keep

    def pool(self, keep, send, bit):
        received = [(s ^ bit, d ^ bit, c) for s, d, c in send]
        return [(0, i, g) for i, g in enumerate(keep)] + [(1, i, g) for i, g in enumerate(received)]

    def split(self, pool, goes):
        stage, groups = ([], []), ([], [])
        for which, place, group in pool:
            side = 1 if goes(group) else 0
            stage[side].append((which, len(groups[side]) * CAP, place * CAP))
            groups[side].append(group)
        return stage, groups[0], groups[1]


def ranked(ids, weight, earlier, rows, here, groups):
    length = ids.shape[1]
    row = lax.broadcasted_iota(jnp.int32, (rows, 1), 0)
    expert = jnp.full((rows, 1), -1, jnp.int32)
    level = jnp.zeros((rows, 1), jnp.int32)
    for place, (_, target, _) in enumerate(groups):
        inside = (row >= place * CAP) & (row < (place + 1) * CAP)
        expert = jnp.where(inside, here ^ target, expert)
        level = jnp.where(inside, row - place * CAP, level)
    hits = jnp.zeros((rows, length), F32)
    share = jnp.zeros((rows, length), F32)
    for pick in range(ids.shape[0]):
        named = ids[pick : pick + 1, :] == expert
        hits = hits + jnp.where(named, 1.0, 0.0)
        if weight is not None:
            share = share + jnp.where(named, weight[pick : pick + 1, :], 0.0)
    ranks = dot(hits.astype(BF), earlier)
    chosen = (hits > 0.5) & (jnp.abs(ranks - level.astype(F32)) < 0.5)
    return jnp.where(chosen, 1.0 if weight is None else share, 0.0)


def cut_rows(matrix, groups, cut):
    row = lax.broadcasted_iota(jnp.int32, (matrix.shape[0], 1), 0)
    inside = jnp.zeros(row.shape, jnp.bool_)
    for place, (_, _, c) in enumerate(groups):
        if c == cut:
            inside = inside | ((row >= place * CAP) & (row < (place + 1) * CAP))
    return jnp.where(inside, matrix, 0.0).astype(BF)


def body(queries, key_rows, value_rows, segments, hidden_entry_rows, expert_ids, route_weight, w_gate, w_up, w_down):
    length = queries.shape[1]
    blocks, sides, cores = lax.axis_size("blk"), lax.axis_size("side"), lax.axis_size("tp")
    quarter, ff = w_gate.shape[1], w_gate.shape[2]
    cuts = next((c for c in (1, 2, 4) if blocks // 2 * CAP * c % 8 == 0 and quarter % (c * 128) == 0), 1)
    plan = Plan(blocks, cuts)
    experts, narrow = plan.experts, quarter // cuts
    ids, shares = expert_ids[0].T, route_weight[0].T
    picks = ids.shape[0]

    def columns_of(run, piece, pieces):
        place = ((lax.axis_index("blk") // experts) ^ run) * pieces + piece
        width = quarter // pieces
        return pl.ds(pl.multiple_of(place * width, width), width)

    def own_expert():
        return lax.axis_index("blk") % experts

    def over_side(value, offset, low):
        return swapped(value, ("blk", "side"), low * sides + offset)

    first_rows = up_to(len(plan.first) * CAP, 8)
    wide = hidden_entry_rows.shape[2]

    def before(before_ref):
        i = lax.broadcasted_iota(jnp.int32, (length, length), 0)
        j = lax.broadcasted_iota(jnp.int32, (length, length), 1)
        before_ref[...] = jnp.where(i < j, 1.0, 0.0).astype(BF)

    (earlier,) = call(before, [shaped(length, length)], flops=COST)

    def rank(earlier_ref, ids_ref, out_ref):
        chosen = ranked(ids_ref[...], None, earlier_ref[...], first_rows, own_expert(), plan.first)
        for cut in range(cuts):
            out_ref[cut] = cut_rows(chosen, plan.first, cut)

    (chosen,) = call(rank, [jax.ShapeDtypeStruct((cuts, first_rows, length), BF)], earlier, ids)

    def choose(run):
        def kernel(chosen_ref, x_ref, out_ref):
            total = 0.0
            for cut in range(cuts):
                total = total + dot(chosen_ref[cut], x_ref[:, columns_of(run, cut, cuts)])
            out_ref[...] = total.astype(BF)

        return call(kernel, [shaped(first_rows, narrow)], chosen, hidden_entry_rows[0], flops=COST)[0]

    send, keep = choose(1), choose(0)

    def share_out(earlier_ref, ids_ref, weight_ref, share_ref):
        share = ranked(ids_ref[...], weight_ref[...], earlier_ref[...], first_rows, own_expert(), plan.last)
        for cut in range(cuts):
            share_ref[cut] = cut_rows(share, plan.last, cut).astype(F32).T.astype(BF)

    (share,) = call(share_out, [jax.ShapeDtypeStruct((cuts, length, first_rows), BF)], earlier, ids, shares)

    def pack(after_ref, key_ref, value_ref, segment_ref, held_ref, segment_here, sems):
        copies = [
            pltpu.make_async_copy(key_ref, held_ref.at[0, pl.ds(0, length)], sems.at[0]),
            pltpu.make_async_copy(value_ref, held_ref.at[0, pl.ds(length, length)], sems.at[1]),
            pltpu.make_async_copy(segment_ref, segment_here, sems.at[2]),
        ]
        for copy in copies:
            copy.start()
        copies[2].wait()
        labels = jnp.broadcast_to(segment_here[...].astype(F32), (16, length))
        held_ref[0, 2 * length : 2 * length + 16, :] = labels.astype(BF)
        copies[0].wait()
        copies[1].wait()

    (held,) = call(
        pack,
        [jax.ShapeDtypeStruct((1, 2 * length + 16, HEAD_DIM), BF)],
        send,
        key_rows[0],
        value_rows[0],
        segments,
        scratch=[pltpu.VMEM((1, length), jnp.int32)],
        semaphores=3,
        far_in=(1, 2, 3),
    )

    def sort(stage, *parts):
        sizes = [up_to(len(pieces) * CAP, 8) for pieces in stage]

        def kernel(*refs):
            values = [ref[...].astype(F32) for ref in refs[: len(parts)]]
            for pieces, size, out in zip(stage, sizes, refs[len(parts) :]):
                out[...] = arranged(values, pieces, size).astype(BF)

        return call(
            kernel,
            [shaped(size, narrow) for size in sizes],
            *parts,
            flops=COST,
        )

    for bit, stage in zip(plan.bits, plan.there):
        received, held = lax.optimization_barrier((swapped(send, "blk", bit), held))
        keep, send = sort(stage, keep, received)
    part_rows = len(plan.near) * CAP
    padded = keep.shape[0]
    own = [keep] + [over_side(keep, offset, 0) for offset in range(1, sides)]
    other = [over_side(send, offset, 1) for offset in range(sides)]

    held, _ = lax.optimization_barrier((held, keep))
    nearby = [1 << i for i in reversed(range(blocks.bit_length() - 1))]
    order = [0]
    received_held = swapped(held, "blk", nearby[0])

    def join(after_ref, held_ref, received_ref, both_ref):
        both_ref[: held_ref.shape[0]] = held_ref[...]
        both_ref[held_ref.shape[0] :] = received_ref[...]

    def joined(after, held, received_held, flops):
        both = jax.ShapeDtypeStruct((2 * held.shape[0], *held.shape[1:]), BF)
        return call(join, [both], after, held, received_held, flops=flops)[0]

    side_rows = 2 * part_rows

    half = sides // 2 * side_rows

    def by_source(build):
        here = build(lambda source: plan.near.index(source) * CAP)
        there = build(lambda source: plan.near.index(source ^ experts) * CAP)
        return jnp.where(lax.axis_index("blk") >= experts, there, here)

    def project(*refs):
        own_refs, other_refs, (gate_ref, up_ref, *out_refs) = refs[:sides], refs[sides : 2 * sides], refs[2 * sides :]
        mine = lax.axis_index("tp") == 0
        away, stay = [], []
        for refs_of in (own_refs, other_refs):
            for at in range(sides // 2):
                low, high = refs_of[at][...].astype(F32), refs_of[sides // 2 + at][...].astype(F32)
                away.append(jnp.where(mine, high, low))
                stay.append(jnp.where(mine, low, high))

        def build(row_of, rows, cut):
            pieces = []
            for part in range(2):
                for at in range(sides // 2):
                    for place, (source, c) in enumerate(plan.arrived):
                        if c == cut:
                            to = at * side_rows + part * part_rows + row_of(source)
                            pieces.append((part * (sides // 2) + at, to, place * CAP))
            return arranged(rows, pieces, half)

        both = jnp.concatenate(
            [
                jnp.concatenate([by_source(lambda row_of: build(row_of, rows, cut)) for cut in range(cuts)], axis=1)
                for rows in (away, stay)
            ],
            axis=0,
        ).astype(BF)
        for weight, send_ref, keep_ref in ((gate_ref, *out_refs[:2]), (up_ref, *out_refs[2:])):
            terms = dot(both, weight[...])
            send_ref[...] = terms[:half].astype(BF)
            keep_ref[...] = terms[half:]

    gate_send, gate_keep, up_send, up_keep = call(
        project,
        [shaped(half, ff), shaped(half, ff, F32)] * 2,
        *own,
        *other,
        w_gate[0],
        w_up[0],
    )
    gate_received, up_received = swapped(gate_send, "tp", 1), swapped(up_send, "tp", 1)

    def add_terms(gate_keep_ref, gate_received_ref, up_keep_ref, up_received_ref, sum_ref, send_ref):
        for at, keep_ref, received_ref in ((0, gate_keep_ref, gate_received_ref), (ff, up_keep_ref, up_received_ref)):
            total = keep_ref[...] + received_ref[...].astype(F32)
            sum_ref[:, at : at + ff] = total
            send_ref[:, at : at + ff] = total.astype(BF)

    sums, sums_send = call(
        add_terms,
        [shaped(half, 2 * ff, F32), shaped(half, 2 * ff)],
        gate_keep,
        gate_received,
        up_keep,
        up_received,
    )
    sums_received = swapped(sums_send, "blk", experts)
    for bit in nearby[1:]:
        held = joined(sums_send, held, received_held, COST)
        received_held = swapped(held, "blk", bit)
    held = joined(sums_send, held, received_held, 0)
    for bit in nearby:
        order = order + [place ^ bit for place in order]

    def activate(sum_ref, received_ref, hidden_ref):
        gate = sum_ref[:, :ff] + received_ref[:, :ff].astype(F32)
        up = sum_ref[:, ff:] + received_ref[:, ff:].astype(F32)
        hidden_ref[...] = (gate / (1.0 + jnp.exp(-gate)) * up).astype(BF)

    (hidden,) = call(activate, [shaped(half, ff)], sums, sums_received, exps=half * ff)
    hidden_received = swapped(hidden, "tp", 1)

    def project_back(hidden_ref, received_ref, down_ref, *out_refs):
        mine = lax.axis_index("tp") == 0
        here, there = hidden_ref[...].astype(F32), received_ref[...].astype(F32)
        ordered = [jnp.where(mine, here, there), jnp.where(mine, there, here)]
        spaced = up_to(part_rows, 8)

        def build(row_of):
            pieces = []
            for at in range(sides):
                for part in range(2):
                    for place, source in enumerate(plan.near):
                        to = (2 * at + part) * spaced + place * CAP
                        start = at % (sides // 2) * side_rows + part * part_rows + row_of(source)
                        pieces.append((at // (sides // 2), to, start))
            return arranged(ordered, pieces, 2 * sides * spaced)

        total = by_source(build)
        out = dot(total.astype(BF), down_ref[...])
        for place, out_ref in enumerate(out_refs):
            rows = out[place * spaced : place * spaced + part_rows]
            pieces = [rows[:, cut * narrow : (cut + 1) * narrow] for cut in range(cuts)]
            out_ref[...] = jnp.concatenate(pieces, axis=0).astype(out_ref.dtype)

    outs = call(
        project_back,
        [shaped(padded, narrow, BF if place else F32) for place in range(2 * sides)],
        hidden,
        hidden_received,
        w_down[0],
        flops=4 * half * ff * quarter,
    )
    other = [over_side(outs[2 * offset + 1], offset, 1) for offset in reversed(range(sides))][::-1]
    own = [outs[0]] + [over_side(outs[2 * offset], offset, 0) for offset in range(1, sides)]

    heads = queries.shape[2] // HEAD_DIM
    factor = 1.0 / math.sqrt(HEAD_DIM)
    span = blocks * length
    batch = math.gcd(heads, max(1, 2048 // span))

    def attend(query_ref, held_ref, segment_ref, out_ref, keys, values, bias):
        here = lax.axis_index("blk")
        i = lax.broadcasted_iota(jnp.int32, (length, length), 0)
        j = lax.broadcasted_iota(jnp.int32, (length, length), 1)
        label_here = jnp.sum(jnp.where(i == j, segment_ref[...].astype(F32), 0.0), axis=1, keepdims=True)
        for place, other_block in enumerate(order):
            at = place * length
            keys[at : at + length, :] = held_ref[place, :length, :]
            values[at : at + length, :] = held_ref[place, length : 2 * length, :]
            label = held_ref[place, 2 * length : 2 * length + 16, :].astype(F32)[:1]
            same = label_here == label
            if other_block == 0:
                seen = same & (j <= i)
            else:
                seen = same & ((here ^ other_block) < here)
            bias[:, at : at + length] = jnp.where(seen, 0.0, -1e30)

        def some_heads(first):
            columns = [pl.ds(pl.multiple_of((first + h) * HEAD_DIM, HEAD_DIM), HEAD_DIM) for h in range(batch)]
            query = jnp.concatenate([query_ref[:, c] for c in columns], axis=0)
            scores = lax.dot_general(query, keys[...], (((1,), (1,)), ((), ())), preferred_element_type=F32)
            scores = (scores.reshape(batch, length, span) + bias[...][None]).reshape(batch * length, span)
            top = jnp.max(scores, axis=1, keepdims=True)
            weights = jnp.exp((scores - top) * factor)
            totals = jnp.sum(weights, axis=1, keepdims=True)
            out = (dot(weights.astype(BF), values[...]) / totals).astype(BF)
            for h, c in enumerate(columns):
                out_ref[:, c] = out[h * length : (h + 1) * length]

        if span <= 1024:
            for first in range(0, heads, batch):
                some_heads(first)
        else:
            lax.fori_loop(0, heads // batch, lambda step, _: (some_heads(step * batch), 0)[1], 0)

    segments_then, _ = lax.optimization_barrier((segments, outs[1]))
    (attended,) = call(
        attend,
        [shaped(length, heads * HEAD_DIM)],
        queries[0],
        held,
        segments_then,
        scratch=[pltpu.VMEM((span, HEAD_DIM), BF)] * 2 + [pltpu.VMEM((length, span), F32)],
        flops=4 * heads * length * span * HEAD_DIM,
        exps=heads * length * span,
    )
    own[0], attended = lax.optimization_barrier((own[0], attended))

    def add_parts(*refs):
        sums = []
        for part in (refs[:sides], refs[sides : 2 * sides]):
            total = part[0][...].astype(F32)
            for ref in part[1:]:
                total = total + ref[...].astype(F32)
            sums.append(total)
        for pieces, out in zip(plan.back[0], refs[2 * sides :]):
            out[...] = arranged(sums, pieces, out.shape[0]).astype(BF)

    keep, send = call(
        add_parts,
        [shaped(up_to(len(pieces) * CAP, 8), narrow) for pieces in plan.back[0]],
        *own,
        *other,
        flops=8 * padded * padded * quarter,
    )
    for bit, stage in zip(plan.bits[::-1], plan.back[1:]):
        keep, send = sort(stage, keep, swapped(send, "blk", bit))
    received = swapped(send, "blk", plan.bits[0])

    def mix(run):
        def kernel(share_ref, rows_ref, *refs):
            out_ref, here, sems = refs[-3:]
            copies = []
            for at in range(4):
                cut, within = at * cuts // 4, at % (4 // cuts)
                rows = rows_ref[:, within * (quarter // 4) : (within + 1) * (quarter // 4)]
                here[at] = dot(share_ref[cut], rows).astype(BF)
                target = out_ref.at[:, columns_of(run, at, 4)]
                copies.append(pltpu.make_async_copy(here.at[at], target, sems.at[at]))
                copies[-1].start()
            for copy in copies:
                copy.wait()

        return kernel

    moe_out = None
    for run, rows in ((0, keep), (1, received)):
        ins = [share, rows] + ([] if moe_out is None else [moe_out])
        (moe_out,) = call(
            mix(run),
            [shaped(length, wide)],
            *ins,
            scratch=[pltpu.VMEM((4, length, quarter // 4), BF)],
            semaphores=4,
            far_in=(2,),
            far_out=(0,),
            aliases={2: 0} if run else None,
            flops=4 * length * first_rows * quarter,
        )
    return attended[None], moe_out[None]


def solution(mesh):
    rows = P(("groups", "side"), "blk", "tp")
    placed = (
        rows,
        rows,
        rows,
        P(("groups", "side"), "blk"),
        rows,
        P(("groups", "side"), "blk", None),
        P(("groups", "side"), "blk", None),
        P("blk", "tp", "side"),
        P("blk", "tp", "side"),
        P("blk", "side", "tp"),
    )
    return jax.shard_map(body, mesh=mesh, in_specs=placed, out_specs=(rows, rows), check_vma=False)
```

```python
import math

import jax
import jax.numpy as jnp
from jax import lax
from jax.experimental import pallas as pl
from jax.experimental.pallas import tpu as pltpu
from jax.sharding import PartitionSpec as P

HEAD_DIM = 128
CAP = 10
COST = 3_000_000_000
BF = jnp.bfloat16
F32 = jnp.float32
VMEM = pl.BlockSpec(memory_space=pltpu.VMEM)
HBM = pl.BlockSpec(memory_space=pltpu.HBM)


def swapped(value, axis, bit):
    count = lax.axis_size(axis)
    return lax.ppermute(value, axis, [(i, i ^ bit) for i in range(count)])


def up_to(value, step):
    return -(-value // step) * step


def call(kernel, outs, *ins, scratch=(), semaphores=0, far_in=(), far_out=(), aliases=None, flops=0, exps=0, grant=0):
    moved = sum(math.prod(a.shape) * a.dtype.itemsize for a in (*ins, *outs))
    held = sum(math.prod(s.shape) * s.dtype.itemsize for s in scratch)
    scratch = list(scratch) + ([pltpu.SemaphoreType.DMA((semaphores,))] if semaphores else [])
    return pl.pallas_call(
        kernel,
        out_shape=list(outs),
        in_specs=[HBM if i in far_in else VMEM for i in range(len(ins))],
        out_specs=[HBM if i in far_out else VMEM for i in range(len(outs))],
        scratch_shapes=scratch,
        input_output_aliases=aliases or {},
        compiler_params=pltpu.CompilerParams(vmem_limit_bytes=grant or 2 * moved + held + (2 << 20)),
        cost_estimate=pl.CostEstimate(flops=flops, bytes_accessed=0 if flops == 0 else moved, transcendentals=exps),
    )(*ins)


def shaped(rows, columns, dtype=BF):
    return jax.ShapeDtypeStruct((rows, columns), dtype)


def dot(a, b):
    return jnp.dot(a, b, preferred_element_type=F32)


def arranged(parts, pieces, rows):
    runs = []
    for which, to, start in sorted(pieces, key=lambda piece: piece[1]):
        if runs and runs[-1][0] == which and runs[-1][1] + runs[-1][3] == to and runs[-1][2] + runs[-1][3] == start:
            runs[-1][3] += CAP
        else:
            runs.append([which, to, start, CAP])
    out, at, width = [], 0, parts[0].shape[1]
    for which, to, start, count in runs + [[None, rows, 0, 0]]:
        if to > at:
            out.append(jnp.zeros((to - at, width), F32))
        if count:
            out.append(parts[which][start : start + count])
        at = to + count
    return jnp.concatenate(out, axis=0) if len(out) > 1 else out[0]


class Plan:
    def __init__(self, count, cuts):
        self.experts = count // 2
        self.bits = [1 << i for i in reversed(range(1, count.bit_length() - 1))]
        self.first = keep = [(0, d, c) for c in range(cuts) for d in range(self.experts)]
        send = [(0, d + self.experts, c) for _, d, c in keep]
        self.there = []
        for bit, later in zip(self.bits, self.bits[1:] + [1]):
            stage, keep, send = self.split(self.pool(keep, send, bit), lambda group: group[1] & later)
            self.there.append(stage)
        self.arrived = [(s, c) for s, _, c in keep]
        near = [s for s, c in self.arrived if c == 0]
        self.near, self.sources = near, near + [s ^ 1 for s in near]
        self.leaving = [(s, c) for c in range(cuts) for s in near]
        self.back = []
        pool = [(i, j, (s, i, c)) for i in range(2) for j, (s, c) in enumerate(self.leaving)]
        for bit in reversed(self.bits):
            stage, keep, send = self.split(pool, lambda group: group[0] & bit)
            self.back.append(stage)
            pool = self.pool(keep, send, bit)
        self.last = keep

    def pool(self, keep, send, bit):
        received = [(s ^ bit, d ^ bit, c) for s, d, c in send]
        return [(0, i, g) for i, g in enumerate(keep)] + [(1, i, g) for i, g in enumerate(received)]

    def split(self, pool, goes):
        stage, groups = ([], []), ([], [])
        for which, place, group in pool:
            side = 1 if goes(group) else 0
            stage[side].append((which, len(groups[side]) * CAP, place * CAP))
            groups[side].append(group)
        return stage, groups[0], groups[1]


def ranked(ids, weight, earlier, rows, here, groups):
    length = ids.shape[1]
    row = lax.broadcasted_iota(jnp.int32, (rows, 1), 0)
    expert = jnp.full((rows, 1), -1, jnp.int32)
    level = jnp.zeros((rows, 1), jnp.int32)
    for place, (_, target, _) in enumerate(groups):
        inside = (row >= place * CAP) & (row < (place + 1) * CAP)
        expert = jnp.where(inside, here ^ target, expert)
        level = jnp.where(inside, row - place * CAP, level)
    hits = jnp.zeros((rows, length), F32)
    share = jnp.zeros((rows, length), F32)
    for pick in range(ids.shape[0]):
        named = ids[pick : pick + 1, :] == expert
        hits = hits + jnp.where(named, 1.0, 0.0)
        if weight is not None:
            share = share + jnp.where(named, weight[pick : pick + 1, :], 0.0)
    ranks = dot(hits.astype(BF), earlier)
    chosen = (hits > 0.5) & (jnp.abs(ranks - level.astype(F32)) < 0.5)
    return jnp.where(chosen, 1.0 if weight is None else share, 0.0)


def cut_rows(matrix, groups, cut):
    row = lax.broadcasted_iota(jnp.int32, (matrix.shape[0], 1), 0)
    inside = jnp.zeros(row.shape, jnp.bool_)
    for place, (_, _, c) in enumerate(groups):
        if c == cut:
            inside = inside | ((row >= place * CAP) & (row < (place + 1) * CAP))
    return jnp.where(inside, matrix, 0.0).astype(BF)


def body(queries, key_rows, value_rows, segments, hidden_entry_rows, expert_ids, route_weight, w_gate, w_up, w_down):
    length = queries.shape[1]
    blocks, sides, cores = lax.axis_size("blk"), lax.axis_size("side"), lax.axis_size("tp")
    quarter, ff = w_gate.shape[1], w_gate.shape[2]
    cuts = next((c for c in (1, 2, 4) if blocks // 2 * CAP * c % 8 == 0 and quarter % (c * 128) == 0), 1)
    plan = Plan(blocks, cuts)
    experts, narrow = plan.experts, quarter // cuts
    ids, shares = expert_ids[0].T, route_weight[0].T
    picks = ids.shape[0]

    def columns_of(run, piece, pieces):
        place = ((lax.axis_index("blk") // experts) ^ run) * pieces + piece
        width = quarter // pieces
        return pl.ds(pl.multiple_of(place * width, width), width)

    def own_expert():
        return lax.axis_index("blk") % experts

    def over_side(value, offset, low):
        return swapped(value, ("blk", "side"), low * sides + offset)

    first_rows = up_to(len(plan.first) * CAP, 8)
    wide = hidden_entry_rows.shape[2]

    def before(before_ref):
        i = lax.broadcasted_iota(jnp.int32, (length, length), 0)
        j = lax.broadcasted_iota(jnp.int32, (length, length), 1)
        before_ref[...] = jnp.where(i < j, 1.0, 0.0).astype(BF)

    (earlier,) = call(before, [shaped(length, length)], flops=COST)

    def rank(earlier_ref, ids_ref, out_ref):
        chosen = ranked(ids_ref[...], None, earlier_ref[...], first_rows, own_expert(), plan.first)
        for cut in range(cuts):
            out_ref[cut] = cut_rows(chosen, plan.first, cut)

    (chosen,) = call(rank, [jax.ShapeDtypeStruct((cuts, first_rows, length), BF)], earlier, ids)

    def choose(run):
        def kernel(chosen_ref, x_ref, out_ref):
            total = 0.0
            for cut in range(cuts):
                total = total + dot(chosen_ref[cut], x_ref[:, columns_of(run, cut, cuts)])
            out_ref[...] = total.astype(BF)

        return call(kernel, [shaped(first_rows, narrow)], chosen, hidden_entry_rows[0], flops=COST)[0]

    send, keep = choose(1), choose(0)

    def share_out(earlier_ref, ids_ref, weight_ref, share_ref):
        share = ranked(ids_ref[...], weight_ref[...], earlier_ref[...], first_rows, own_expert(), plan.last)
        for cut in range(cuts):
            share_ref[cut] = cut_rows(share, plan.last, cut).astype(F32).T.astype(BF)

    (share,) = call(share_out, [jax.ShapeDtypeStruct((cuts, length, first_rows), BF)], earlier, ids, shares)

    def pack(after_ref, key_ref, value_ref, segment_ref, held_ref, segment_here, sems):
        copies = [
            pltpu.make_async_copy(key_ref, held_ref.at[0, pl.ds(0, length)], sems.at[0]),
            pltpu.make_async_copy(value_ref, held_ref.at[0, pl.ds(length, length)], sems.at[1]),
            pltpu.make_async_copy(segment_ref, segment_here, sems.at[2]),
        ]
        for copy in copies:
            copy.start()
        copies[2].wait()
        labels = jnp.broadcast_to(segment_here[...].astype(F32), (16, length))
        held_ref[0, 2 * length : 2 * length + 16, :] = labels.astype(BF)
        copies[0].wait()
        copies[1].wait()

    (held,) = call(
        pack,
        [jax.ShapeDtypeStruct((1, 2 * length + 16, HEAD_DIM), BF)],
        send,
        key_rows[0],
        value_rows[0],
        segments,
        scratch=[pltpu.VMEM((1, length), jnp.int32)],
        semaphores=3,
        far_in=(1, 2, 3),
    )

    def sort(stage, *parts):
        sizes = [up_to(len(pieces) * CAP, 8) for pieces in stage]

        def kernel(*refs):
            values = [ref[...].astype(F32) for ref in refs[: len(parts)]]
            for pieces, size, out in zip(stage, sizes, refs[len(parts) :]):
                out[...] = arranged(values, pieces, size).astype(BF)

        return call(
            kernel,
            [shaped(size, narrow) for size in sizes],
            *parts,
            flops=COST,
        )

    for bit, stage in zip(plan.bits, plan.there):
        received, held = lax.optimization_barrier((swapped(send, "blk", bit), held))
        keep, send = sort(stage, keep, received)
    part_rows = len(plan.near) * CAP
    padded = keep.shape[0]
    own = [keep] + [over_side(keep, offset, 0) for offset in range(1, sides)]
    other = [over_side(send, offset, 1) for offset in range(sides)]

    held, _ = lax.optimization_barrier((held, keep))
    nearby = [1 << i for i in reversed(range(blocks.bit_length() - 1))]
    order = [0]
    received_held = swapped(held, "blk", nearby[0])

    def join(after_ref, held_ref, received_ref, both_ref):
        both_ref[: held_ref.shape[0]] = held_ref[...]
        both_ref[held_ref.shape[0] :] = received_ref[...]

    def joined(after, held, received_held, flops):
        both = jax.ShapeDtypeStruct((2 * held.shape[0], *held.shape[1:]), BF)
        return call(join, [both], after, held, received_held, flops=flops)[0]

    side_rows = 2 * part_rows

    half = sides // 2 * side_rows

    def by_source(build):
        here = build(lambda source: plan.near.index(source) * CAP)
        there = build(lambda source: plan.near.index(source ^ experts) * CAP)
        return jnp.where(lax.axis_index("blk") >= experts, there, here)

    def project(*refs):
        own_refs, other_refs, (gate_ref, up_ref, *out_refs) = refs[:sides], refs[sides : 2 * sides], refs[2 * sides :]
        mine = lax.axis_index("tp") == 0
        away, stay = [], []
        for refs_of in (own_refs, other_refs):
            for at in range(sides // 2):
                low, high = refs_of[at][...].astype(F32), refs_of[sides // 2 + at][...].astype(F32)
                away.append(jnp.where(mine, high, low))
                stay.append(jnp.where(mine, low, high))

        def build(row_of, rows, cut):
            pieces = []
            for part in range(2):
                for at in range(sides // 2):
                    for place, (source, c) in enumerate(plan.arrived):
                        if c == cut:
                            to = at * side_rows + part * part_rows + row_of(source)
                            pieces.append((part * (sides // 2) + at, to, place * CAP))
            return arranged(rows, pieces, half)

        both = jnp.concatenate(
            [
                jnp.concatenate([by_source(lambda row_of: build(row_of, rows, cut)) for cut in range(cuts)], axis=1)
                for rows in (away, stay)
            ],
            axis=0,
        ).astype(BF)
        for weight, send_ref, keep_ref in ((gate_ref, *out_refs[:2]), (up_ref, *out_refs[2:])):
            terms = dot(both, weight[...])
            send_ref[...] = terms[:half].astype(BF)
            keep_ref[...] = terms[half:]

    gate_send, gate_keep, up_send, up_keep = call(
        project,
        [shaped(half, ff), shaped(half, ff, F32)] * 2,
        *own,
        *other,
        w_gate[0],
        w_up[0],
    )
    gate_received, up_received = swapped(gate_send, "tp", 1), swapped(up_send, "tp", 1)

    def add_terms(gate_keep_ref, gate_received_ref, up_keep_ref, up_received_ref, sum_ref, send_ref):
        for at, keep_ref, received_ref in ((0, gate_keep_ref, gate_received_ref), (ff, up_keep_ref, up_received_ref)):
            total = keep_ref[...] + received_ref[...].astype(F32)
            sum_ref[:, at : at + ff] = total
            send_ref[:, at : at + ff] = total.astype(BF)

    sums, sums_send = call(
        add_terms,
        [shaped(half, 2 * ff, F32), shaped(half, 2 * ff)],
        gate_keep,
        gate_received,
        up_keep,
        up_received,
    )
    sums_received = swapped(sums_send, "blk", experts)
    for bit in nearby[1:]:
        held = joined(sums_send, held, received_held, COST)
        received_held = swapped(held, "blk", bit)
    held = joined(sums_send, held, received_held, 0)
    for bit in nearby:
        order = order + [place ^ bit for place in order]

    def activate(sum_ref, received_ref, hidden_ref):
        gate = sum_ref[:, :ff] + received_ref[:, :ff].astype(F32)
        up = sum_ref[:, ff:] + received_ref[:, ff:].astype(F32)
        hidden_ref[...] = (gate / (1.0 + jnp.exp(-gate)) * up).astype(BF)

    (hidden,) = call(activate, [shaped(half, ff)], sums, sums_received, exps=half * ff)
    hidden_received = swapped(hidden, "tp", 1)

    def project_back(hidden_ref, received_ref, down_ref, *out_refs):
        mine = lax.axis_index("tp") == 0
        here, there = hidden_ref[...].astype(F32), received_ref[...].astype(F32)
        ordered = [jnp.where(mine, here, there), jnp.where(mine, there, here)]
        spaced = up_to(part_rows, 8)

        def build(row_of):
            pieces = []
            for at in range(sides):
                for part in range(2):
                    for place, source in enumerate(plan.near):
                        to = (2 * at + part) * spaced + place * CAP
                        start = at % (sides // 2) * side_rows + part * part_rows + row_of(source)
                        pieces.append((at // (sides // 2), to, start))
            return arranged(ordered, pieces, 2 * sides * spaced)

        total = by_source(build)
        out = dot(total.astype(BF), down_ref[...])
        for place, out_ref in enumerate(out_refs):
            rows = out[place * spaced : place * spaced + part_rows]
            pieces = [rows[:, cut * narrow : (cut + 1) * narrow] for cut in range(cuts)]
            out_ref[...] = jnp.concatenate(pieces, axis=0).astype(out_ref.dtype)

    outs = call(
        project_back,
        [shaped(padded, narrow, BF if place else F32) for place in range(2 * sides)],
        hidden,
        hidden_received,
        w_down[0],
        flops=4 * half * ff * quarter,
    )
    other = [over_side(outs[2 * offset + 1], offset, 1) for offset in reversed(range(sides))][::-1]
    own = [outs[0]] + [over_side(outs[2 * offset], offset, 0) for offset in range(1, sides)]

    heads = queries.shape[2] // HEAD_DIM
    factor = math.log2(math.e) / math.sqrt(HEAD_DIM)
    span = blocks * length
    batch = math.gcd(heads, 4)

    def attend(query_ref, held_ref, segment_ref, out_ref, keys, values, bias, done, sems):
        here = lax.axis_index("blk")
        i = lax.broadcasted_iota(jnp.int32, (length, length), 0)
        j = lax.broadcasted_iota(jnp.int32, (length, length), 1)
        label_here = jnp.sum(jnp.where(i == j, segment_ref[...].astype(F32), 0.0), axis=1, keepdims=True)
        for place, other_block in enumerate(order):
            at = place * length
            keys[at : at + length, :] = held_ref[place, :length, :]
            values[at : at + length, :HEAD_DIM] = held_ref[place, length : 2 * length, :]
            label = held_ref[place, 2 * length : 2 * length + 16, :].astype(F32)[:1]
            same = label_here == label
            if other_block == 0:
                seen = same & (j <= i)
            else:
                seen = same & ((here ^ other_block) < here)
            bias[:, at : at + length] = jnp.where(seen, 0.0, -1e30)

        values[:, HEAD_DIM:] = jnp.ones((span, HEAD_DIM), BF)

        def one_head(head):
            columns = pl.ds(pl.multiple_of(head * HEAD_DIM, HEAD_DIM), HEAD_DIM)
            scores = lax.dot_general(
                query_ref[:, columns], keys[...], (((1,), (1,)), ((), ())), preferred_element_type=F32
            )
            scores = scores + bias[...]
            weights = jnp.exp2((scores - jnp.max(scores, axis=1, keepdims=True)) * factor)
            out = dot(weights.astype(BF), values[...])
            done[:, columns] = (out[:, :HEAD_DIM] / out[:, HEAD_DIM:]).astype(BF)

        def copied(first):
            columns = pl.ds(first * HEAD_DIM, batch * HEAD_DIM)
            return pltpu.make_async_copy(done.at[:, columns], out_ref.at[:, columns], sems.at[first // batch])

        if span <= 1024:
            for head in range(heads):
                one_head(head)
                if (head + 1) % batch == 0:
                    copied(head + 1 - batch).start()
        else:
            lax.fori_loop(0, heads, lambda head, _: (one_head(head), 0)[1], 0)
            for first in range(0, heads, batch):
                copied(first).start()
        for first in range(0, heads, batch):
            copied(first).wait()

    segments_then, _ = lax.optimization_barrier((segments, outs[1]))
    (attended,) = call(
        attend,
        [shaped(length, heads * HEAD_DIM)],
        queries[0],
        held,
        segments_then,
        scratch=[
            pltpu.VMEM((span, HEAD_DIM), BF),
            pltpu.VMEM((span, 2 * HEAD_DIM), BF),
            pltpu.VMEM((length, span), F32),
            pltpu.VMEM((length, heads * HEAD_DIM), BF),
        ],
        semaphores=heads // batch,
        far_out=(0,),
    )
    own[0], attended = lax.optimization_barrier((own[0], attended))

    def add_parts(*refs):
        sums = []
        for part in (refs[:sides], refs[sides : 2 * sides]):
            total = part[0][...].astype(F32)
            for ref in part[1:]:
                total = total + ref[...].astype(F32)
            sums.append(total)
        for pieces, out in zip(plan.back[0], refs[2 * sides :]):
            out[...] = arranged(sums, pieces, out.shape[0]).astype(BF)

    keep, send = call(
        add_parts,
        [shaped(up_to(len(pieces) * CAP, 8), narrow) for pieces in plan.back[0]],
        *own,
        *other,
        flops=8 * padded * padded * quarter,
    )
    for bit, stage in zip(plan.bits[::-1], plan.back[1:]):
        keep, send = sort(stage, keep, swapped(send, "blk", bit))
    received = swapped(send, "blk", plan.bits[0])

    def mix(run):
        def kernel(share_ref, rows_ref, *refs):
            out_ref, here, sems = refs[-3:]
            copies = []
            for at in range(4):
                cut, within = at * cuts // 4, at % (4 // cuts)
                rows = rows_ref[:, within * (quarter // 4) : (within + 1) * (quarter // 4)]
                here[at] = dot(share_ref[cut], rows).astype(BF)
                target = out_ref.at[:, columns_of(run, at, 4)]
                copies.append(pltpu.make_async_copy(here.at[at], target, sems.at[at]))
                copies[-1].start()
            for copy in copies:
                copy.wait()

        return kernel

    moe_out = None
    for run, rows in ((0, keep), (1, received)):
        ins = [share, rows] + ([] if moe_out is None else [moe_out])
        (moe_out,) = call(
            mix(run),
            [shaped(length, wide)],
            *ins,
            scratch=[pltpu.VMEM((4, length, quarter // 4), BF)],
            semaphores=4,
            far_in=(2,),
            far_out=(0,),
            aliases={2: 0} if run else None,
            flops=4 * length * first_rows * quarter,
        )
    return attended[None], moe_out[None]


def solution(mesh):
    rows = P(("groups", "side"), "blk", "tp")
    placed = (
        rows,
        rows,
        rows,
        P(("groups", "side"), "blk"),
        rows,
        P(("groups", "side"), "blk", None),
        P(("groups", "side"), "blk", None),
        P("blk", "tp", "side"),
        P("blk", "tp", "side"),
        P("blk", "side", "tp"),
    )
    return jax.shard_map(body, mesh=mesh, in_specs=placed, out_specs=(rows, rows), check_vma=False)
```

```python
import math

import jax
import jax.numpy as jnp
from jax import lax
from jax.experimental import pallas as pl
from jax.experimental.pallas import tpu as pltpu
from jax.sharding import PartitionSpec as P

HEAD_DIM = 128
CAP = 10
COST = 3_000_000_000
BF = jnp.bfloat16
F32 = jnp.float32
VMEM = pl.BlockSpec(memory_space=pltpu.VMEM)
HBM = pl.BlockSpec(memory_space=pltpu.HBM)


def swapped(value, axis, bit):
    count = lax.axis_size(axis)
    return lax.ppermute(value, axis, [(i, i ^ bit) for i in range(count)])


def up_to(value, step):
    return -(-value // step) * step


def call(kernel, outs, *ins, scratch=(), semaphores=0, far_in=(), far_out=(), aliases=None, flops=0, exps=0, grant=0):
    moved = sum(math.prod(a.shape) * a.dtype.itemsize for a in (*ins, *outs))
    held = sum(math.prod(s.shape) * s.dtype.itemsize for s in scratch)
    scratch = list(scratch) + ([pltpu.SemaphoreType.DMA((semaphores,))] if semaphores else [])
    return pl.pallas_call(
        kernel,
        out_shape=list(outs),
        in_specs=[HBM if i in far_in else VMEM for i in range(len(ins))],
        out_specs=[HBM if i in far_out else VMEM for i in range(len(outs))],
        scratch_shapes=scratch,
        input_output_aliases=aliases or {},
        compiler_params=pltpu.CompilerParams(vmem_limit_bytes=grant or 2 * moved + held + (2 << 20)),
        cost_estimate=pl.CostEstimate(flops=flops, bytes_accessed=0 if flops == 0 else moved, transcendentals=exps),
    )(*ins)


def shaped(rows, columns, dtype=BF):
    return jax.ShapeDtypeStruct((rows, columns), dtype)


def dot(a, b):
    return jnp.dot(a, b, preferred_element_type=F32)


def arranged(parts, pieces, rows):
    runs = []
    for which, to, start in sorted(pieces, key=lambda piece: piece[1]):
        if runs and runs[-1][0] == which and runs[-1][1] + runs[-1][3] == to and runs[-1][2] + runs[-1][3] == start:
            runs[-1][3] += CAP
        else:
            runs.append([which, to, start, CAP])
    out, at, width = [], 0, parts[0].shape[1]
    for which, to, start, count in runs + [[None, rows, 0, 0]]:
        if to > at:
            out.append(jnp.zeros((to - at, width), F32))
        if count:
            out.append(parts[which][start : start + count])
        at = to + count
    return jnp.concatenate(out, axis=0) if len(out) > 1 else out[0]


class Plan:
    def __init__(self, count, cuts):
        self.experts = count // 2
        self.bits = [1 << i for i in reversed(range(1, count.bit_length() - 1))]
        self.first = keep = [(0, d, c) for c in range(cuts) for d in range(self.experts)]
        send = [(0, d + self.experts, c) for _, d, c in keep]
        self.there = []
        for bit, later in zip(self.bits, self.bits[1:] + [1]):
            stage, keep, send = self.split(self.pool(keep, send, bit), lambda group: group[1] & later)
            self.there.append(stage)
        self.arrived = [(s, c) for s, _, c in keep]
        near = [s for s, c in self.arrived if c == 0]
        self.near, self.sources = near, near + [s ^ 1 for s in near]
        self.leaving = [(s, c) for c in range(cuts) for s in near]
        self.back = []
        pool = [(i, j, (s, i, c)) for i in range(2) for j, (s, c) in enumerate(self.leaving)]
        for bit in reversed(self.bits):
            stage, keep, send = self.split(pool, lambda group: group[0] & bit)
            self.back.append(stage)
            pool = self.pool(keep, send, bit)
        self.last = keep

    def pool(self, keep, send, bit):
        received = [(s ^ bit, d ^ bit, c) for s, d, c in send]
        return [(0, i, g) for i, g in enumerate(keep)] + [(1, i, g) for i, g in enumerate(received)]

    def split(self, pool, goes):
        stage, groups = ([], []), ([], [])
        for which, place, group in pool:
            side = 1 if goes(group) else 0
            stage[side].append((which, len(groups[side]) * CAP, place * CAP))
            groups[side].append(group)
        return stage, groups[0], groups[1]


def ranked(ids, weight, earlier, rows, here, groups):
    length = ids.shape[1]
    row = lax.broadcasted_iota(jnp.int32, (rows, 1), 0)
    expert = jnp.full((rows, 1), -1, jnp.int32)
    level = jnp.zeros((rows, 1), jnp.int32)
    for place, (_, target, _) in enumerate(groups):
        inside = (row >= place * CAP) & (row < (place + 1) * CAP)
        expert = jnp.where(inside, here ^ target, expert)
        level = jnp.where(inside, row - place * CAP, level)
    hits = jnp.zeros((rows, length), F32)
    share = jnp.zeros((rows, length), F32)
    for pick in range(ids.shape[0]):
        named = ids[pick : pick + 1, :] == expert
        hits = hits + jnp.where(named, 1.0, 0.0)
        if weight is not None:
            share = share + jnp.where(named, weight[pick : pick + 1, :], 0.0)
    ranks = dot(hits.astype(BF), earlier)
    chosen = (hits > 0.5) & (jnp.abs(ranks - level.astype(F32)) < 0.5)
    return jnp.where(chosen, 1.0 if weight is None else share, 0.0)


def cut_rows(matrix, groups, cut):
    row = lax.broadcasted_iota(jnp.int32, (matrix.shape[0], 1), 0)
    inside = jnp.zeros(row.shape, jnp.bool_)
    for place, (_, _, c) in enumerate(groups):
        if c == cut:
            inside = inside | ((row >= place * CAP) & (row < (place + 1) * CAP))
    return jnp.where(inside, matrix, 0.0).astype(BF)


def body(queries, key_rows, value_rows, segments, hidden_entry_rows, expert_ids, route_weight, w_gate, w_up, w_down):
    length = queries.shape[1]
    blocks, sides, cores = lax.axis_size("blk"), lax.axis_size("side"), lax.axis_size("tp")
    quarter, ff = w_gate.shape[1], w_gate.shape[2]
    cuts = next((c for c in (1, 2, 4) if blocks // 2 * CAP * c % 8 == 0 and quarter % (c * 128) == 0), 1)
    plan = Plan(blocks, cuts)
    experts, narrow = plan.experts, quarter // cuts
    ids, shares = expert_ids[0].T, route_weight[0].T
    picks = ids.shape[0]

    def columns_of(run, piece, pieces):
        place = ((lax.axis_index("blk") // experts) ^ run) * pieces + piece
        width = quarter // pieces
        return pl.ds(pl.multiple_of(place * width, width), width)

    def own_expert():
        return lax.axis_index("blk") % experts

    def over_side(value, offset, low):
        return swapped(value, ("blk", "side"), low * sides + offset)

    first_rows = up_to(len(plan.first) * CAP, 8)
    wide = hidden_entry_rows.shape[2]

    def before(before_ref):
        i = lax.broadcasted_iota(jnp.int32, (length, length), 0)
        j = lax.broadcasted_iota(jnp.int32, (length, length), 1)
        before_ref[...] = jnp.where(i < j, 1.0, 0.0).astype(BF)

    (earlier,) = call(before, [shaped(length, length)], flops=COST)

    whole_groups = plan.first[:experts]
    whole_rows = up_to(experts * CAP, 8)

    def rank(earlier_ref, ids_ref, out_ref):
        chosen = ranked(ids_ref[...], None, earlier_ref[...], whole_rows, own_expert(), whole_groups)
        out_ref[...] = chosen.astype(BF)

    (chosen,) = call(rank, [shaped(whole_rows, length)], earlier, ids)

    def choose(run):
        def kernel(chosen_ref, x_ref, out_ref):
            rows = dot(chosen_ref[...], x_ref[:, columns_of(run, 0, 1)])[: experts * CAP]
            pieces = [rows[:, cut * narrow : (cut + 1) * narrow] for cut in range(cuts)]
            if first_rows > cuts * experts * CAP:
                pieces.append(jnp.zeros((first_rows - cuts * experts * CAP, narrow), F32))
            out_ref[...] = jnp.concatenate(pieces, axis=0).astype(BF)

        return call(kernel, [shaped(first_rows, narrow)], chosen, hidden_entry_rows[0], flops=COST)[0]

    send, keep = choose(1), choose(0)

    def share_out(earlier_ref, ids_ref, weight_ref, share_ref):
        share = ranked(ids_ref[...], weight_ref[...], earlier_ref[...], first_rows, own_expert(), plan.last)
        for cut in range(cuts):
            share_ref[cut] = cut_rows(share, plan.last, cut).astype(F32).T.astype(BF)

    (share,) = call(share_out, [jax.ShapeDtypeStruct((cuts, length, first_rows), BF)], earlier, ids, shares)

    def pack(after_ref, key_ref, value_ref, segment_ref, held_ref, segment_here, sems):
        copies = [
            pltpu.make_async_copy(key_ref, held_ref.at[0, pl.ds(0, length)], sems.at[0]),
            pltpu.make_async_copy(value_ref, held_ref.at[0, pl.ds(length, length)], sems.at[1]),
            pltpu.make_async_copy(segment_ref, segment_here, sems.at[2]),
        ]
        for copy in copies:
            copy.start()
        copies[2].wait()
        labels = jnp.broadcast_to(segment_here[...].astype(F32), (16, length))
        held_ref[0, 2 * length : 2 * length + 16, :] = labels.astype(BF)
        copies[0].wait()
        copies[1].wait()

    (held,) = call(
        pack,
        [jax.ShapeDtypeStruct((1, 2 * length + 16, HEAD_DIM), BF)],
        send,
        key_rows[0],
        value_rows[0],
        segments,
        scratch=[pltpu.VMEM((1, length), jnp.int32)],
        semaphores=3,
        far_in=(1, 2, 3),
    )

    def sort(stage, *parts):
        sizes = [up_to(len(pieces) * CAP, 8) for pieces in stage]

        def kernel(*refs):
            values = [ref[...].astype(F32) for ref in refs[: len(parts)]]
            for pieces, size, out in zip(stage, sizes, refs[len(parts) :]):
                out[...] = arranged(values, pieces, size).astype(BF)

        return call(
            kernel,
            [shaped(size, narrow) for size in sizes],
            *parts,
            flops=COST,
        )

    for bit, stage in zip(plan.bits, plan.there):
        received, held = lax.optimization_barrier((swapped(send, "blk", bit), held))
        keep, send = sort(stage, keep, received)
    part_rows = len(plan.near) * CAP
    padded = keep.shape[0]
    own = [keep] + [over_side(keep, offset, 0) for offset in range(1, sides)]
    other = [over_side(send, offset, 1) for offset in range(sides)]

    held, _ = lax.optimization_barrier((held, keep))
    nearby = [1 << i for i in reversed(range(blocks.bit_length() - 1))]
    order = [0]
    received_held = swapped(held, "blk", nearby[0])

    def join(after_ref, held_ref, received_ref, both_ref):
        both_ref[: held_ref.shape[0]] = held_ref[...]
        both_ref[held_ref.shape[0] :] = received_ref[...]

    def joined(after, held, received_held, flops):
        both = jax.ShapeDtypeStruct((2 * held.shape[0], *held.shape[1:]), BF)
        return call(join, [both], after, held, received_held, flops=flops)[0]

    side_rows = 2 * part_rows

    half = sides // 2 * side_rows

    def by_source(build):
        here = build(lambda source: plan.near.index(source) * CAP)
        there = build(lambda source: plan.near.index(source ^ experts) * CAP)
        return jnp.where(lax.axis_index("blk") >= experts, there, here)

    def project(*refs):
        own_refs, other_refs, (gate_ref, up_ref, *out_refs) = refs[:sides], refs[sides : 2 * sides], refs[2 * sides :]
        mine = lax.axis_index("tp") == 0
        away, stay = [], []
        for refs_of in (own_refs, other_refs):
            for at in range(sides // 2):
                low, high = refs_of[at][...].astype(F32), refs_of[sides // 2 + at][...].astype(F32)
                away.append(jnp.where(mine, high, low))
                stay.append(jnp.where(mine, low, high))

        def build(row_of, rows, cut):
            pieces = []
            for part in range(2):
                for at in range(sides // 2):
                    for place, (source, c) in enumerate(plan.arrived):
                        if c == cut:
                            to = at * side_rows + part * part_rows + row_of(source)
                            pieces.append((part * (sides // 2) + at, to, place * CAP))
            return arranged(rows, pieces, half)

        both = jnp.concatenate(
            [
                jnp.concatenate([by_source(lambda row_of: build(row_of, rows, cut)) for cut in range(cuts)], axis=1)
                for rows in (away, stay)
            ],
            axis=0,
        ).astype(BF)
        for weight, send_ref, keep_ref in ((gate_ref, *out_refs[:2]), (up_ref, *out_refs[2:])):
            terms = dot(both, weight[...])
            send_ref[...] = terms[:half].astype(BF)
            keep_ref[...] = terms[half:]

    gate_send, gate_keep, up_send, up_keep = call(
        project,
        [shaped(half, ff), shaped(half, ff, F32)] * 2,
        *own,
        *other,
        w_gate[0],
        w_up[0],
    )
    gate_received, up_received = swapped(gate_send, "tp", 1), swapped(up_send, "tp", 1)

    def add_terms(gate_keep_ref, gate_received_ref, up_keep_ref, up_received_ref, sum_ref, send_ref):
        for at, keep_ref, received_ref in ((0, gate_keep_ref, gate_received_ref), (ff, up_keep_ref, up_received_ref)):
            total = keep_ref[...] + received_ref[...].astype(F32)
            sum_ref[:, at : at + ff] = total
            send_ref[:, at : at + ff] = total.astype(BF)

    sums, sums_send = call(
        add_terms,
        [shaped(half, 2 * ff, F32), shaped(half, 2 * ff)],
        gate_keep,
        gate_received,
        up_keep,
        up_received,
    )
    sums_received = swapped(sums_send, "blk", experts)
    for bit in nearby[1:]:
        held = joined(sums_send, held, received_held, COST)
        received_held = swapped(held, "blk", bit)
    held = joined(sums_send, held, received_held, 0)
    for bit in nearby:
        order = order + [place ^ bit for place in order]

    def activate(sum_ref, received_ref, hidden_ref):
        gate = sum_ref[:, :ff] + received_ref[:, :ff].astype(F32)
        up = sum_ref[:, ff:] + received_ref[:, ff:].astype(F32)
        hidden_ref[...] = (gate / (1.0 + jnp.exp(-gate)) * up).astype(BF)

    (hidden,) = call(activate, [shaped(half, ff)], sums, sums_received, exps=half * ff)
    hidden_received = swapped(hidden, "tp", 1)

    def project_back(hidden_ref, received_ref, down_ref, *out_refs):
        mine = lax.axis_index("tp") == 0
        here, there = hidden_ref[...].astype(F32), received_ref[...].astype(F32)
        ordered = [jnp.where(mine, here, there), jnp.where(mine, there, here)]
        spaced = up_to(part_rows, 8)

        def build(row_of):
            pieces = []
            for at in range(sides):
                for part in range(2):
                    for place, source in enumerate(plan.near):
                        to = (2 * at + part) * spaced + place * CAP
                        start = at % (sides // 2) * side_rows + part * part_rows + row_of(source)
                        pieces.append((at // (sides // 2), to, start))
            return arranged(ordered, pieces, 2 * sides * spaced)

        total = by_source(build)
        out = dot(total.astype(BF), down_ref[...])
        for place, out_ref in enumerate(out_refs):
            rows = out[place * spaced : place * spaced + part_rows]
            pieces = [rows[:, cut * narrow : (cut + 1) * narrow] for cut in range(cuts)]
            out_ref[...] = jnp.concatenate(pieces, axis=0).astype(out_ref.dtype)

    outs = call(
        project_back,
        [shaped(padded, narrow, BF if place else F32) for place in range(2 * sides)],
        hidden,
        hidden_received,
        w_down[0],
        flops=4 * half * ff * quarter,
    )
    other = [over_side(outs[2 * offset + 1], offset, 1) for offset in reversed(range(sides))][::-1]
    own = [outs[0]] + [over_side(outs[2 * offset], offset, 0) for offset in range(1, sides)]

    heads = queries.shape[2] // HEAD_DIM
    factor = math.log2(math.e) / math.sqrt(HEAD_DIM)
    span = blocks * length
    batch = math.gcd(heads, 4)

    def attend(query_ref, held_ref, segment_ref, out_ref, keys, values, bias, done, sems):
        here = lax.axis_index("blk")
        i = lax.broadcasted_iota(jnp.int32, (length, length), 0)
        j = lax.broadcasted_iota(jnp.int32, (length, length), 1)
        label_here = jnp.sum(jnp.where(i == j, segment_ref[...].astype(F32), 0.0), axis=1, keepdims=True)
        for place, other_block in enumerate(order):
            at = place * length
            keys[at : at + length, :] = held_ref[place, :length, :]
            values[at : at + length, :HEAD_DIM] = held_ref[place, length : 2 * length, :]
            label = held_ref[place, 2 * length : 2 * length + 16, :].astype(F32)[:1]
            same = label_here == label
            if other_block == 0:
                seen = same & (j <= i)
            else:
                seen = same & ((here ^ other_block) < here)
            bias[:, at : at + length] = jnp.where(seen, 0.0, -1e30)

        values[:, HEAD_DIM:] = jnp.ones((span, HEAD_DIM), BF)

        def one_head(head):
            columns = pl.ds(pl.multiple_of(head * HEAD_DIM, HEAD_DIM), HEAD_DIM)
            scores = lax.dot_general(
                query_ref[:, columns], keys[...], (((1,), (1,)), ((), ())), preferred_element_type=F32
            )
            scores = scores + bias[...]
            weights = jnp.exp2((scores - jnp.max(scores, axis=1, keepdims=True)) * factor)
            out = dot(weights.astype(BF), values[...])
            done[:, columns] = (out[:, :HEAD_DIM] / out[:, HEAD_DIM:]).astype(BF)

        def copied(first):
            columns = pl.ds(first * HEAD_DIM, batch * HEAD_DIM)
            return pltpu.make_async_copy(done.at[:, columns], out_ref.at[:, columns], sems.at[first // batch])

        if span <= 1024:
            for head in range(heads):
                one_head(head)
                if (head + 1) % batch == 0:
                    copied(head + 1 - batch).start()
        else:
            lax.fori_loop(0, heads, lambda head, _: (one_head(head), 0)[1], 0)
            for first in range(0, heads, batch):
                copied(first).start()
        for first in range(0, heads, batch):
            copied(first).wait()

    segments_then, _ = lax.optimization_barrier((segments, outs[1]))
    (attended,) = call(
        attend,
        [shaped(length, heads * HEAD_DIM)],
        queries[0],
        held,
        segments_then,
        scratch=[
            pltpu.VMEM((span, HEAD_DIM), BF),
            pltpu.VMEM((span, 2 * HEAD_DIM), BF),
            pltpu.VMEM((length, span), F32),
            pltpu.VMEM((length, heads * HEAD_DIM), BF),
        ],
        semaphores=heads // batch,
        far_out=(0,),
    )
    own[0], attended = lax.optimization_barrier((own[0], attended))

    def add_parts(*refs):
        sums = []
        for part in (refs[:sides], refs[sides : 2 * sides]):
            total = part[0][...].astype(F32)
            for ref in part[1:]:
                total = total + ref[...].astype(F32)
            sums.append(total)
        for pieces, out in zip(plan.back[0], refs[2 * sides :]):
            out[...] = arranged(sums, pieces, out.shape[0]).astype(BF)

    keep, send = call(
        add_parts,
        [shaped(up_to(len(pieces) * CAP, 8), narrow) for pieces in plan.back[0]],
        *own,
        *other,
        flops=8 * padded * padded * quarter,
    )
    for bit, stage in zip(plan.bits[::-1], plan.back[1:]):
        keep, send = sort(stage, keep, swapped(send, "blk", bit))
    received = swapped(send, "blk", plan.bits[0])

    def mix(run):
        def kernel(share_ref, rows_ref, *refs):
            out_ref, here, sems = refs[-3:]
            copies = []
            for at in range(4):
                cut, within = at * cuts // 4, at % (4 // cuts)
                rows = rows_ref[:, within * (quarter // 4) : (within + 1) * (quarter // 4)]
                here[at] = dot(share_ref[cut], rows).astype(BF)
                target = out_ref.at[:, columns_of(run, at, 4)]
                copies.append(pltpu.make_async_copy(here.at[at], target, sems.at[at]))
                copies[-1].start()
            for copy in copies:
                copy.wait()

        return kernel

    moe_out = None
    for run, rows in ((0, keep), (1, received)):
        ins = [share, rows] + ([] if moe_out is None else [moe_out])
        (moe_out,) = call(
            mix(run),
            [shaped(length, wide)],
            *ins,
            scratch=[pltpu.VMEM((4, length, quarter // 4), BF)],
            semaphores=4,
            far_in=(2,),
            far_out=(0,),
            aliases={2: 0} if run else None,
            flops=4 * length * first_rows * quarter,
        )
    return attended[None], moe_out[None]


def solution(mesh):
    rows = P(("groups", "side"), "blk", "tp")
    placed = (
        rows,
        rows,
        rows,
        P(("groups", "side"), "blk"),
        rows,
        P(("groups", "side"), "blk", None),
        P(("groups", "side"), "blk", None),
        P("blk", "tp", "side"),
        P("blk", "tp", "side"),
        P("blk", "side", "tp"),
    )
    return jax.shard_map(body, mesh=mesh, in_specs=placed, out_specs=(rows, rows), check_vma=False)
```

```python
import math

import jax
import jax.numpy as jnp
from jax import lax
from jax.experimental import pallas as pl
from jax.experimental.pallas import tpu as pltpu
from jax.sharding import PartitionSpec as P

HEAD_DIM = 128
CAP = 10
COST = 3_000_000_000
BF = jnp.bfloat16
F32 = jnp.float32
VMEM = pl.BlockSpec(memory_space=pltpu.VMEM)
HBM = pl.BlockSpec(memory_space=pltpu.HBM)


def swapped(value, axis, bit):
    count = lax.axis_size(axis)
    return lax.ppermute(value, axis, [(i, i ^ bit) for i in range(count)])


def up_to(value, step):
    return -(-value // step) * step


def call(kernel, outs, *ins, scratch=(), semaphores=0, far_in=(), far_out=(), aliases=None, flops=0, exps=0, grant=0):
    moved = sum(math.prod(a.shape) * a.dtype.itemsize for a in (*ins, *outs))
    held = sum(math.prod(s.shape) * s.dtype.itemsize for s in scratch)
    scratch = list(scratch) + ([pltpu.SemaphoreType.DMA((semaphores,))] if semaphores else [])
    return pl.pallas_call(
        kernel,
        out_shape=list(outs),
        in_specs=[HBM if i in far_in else VMEM for i in range(len(ins))],
        out_specs=[HBM if i in far_out else VMEM for i in range(len(outs))],
        scratch_shapes=scratch,
        input_output_aliases=aliases or {},
        compiler_params=pltpu.CompilerParams(vmem_limit_bytes=grant or 2 * moved + held + (2 << 20)),
        cost_estimate=pl.CostEstimate(flops=flops, bytes_accessed=0 if flops == 0 else moved, transcendentals=exps),
    )(*ins)


def shaped(rows, columns, dtype=BF):
    return jax.ShapeDtypeStruct((rows, columns), dtype)


def dot(a, b):
    return jnp.dot(a, b, preferred_element_type=F32)


def arranged(parts, pieces, rows):
    runs = []
    for which, to, start in sorted(pieces, key=lambda piece: piece[1]):
        if runs and runs[-1][0] == which and runs[-1][1] + runs[-1][3] == to and runs[-1][2] + runs[-1][3] == start:
            runs[-1][3] += CAP
        else:
            runs.append([which, to, start, CAP])
    out, at, width = [], 0, parts[0].shape[1]
    for which, to, start, count in runs + [[None, rows, 0, 0]]:
        if to > at:
            out.append(jnp.zeros((to - at, width), F32))
        if count:
            out.append(parts[which][start : start + count])
        at = to + count
    return jnp.concatenate(out, axis=0) if len(out) > 1 else out[0]


class Plan:
    def __init__(self, count, cuts):
        self.experts = count // 2
        self.bits = [1 << i for i in reversed(range(1, count.bit_length() - 1))]
        self.first = keep = [(0, d, c) for c in range(cuts) for d in range(self.experts)]
        send = [(0, d + self.experts, c) for _, d, c in keep]
        self.there = []
        for bit, later in zip(self.bits, self.bits[1:] + [1]):
            stage, keep, send = self.split(self.pool(keep, send, bit), lambda group: group[1] & later)
            self.there.append(stage)
        self.arrived = [(s, c) for s, _, c in keep]
        near = [s for s, c in self.arrived if c == 0]
        self.near, self.sources = near, near + [s ^ 1 for s in near]
        self.leaving = [(s, c) for c in range(cuts) for s in near]
        self.back = []
        pool = [(i, j, (s, i, c)) for i in range(2) for j, (s, c) in enumerate(self.leaving)]
        for bit in reversed(self.bits):
            stage, keep, send = self.split(pool, lambda group: group[0] & bit)
            self.back.append(stage)
            pool = self.pool(keep, send, bit)
        self.last = keep

    def pool(self, keep, send, bit):
        received = [(s ^ bit, d ^ bit, c) for s, d, c in send]
        return [(0, i, g) for i, g in enumerate(keep)] + [(1, i, g) for i, g in enumerate(received)]

    def split(self, pool, goes):
        stage, groups = ([], []), ([], [])
        for which, place, group in pool:
            side = 1 if goes(group) else 0
            stage[side].append((which, len(groups[side]) * CAP, place * CAP))
            groups[side].append(group)
        return stage, groups[0], groups[1]


def ranked(ids, weight, earlier, rows, here, groups):
    length = ids.shape[1]
    row = lax.broadcasted_iota(jnp.int32, (rows, 1), 0)
    expert = jnp.full((rows, 1), -1, jnp.int32)
    level = jnp.zeros((rows, 1), jnp.int32)
    for place, (_, target, _) in enumerate(groups):
        inside = (row >= place * CAP) & (row < (place + 1) * CAP)
        expert = jnp.where(inside, here ^ target, expert)
        level = jnp.where(inside, row - place * CAP, level)
    hits = jnp.zeros((rows, length), F32)
    share = jnp.zeros((rows, length), F32)
    for pick in range(ids.shape[0]):
        named = ids[pick : pick + 1, :] == expert
        hits = hits + jnp.where(named, 1.0, 0.0)
        if weight is not None:
            share = share + jnp.where(named, weight[pick : pick + 1, :], 0.0)
    ranks = dot(hits.astype(BF), earlier)
    chosen = (hits > 0.5) & (jnp.abs(ranks - level.astype(F32)) < 0.5)
    return jnp.where(chosen, 1.0 if weight is None else share, 0.0)


def cut_rows(matrix, groups, cut):
    row = lax.broadcasted_iota(jnp.int32, (matrix.shape[0], 1), 0)
    inside = jnp.zeros(row.shape, jnp.bool_)
    for place, (_, _, c) in enumerate(groups):
        if c == cut:
            inside = inside | ((row >= place * CAP) & (row < (place + 1) * CAP))
    return jnp.where(inside, matrix, 0.0).astype(BF)


def body(queries, key_rows, value_rows, segments, hidden_entry_rows, expert_ids, route_weight, w_gate, w_up, w_down):
    length = queries.shape[1]
    blocks, sides, cores = lax.axis_size("blk"), lax.axis_size("side"), lax.axis_size("tp")
    quarter, ff = w_gate.shape[1], w_gate.shape[2]
    cuts = next((c for c in (1, 2, 4) if blocks // 2 * CAP * c % 8 == 0 and quarter % (c * 128) == 0), 1)
    plan = Plan(blocks, cuts)
    experts, narrow = plan.experts, quarter // cuts
    ids, shares = expert_ids[0].T, route_weight[0].T
    picks = ids.shape[0]

    def columns_of(run, piece, pieces):
        place = ((lax.axis_index("blk") // experts) ^ run) * pieces + piece
        width = quarter // pieces
        return pl.ds(pl.multiple_of(place * width, width), width)

    def own_expert():
        return lax.axis_index("blk") % experts

    def over_side(value, offset, low):
        return swapped(value, ("blk", "side"), low * sides + offset)

    first_rows = up_to(len(plan.first) * CAP, 8)
    wide = hidden_entry_rows.shape[2]

    def before(before_ref):
        i = lax.broadcasted_iota(jnp.int32, (length, length), 0)
        j = lax.broadcasted_iota(jnp.int32, (length, length), 1)
        before_ref[...] = jnp.where(i < j, 1.0, 0.0).astype(BF)

    (earlier,) = call(before, [shaped(length, length)], flops=COST)

    whole_groups = plan.first[:experts]
    whole_rows = up_to(experts * CAP, 8)

    def rank(earlier_ref, ids_ref, out_ref):
        chosen = ranked(ids_ref[...], None, earlier_ref[...], whole_rows, own_expert(), whole_groups)
        out_ref[...] = chosen.astype(BF)

    (chosen,) = call(rank, [shaped(whole_rows, length)], earlier, ids)

    def choose(run):
        def kernel(chosen_ref, x_ref, out_ref):
            rows = dot(chosen_ref[...], x_ref[:, columns_of(run, 0, 1)])[: experts * CAP]
            pieces = [rows[:, cut * narrow : (cut + 1) * narrow] for cut in range(cuts)]
            if first_rows > cuts * experts * CAP:
                pieces.append(jnp.zeros((first_rows - cuts * experts * CAP, narrow), F32))
            out_ref[...] = jnp.concatenate(pieces, axis=0).astype(BF)

        return call(kernel, [shaped(first_rows, narrow)], chosen, hidden_entry_rows[0], flops=COST)[0]

    send, keep = choose(1), choose(0)

    def share_out(earlier_ref, ids_ref, weight_ref, share_ref):
        share = ranked(ids_ref[...], weight_ref[...], earlier_ref[...], first_rows, own_expert(), plan.last)
        for cut in range(cuts):
            share_ref[cut] = cut_rows(share, plan.last, cut).astype(F32).T.astype(BF)

    (share,) = call(share_out, [jax.ShapeDtypeStruct((cuts, length, first_rows), BF)], earlier, ids, shares)

    def pack(after_ref, key_ref, value_ref, segment_ref, held_ref, segment_here, sems):
        copies = [
            pltpu.make_async_copy(key_ref, held_ref.at[0, pl.ds(0, length)], sems.at[0]),
            pltpu.make_async_copy(value_ref, held_ref.at[0, pl.ds(length, length)], sems.at[1]),
            pltpu.make_async_copy(segment_ref, segment_here, sems.at[2]),
        ]
        for copy in copies:
            copy.start()
        copies[2].wait()
        labels = jnp.broadcast_to(segment_here[...].astype(F32), (16, length))
        held_ref[0, 2 * length : 2 * length + 16, :] = labels.astype(BF)
        copies[0].wait()
        copies[1].wait()

    (held,) = call(
        pack,
        [jax.ShapeDtypeStruct((1, 2 * length + 16, HEAD_DIM), BF)],
        send,
        key_rows[0],
        value_rows[0],
        segments,
        scratch=[pltpu.VMEM((1, length), jnp.int32)],
        semaphores=3,
        far_in=(1, 2, 3),
    )

    def sort(stage, *parts):
        sizes = [up_to(len(pieces) * CAP, 8) for pieces in stage]

        def kernel(*refs):
            values = [ref[...].astype(F32) for ref in refs[: len(parts)]]
            for pieces, size, out in zip(stage, sizes, refs[len(parts) :]):
                out[...] = arranged(values, pieces, size).astype(BF)

        return call(
            kernel,
            [shaped(size, narrow) for size in sizes],
            *parts,
            flops=COST,
        )

    for bit, stage in zip(plan.bits, plan.there):
        received, held = lax.optimization_barrier((swapped(send, "blk", bit), held))
        keep, send = sort(stage, keep, received)
    part_rows = len(plan.near) * CAP
    padded = keep.shape[0]
    own = [keep] + [over_side(keep, offset, 0) for offset in range(1, sides)]
    other = [over_side(send, offset, 1) for offset in range(sides)]

    held, _ = lax.optimization_barrier((held, keep))
    nearby = [1 << i for i in reversed(range(blocks.bit_length() - 1))]
    order = [0]
    received_held = swapped(held, "blk", nearby[0])

    def join(after_ref, held_ref, received_ref, both_ref):
        both_ref[: held_ref.shape[0]] = held_ref[...]
        both_ref[held_ref.shape[0] :] = received_ref[...]

    def joined(after, held, received_held, flops):
        both = jax.ShapeDtypeStruct((2 * held.shape[0], *held.shape[1:]), BF)
        return call(join, [both], after, held, received_held, flops=flops)[0]

    side_rows = 2 * part_rows

    half = sides // 2 * side_rows

    def by_source(build):
        here = build(lambda source: plan.near.index(source) * CAP)
        there = build(lambda source: plan.near.index(source ^ experts) * CAP)
        return jnp.where(lax.axis_index("blk") >= experts, there, here)

    def project(*refs):
        own_refs, other_refs, (gate_ref, up_ref, *out_refs) = refs[:sides], refs[sides : 2 * sides], refs[2 * sides :]
        mine = lax.axis_index("tp") == 0
        away, stay = [], []
        for refs_of in (own_refs, other_refs):
            for at in range(sides // 2):
                low, high = refs_of[at][...].astype(F32), refs_of[sides // 2 + at][...].astype(F32)
                away.append(jnp.where(mine, high, low))
                stay.append(jnp.where(mine, low, high))

        def build(row_of, rows, cut):
            pieces = []
            for part in range(2):
                for at in range(sides // 2):
                    for place, (source, c) in enumerate(plan.arrived):
                        if c == cut:
                            to = at * side_rows + part * part_rows + row_of(source)
                            pieces.append((part * (sides // 2) + at, to, place * CAP))
            return arranged(rows, pieces, half)

        both = jnp.concatenate(
            [
                jnp.concatenate([by_source(lambda row_of: build(row_of, rows, cut)) for cut in range(cuts)], axis=1)
                for rows in (away, stay)
            ],
            axis=0,
        ).astype(BF)
        for weight, send_ref, keep_ref in ((gate_ref, *out_refs[:2]), (up_ref, *out_refs[2:])):
            terms = dot(both, weight[...])
            send_ref[...] = terms[:half].astype(BF)
            keep_ref[...] = terms[half:]

    gate_send, gate_keep, up_send, up_keep = call(
        project,
        [shaped(half, ff), shaped(half, ff, F32)] * 2,
        *own,
        *other,
        w_gate[0],
        w_up[0],
    )
    gate_received, up_received = swapped(gate_send, "tp", 1), swapped(up_send, "tp", 1)

    def add_terms(gate_keep_ref, gate_received_ref, up_keep_ref, up_received_ref, sum_ref, send_ref):
        for at, keep_ref, received_ref in ((0, gate_keep_ref, gate_received_ref), (ff, up_keep_ref, up_received_ref)):
            total = keep_ref[...] + received_ref[...].astype(F32)
            sum_ref[:, at : at + ff] = total
            send_ref[:, at : at + ff] = total.astype(BF)

    sums, sums_send = call(
        add_terms,
        [shaped(half, 2 * ff, F32), shaped(half, 2 * ff)],
        gate_keep,
        gate_received,
        up_keep,
        up_received,
    )
    sums_received = swapped(sums_send, "blk", experts)
    for bit in nearby[1:]:
        held = joined(sums_send, held, received_held, COST)
        received_held = swapped(held, "blk", bit)
    held = joined(sums_send, held, received_held, 0)
    for bit in nearby:
        order = order + [place ^ bit for place in order]

    def activate(sum_ref, received_ref, hidden_ref):
        gate = sum_ref[:, :ff] + received_ref[:, :ff].astype(F32)
        up = sum_ref[:, ff:] + received_ref[:, ff:].astype(F32)
        hidden_ref[...] = (gate / (1.0 + jnp.exp(-gate)) * up).astype(BF)

    (hidden,) = call(activate, [shaped(half, ff)], sums, sums_received, exps=half * ff)
    hidden_received = swapped(hidden, "tp", 1)

    def project_back(hidden_ref, received_ref, down_ref, *out_refs):
        mine = lax.axis_index("tp") == 0
        here, there = hidden_ref[...].astype(F32), received_ref[...].astype(F32)
        ordered = [jnp.where(mine, here, there), jnp.where(mine, there, here)]
        spaced = up_to(part_rows, 8)

        def build(row_of):
            pieces = []
            for at in range(sides):
                for part in range(2):
                    for place, source in enumerate(plan.near):
                        to = (2 * at + part) * spaced + place * CAP
                        start = at % (sides // 2) * side_rows + part * part_rows + row_of(source)
                        pieces.append((at // (sides // 2), to, start))
            return arranged(ordered, pieces, 2 * sides * spaced)

        total = by_source(build)
        out = dot(total.astype(BF), down_ref[...])
        for place, out_ref in enumerate(out_refs):
            rows = out[place * spaced : place * spaced + part_rows]
            pieces = [rows[:, cut * narrow : (cut + 1) * narrow] for cut in range(cuts)]
            out_ref[...] = jnp.concatenate(pieces, axis=0).astype(out_ref.dtype)

    outs = call(
        project_back,
        [shaped(padded, narrow, BF if place else F32) for place in range(2 * sides)],
        hidden,
        hidden_received,
        w_down[0],
        flops=4 * half * ff * quarter,
    )
    other = [over_side(outs[2 * offset + 1], offset, 1) for offset in reversed(range(sides))][::-1]
    own = [outs[0]] + [over_side(outs[2 * offset], offset, 0) for offset in range(1, sides)]

    heads = queries.shape[2] // HEAD_DIM
    factor = math.log2(math.e) / math.sqrt(HEAD_DIM)
    span = blocks * length
    batch = math.gcd(heads, 4)

    def attend(query_ref, held_ref, segment_ref, out_ref, keys, values, bias, done, sems):
        here = lax.axis_index("blk")
        i = lax.broadcasted_iota(jnp.int32, (length, length), 0)
        j = lax.broadcasted_iota(jnp.int32, (length, length), 1)
        label_here = jnp.sum(jnp.where(i == j, segment_ref[...].astype(F32), 0.0), axis=1, keepdims=True)
        for place, other_block in enumerate(order):
            at = place * length
            keys[at : at + length, :] = held_ref[place, :length, :]
            values[at : at + length, :HEAD_DIM] = held_ref[place, length : 2 * length, :]
            label = held_ref[place, 2 * length : 2 * length + 16, :].astype(F32)[:1]
            same = label_here == label
            if other_block == 0:
                seen = same & (j <= i)
            else:
                seen = same & ((here ^ other_block) < here)
            bias[:, at : at + length] = jnp.where(seen, 0.0, -1e30)

        values[:, HEAD_DIM:] = jnp.ones((span, HEAD_DIM), BF)

        def one_head(head):
            columns = pl.ds(pl.multiple_of(head * HEAD_DIM, HEAD_DIM), HEAD_DIM)
            scores = lax.dot_general(
                query_ref[:, columns], keys[...], (((1,), (1,)), ((), ())), preferred_element_type=F32
            )
            scores = scores + bias[...]
            weights = jnp.exp2((scores - jnp.max(scores, axis=1, keepdims=True)) * factor)
            out = dot(weights.astype(BF), values[...])
            done[:, columns] = (out[:, :HEAD_DIM] / out[:, HEAD_DIM:]).astype(BF)

        def copied(first):
            columns = pl.ds(first * HEAD_DIM, batch * HEAD_DIM)
            return pltpu.make_async_copy(done.at[:, columns], out_ref.at[:, columns], sems.at[first // batch])

        if span <= 1024:
            for head in range(heads):
                one_head(head)
                if (head + 1) % batch == 0:
                    copied(head + 1 - batch).start()
        else:
            lax.fori_loop(0, heads, lambda head, _: (one_head(head), 0)[1], 0)
            for first in range(0, heads, batch):
                copied(first).start()
        for first in range(0, heads, batch):
            copied(first).wait()

    segments_then, _ = lax.optimization_barrier((segments, outs[1]))
    (attended,) = call(
        attend,
        [shaped(length, heads * HEAD_DIM)],
        queries[0],
        held,
        segments_then,
        scratch=[
            pltpu.VMEM((span, HEAD_DIM), BF),
            pltpu.VMEM((span, 2 * HEAD_DIM), BF),
            pltpu.VMEM((length, span), F32),
            pltpu.VMEM((length, heads * HEAD_DIM), BF),
        ],
        semaphores=heads // batch,
        far_out=(0,),
    )
    own[0], attended = lax.optimization_barrier((own[0], attended))

    def add_parts(*refs):
        sums = []
        for part in (refs[:sides], refs[sides : 2 * sides]):
            total = part[0][...].astype(F32)
            for ref in part[1:]:
                total = total + ref[...].astype(F32)
            sums.append(total)
        for pieces, out in zip(plan.back[0], refs[2 * sides :]):
            out[...] = arranged(sums, pieces, out.shape[0]).astype(BF)

    keep, send = call(
        add_parts,
        [shaped(up_to(len(pieces) * CAP, 8), narrow) for pieces in plan.back[0]],
        *own,
        *other,
        flops=8 * padded * padded * quarter,
    )
    for bit, stage in zip(plan.bits[::-1], plan.back[1:]):
        keep, send = sort(stage, keep, swapped(send, "blk", bit))
    received = swapped(send, "blk", plan.bits[0])

    def mix(run):
        def kernel(share_ref, rows_ref, *refs):
            out_ref, here, sems = refs[-3:]
            copies = []
            block = length // 4
            for at in range(4):
                lines = pl.ds(at * block, block)
                for cut in range(cuts):
                    here[lines, cut * narrow : (cut + 1) * narrow] = dot(share_ref[cut, lines], rows_ref[...]).astype(BF)
                target = out_ref.at[lines, columns_of(run, 0, 1)]
                copies.append(pltpu.make_async_copy(here.at[lines], target, sems.at[at]))
                copies[-1].start()
            for copy in copies:
                copy.wait()

        return kernel

    moe_out = None
    for run, rows in ((0, keep), (1, received)):
        ins = [share, rows] + ([] if moe_out is None else [moe_out])
        (moe_out,) = call(
            mix(run),
            [shaped(length, wide)],
            *ins,
            scratch=[pltpu.VMEM((length, quarter), BF)],
            semaphores=4,
            far_in=(2,),
            far_out=(0,),
            aliases={2: 0} if run else None,
            flops=4 * length * first_rows * quarter,
        )
    return attended[None], moe_out[None]


def solution(mesh):
    rows = P(("groups", "side"), "blk", "tp")
    placed = (
        rows,
        rows,
        rows,
        P(("groups", "side"), "blk"),
        rows,
        P(("groups", "side"), "blk", None),
        P(("groups", "side"), "blk", None),
        P("blk", "tp", "side"),
        P("blk", "tp", "side"),
        P("blk", "side", "tp"),
    )
    return jax.shard_map(body, mesh=mesh, in_specs=placed, out_specs=(rows, rows), check_vma=False)
```

```python
import math

import jax
import jax.numpy as jnp
from jax import lax
from jax.experimental import pallas as pl
from jax.experimental.pallas import tpu as pltpu
from jax.sharding import PartitionSpec as P

HEAD_DIM = 128
CAP = 10
COST = 3_000_000_000
BF = jnp.bfloat16
F32 = jnp.float32
VMEM = pl.BlockSpec(memory_space=pltpu.VMEM)
HBM = pl.BlockSpec(memory_space=pltpu.HBM)


def swapped(value, axis, bit):
    count = lax.axis_size(axis)
    return lax.ppermute(value, axis, [(i, i ^ bit) for i in range(count)])


def up_to(value, step):
    return -(-value // step) * step


def call(kernel, outs, *ins, scratch=(), semaphores=0, far_in=(), far_out=(), aliases=None, flops=0, exps=0, grant=0):
    moved = sum(math.prod(a.shape) * a.dtype.itemsize for a in (*ins, *outs))
    held = sum(math.prod(s.shape) * s.dtype.itemsize for s in scratch)
    scratch = list(scratch) + ([pltpu.SemaphoreType.DMA((semaphores,))] if semaphores else [])
    return pl.pallas_call(
        kernel,
        out_shape=list(outs),
        in_specs=[HBM if i in far_in else VMEM for i in range(len(ins))],
        out_specs=[HBM if i in far_out else VMEM for i in range(len(outs))],
        scratch_shapes=scratch,
        input_output_aliases=aliases or {},
        compiler_params=pltpu.CompilerParams(vmem_limit_bytes=grant or 2 * moved + held + (2 << 20)),
        cost_estimate=pl.CostEstimate(flops=flops, bytes_accessed=0 if flops == 0 else moved, transcendentals=exps),
    )(*ins)


def shaped(rows, columns, dtype=BF):
    return jax.ShapeDtypeStruct((rows, columns), dtype)


def dot(a, b):
    return jnp.dot(a, b, preferred_element_type=F32)


def arranged(parts, pieces, rows):
    runs = []
    for which, to, start in sorted(pieces, key=lambda piece: piece[1]):
        if runs and runs[-1][0] == which and runs[-1][1] + runs[-1][3] == to and runs[-1][2] + runs[-1][3] == start:
            runs[-1][3] += CAP
        else:
            runs.append([which, to, start, CAP])
    out, at, width = [], 0, parts[0].shape[1]
    for which, to, start, count in runs + [[None, rows, 0, 0]]:
        if to > at:
            out.append(jnp.zeros((to - at, width), F32))
        if count:
            out.append(parts[which][start : start + count])
        at = to + count
    return jnp.concatenate(out, axis=0) if len(out) > 1 else out[0]


class Plan:
    def __init__(self, count, cuts):
        self.experts = count // 2
        self.bits = [1 << i for i in reversed(range(1, count.bit_length() - 1))]
        self.first = keep = [(0, d, c) for c in range(cuts) for d in range(self.experts)]
        send = [(0, d + self.experts, c) for _, d, c in keep]
        self.there = []
        for bit, later in zip(self.bits, self.bits[1:] + [1]):
            stage, keep, send = self.split(self.pool(keep, send, bit), lambda group: group[1] & later)
            self.there.append(stage)
        self.arrived = [(s, c) for s, _, c in keep]
        near = [s for s, c in self.arrived if c == 0]
        self.near, self.sources = near, near + [s ^ 1 for s in near]
        self.leaving = [(s, c) for c in range(cuts) for s in near]
        self.back = []
        pool = [(i, j, (s, i, c)) for i in range(2) for j, (s, c) in enumerate(self.leaving)]
        for bit in reversed(self.bits):
            stage, keep, send = self.split(pool, lambda group: group[0] & bit)
            self.back.append(stage)
            pool = self.pool(keep, send, bit)
        self.last = keep

    def pool(self, keep, send, bit):
        received = [(s ^ bit, d ^ bit, c) for s, d, c in send]
        return [(0, i, g) for i, g in enumerate(keep)] + [(1, i, g) for i, g in enumerate(received)]

    def split(self, pool, goes):
        stage, groups = ([], []), ([], [])
        for which, place, group in pool:
            side = 1 if goes(group) else 0
            stage[side].append((which, len(groups[side]) * CAP, place * CAP))
            groups[side].append(group)
        return stage, groups[0], groups[1]


def ranked(ids, weight, earlier, rows, here, groups):
    length = ids.shape[1]
    row = lax.broadcasted_iota(jnp.int32, (rows, 1), 0)
    expert = jnp.full((rows, 1), -1, jnp.int32)
    level = jnp.zeros((rows, 1), jnp.int32)
    for place, (_, target, _) in enumerate(groups):
        inside = (row >= place * CAP) & (row < (place + 1) * CAP)
        expert = jnp.where(inside, here ^ target, expert)
        level = jnp.where(inside, row - place * CAP, level)
    hits = jnp.zeros((rows, length), F32)
    share = jnp.zeros((rows, length), F32)
    for pick in range(ids.shape[0]):
        named = ids[pick : pick + 1, :] == expert
        hits = hits + jnp.where(named, 1.0, 0.0)
        if weight is not None:
            share = share + jnp.where(named, weight[pick : pick + 1, :], 0.0)
    ranks = dot(hits.astype(BF), earlier)
    chosen = (hits > 0.5) & (jnp.abs(ranks - level.astype(F32)) < 0.5)
    return jnp.where(chosen, 1.0 if weight is None else share, 0.0)


def cut_rows(matrix, groups, cut):
    row = lax.broadcasted_iota(jnp.int32, (matrix.shape[0], 1), 0)
    inside = jnp.zeros(row.shape, jnp.bool_)
    for place, (_, _, c) in enumerate(groups):
        if c == cut:
            inside = inside | ((row >= place * CAP) & (row < (place + 1) * CAP))
    return jnp.where(inside, matrix, 0.0).astype(BF)


def body(queries, key_rows, value_rows, segments, hidden_entry_rows, expert_ids, route_weight, w_gate, w_up, w_down):
    length = queries.shape[1]
    blocks, sides, cores = lax.axis_size("blk"), lax.axis_size("side"), lax.axis_size("tp")
    quarter, ff = w_gate.shape[1], w_gate.shape[2]
    cuts = next((c for c in (1, 2, 4) if blocks // 2 * CAP * c % 8 == 0 and quarter % (c * 128) == 0), 1)
    plan = Plan(blocks, cuts)
    experts, narrow = plan.experts, quarter // cuts
    ids, shares = expert_ids[0].T, route_weight[0].T
    picks = ids.shape[0]

    def columns_of(run, piece, pieces):
        place = ((lax.axis_index("blk") // experts) ^ run) * pieces + piece
        width = quarter // pieces
        return pl.ds(pl.multiple_of(place * width, width), width)

    def own_expert():
        return lax.axis_index("blk") % experts

    def over_side(value, offset, low):
        return swapped(value, ("blk", "side"), low * sides + offset)

    first_rows = up_to(len(plan.first) * CAP, 8)
    wide = hidden_entry_rows.shape[2]

    def before(before_ref):
        i = lax.broadcasted_iota(jnp.int32, (length, length), 0)
        j = lax.broadcasted_iota(jnp.int32, (length, length), 1)
        before_ref[...] = jnp.where(i < j, 1.0, 0.0).astype(BF)

    (earlier,) = call(before, [shaped(length, length)], flops=COST)

    whole_groups = plan.first[:experts]
    whole_rows = up_to(experts * CAP, 8)

    def rank(earlier_ref, ids_ref, out_ref):
        chosen = ranked(ids_ref[...], None, earlier_ref[...], whole_rows, own_expert(), whole_groups)
        out_ref[...] = chosen.astype(BF)

    (chosen,) = call(rank, [shaped(whole_rows, length)], earlier, ids)

    def choose(run):
        def kernel(chosen_ref, x_ref, out_ref):
            rows = dot(chosen_ref[...], x_ref[:, columns_of(run, 0, 1)])[: experts * CAP]
            pieces = [rows[:, cut * narrow : (cut + 1) * narrow] for cut in range(cuts)]
            if first_rows > cuts * experts * CAP:
                pieces.append(jnp.zeros((first_rows - cuts * experts * CAP, narrow), F32))
            out_ref[...] = jnp.concatenate(pieces, axis=0).astype(BF)

        return call(kernel, [shaped(first_rows, narrow)], chosen, hidden_entry_rows[0], flops=COST)[0]

    send, keep = choose(1), choose(0)

    def share_out(earlier_ref, ids_ref, weight_ref, share_ref):
        share = ranked(ids_ref[...], weight_ref[...], earlier_ref[...], first_rows, own_expert(), plan.last)
        for cut in range(cuts):
            share_ref[cut] = cut_rows(share, plan.last, cut).astype(F32).T.astype(BF)

    (share,) = call(share_out, [jax.ShapeDtypeStruct((cuts, length, first_rows), BF)], earlier, ids, shares)

    def pack(after_ref, key_ref, value_ref, segment_ref, held_ref, segment_here, sems):
        copies = [
            pltpu.make_async_copy(key_ref, held_ref.at[0, pl.ds(0, length)], sems.at[0]),
            pltpu.make_async_copy(value_ref, held_ref.at[0, pl.ds(length, length)], sems.at[1]),
            pltpu.make_async_copy(segment_ref, segment_here, sems.at[2]),
        ]
        for copy in copies:
            copy.start()
        copies[2].wait()
        labels = jnp.broadcast_to(segment_here[...].astype(F32), (16, length))
        held_ref[0, 2 * length : 2 * length + 16, :] = labels.astype(BF)
        copies[0].wait()
        copies[1].wait()

    (held,) = call(
        pack,
        [jax.ShapeDtypeStruct((1, 2 * length + 16, HEAD_DIM), BF)],
        send,
        key_rows[0],
        value_rows[0],
        segments,
        scratch=[pltpu.VMEM((1, length), jnp.int32)],
        semaphores=3,
        far_in=(1, 2, 3),
    )

    def sort(stage, *parts):
        sizes = [up_to(len(pieces) * CAP, 8) for pieces in stage]

        def kernel(*refs):
            values = [ref[...].astype(F32) for ref in refs[: len(parts)]]
            for pieces, size, out in zip(stage, sizes, refs[len(parts) :]):
                out[...] = arranged(values, pieces, size).astype(BF)

        return call(
            kernel,
            [shaped(size, narrow) for size in sizes],
            *parts,
            flops=COST,
        )

    for bit, stage in zip(plan.bits, plan.there):
        received, held = lax.optimization_barrier((swapped(send, "blk", bit), held))
        keep, send = sort(stage, keep, received)
    part_rows = len(plan.near) * CAP
    padded = keep.shape[0]
    own = [keep] + [over_side(keep, offset, 0) for offset in range(1, sides)]
    other = [over_side(send, offset, 1) for offset in range(sides)]

    held, _ = lax.optimization_barrier((held, keep))
    nearby = [1 << i for i in reversed(range(blocks.bit_length() - 1))]
    order = [0]
    received_held = swapped(held, "blk", nearby[0])

    def join(after_ref, held_ref, received_ref, both_ref):
        both_ref[: held_ref.shape[0]] = held_ref[...]
        both_ref[held_ref.shape[0] :] = received_ref[...]

    def joined(after, held, received_held, flops):
        both = jax.ShapeDtypeStruct((2 * held.shape[0], *held.shape[1:]), BF)
        return call(join, [both], after, held, received_held, flops=flops)[0]

    side_rows = 2 * part_rows

    half = sides // 2 * side_rows

    def by_source(build):
        here = build(lambda source: plan.near.index(source) * CAP)
        there = build(lambda source: plan.near.index(source ^ experts) * CAP)
        return jnp.where(lax.axis_index("blk") >= experts, there, here)

    def project(*refs):
        own_refs, other_refs, (gate_ref, up_ref, *out_refs) = refs[:sides], refs[sides : 2 * sides], refs[2 * sides :]
        mine = lax.axis_index("tp") == 0
        away, stay = [], []
        for refs_of in (own_refs, other_refs):
            for at in range(sides // 2):
                low, high = refs_of[at][...].astype(F32), refs_of[sides // 2 + at][...].astype(F32)
                away.append(jnp.where(mine, high, low))
                stay.append(jnp.where(mine, low, high))

        def build(row_of, rows, cut):
            pieces = []
            for part in range(2):
                for at in range(sides // 2):
                    for place, (source, c) in enumerate(plan.arrived):
                        if c == cut:
                            to = at * side_rows + part * part_rows + row_of(source)
                            pieces.append((part * (sides // 2) + at, to, place * CAP))
            return arranged(rows, pieces, half)

        both = jnp.concatenate(
            [
                jnp.concatenate([by_source(lambda row_of: build(row_of, rows, cut)) for cut in range(cuts)], axis=1)
                for rows in (away, stay)
            ],
            axis=0,
        ).astype(BF)
        for weight, send_ref, keep_ref in ((gate_ref, *out_refs[:2]), (up_ref, *out_refs[2:])):
            terms = dot(both, weight[...])
            send_ref[...] = terms[:half].astype(BF)
            keep_ref[...] = terms[half:]

    gate_send, gate_keep, up_send, up_keep = call(
        project,
        [shaped(half, ff), shaped(half, ff, F32)] * 2,
        *own,
        *other,
        w_gate[0],
        w_up[0],
    )
    gate_received, up_received = swapped(gate_send, "tp", 1), swapped(up_send, "tp", 1)

    def add_terms(gate_keep_ref, gate_received_ref, up_keep_ref, up_received_ref, sum_ref, send_ref):
        for at, keep_ref, received_ref in ((0, gate_keep_ref, gate_received_ref), (ff, up_keep_ref, up_received_ref)):
            total = keep_ref[...] + received_ref[...].astype(F32)
            sum_ref[:, at : at + ff] = total
            send_ref[:, at : at + ff] = total.astype(BF)

    sums, sums_send = call(
        add_terms,
        [shaped(half, 2 * ff, F32), shaped(half, 2 * ff)],
        gate_keep,
        gate_received,
        up_keep,
        up_received,
    )
    sums_received = swapped(sums_send, "blk", experts)
    for bit in nearby[1:]:
        held = joined(sums_send, held, received_held, COST)
        received_held = swapped(held, "blk", bit)
    held = joined(sums_send, held, received_held, 0)
    for bit in nearby:
        order = order + [place ^ bit for place in order]

    def activate(sum_ref, received_ref, hidden_ref):
        gate = sum_ref[:, :ff] + received_ref[:, :ff].astype(F32)
        up = sum_ref[:, ff:] + received_ref[:, ff:].astype(F32)
        hidden_ref[...] = (gate / (1.0 + jnp.exp(-gate)) * up).astype(BF)

    (hidden,) = call(activate, [shaped(half, ff)], sums, sums_received, exps=half * ff)
    hidden_received = swapped(hidden, "tp", 1)

    def project_back(hidden_ref, received_ref, down_ref, *out_refs):
        mine = lax.axis_index("tp") == 0
        here, there = hidden_ref[...].astype(F32), received_ref[...].astype(F32)
        ordered = [jnp.where(mine, here, there), jnp.where(mine, there, here)]
        spaced = up_to(part_rows, 8)

        def build(row_of):
            pieces = []
            for at in range(sides):
                for part in range(2):
                    for place, source in enumerate(plan.near):
                        to = (2 * at + part) * spaced + place * CAP
                        start = at % (sides // 2) * side_rows + part * part_rows + row_of(source)
                        pieces.append((at // (sides // 2), to, start))
            return arranged(ordered, pieces, 2 * sides * spaced)

        total = by_source(build)
        out = dot(total.astype(BF), down_ref[...])
        for place, out_ref in enumerate(out_refs):
            rows = out[place * spaced : place * spaced + part_rows]
            pieces = [rows[:, cut * narrow : (cut + 1) * narrow] for cut in range(cuts)]
            out_ref[...] = jnp.concatenate(pieces, axis=0).astype(out_ref.dtype)

    outs = call(
        project_back,
        [shaped(padded, narrow, BF if place else F32) for place in range(2 * sides)],
        hidden,
        hidden_received,
        w_down[0],
        flops=4 * half * ff * quarter,
    )
    other = [over_side(outs[2 * offset + 1], offset, 1) for offset in reversed(range(sides))][::-1]
    own = [outs[0]] + [over_side(outs[2 * offset], offset, 0) for offset in range(1, sides)]

    heads = queries.shape[2] // HEAD_DIM
    factor = math.log2(math.e) / math.sqrt(HEAD_DIM)
    span = blocks * length
    batch = math.gcd(heads, 4)

    def attend(query_ref, held_ref, segment_ref, out_ref, keys, values, bias, done, sems):
        here = lax.axis_index("blk")
        i = lax.broadcasted_iota(jnp.int32, (length, length), 0)
        j = lax.broadcasted_iota(jnp.int32, (length, length), 1)
        label_here = jnp.sum(jnp.where(i == j, segment_ref[...].astype(F32), 0.0), axis=1, keepdims=True)
        for place, other_block in enumerate(order):
            at = place * length
            keys[at : at + length, :] = held_ref[place, :length, :]
            values[at : at + length, :HEAD_DIM] = held_ref[place, length : 2 * length, :]
            label = held_ref[place, 2 * length : 2 * length + 16, :].astype(F32)[:1]
            same = label_here == label
            if other_block == 0:
                seen = same & (j <= i)
            else:
                seen = same & ((here ^ other_block) < here)
            bias[:, at : at + length] = jnp.where(seen, 0.0, -1e30)

        values[:, HEAD_DIM:] = jnp.ones((span, HEAD_DIM), BF)

        def one_head(head):
            columns = pl.ds(pl.multiple_of(head * HEAD_DIM, HEAD_DIM), HEAD_DIM)
            scores = lax.dot_general(
                query_ref[:, columns], keys[...], (((1,), (1,)), ((), ())), preferred_element_type=F32
            )
            scores = scores + bias[...]
            weights = jnp.exp2((scores - jnp.max(scores, axis=1, keepdims=True)) * factor)
            out = dot(weights.astype(BF), values[...])
            done[:, columns] = (out[:, :HEAD_DIM] / out[:, HEAD_DIM:]).astype(BF)

        def copied(first):
            columns = pl.ds(first * HEAD_DIM, batch * HEAD_DIM)
            return pltpu.make_async_copy(done.at[:, columns], out_ref.at[:, columns], sems.at[first // batch])

        if span <= 1024:
            for head in range(heads):
                one_head(head)
                if (head + 1) % batch == 0:
                    copied(head + 1 - batch).start()
        else:
            lax.fori_loop(0, heads, lambda head, _: (one_head(head), 0)[1], 0)
            for first in range(0, heads, batch):
                copied(first).start()
        for first in range(0, heads, batch):
            copied(first).wait()

    segments_then, _ = lax.optimization_barrier((segments, outs[1]))
    (attended,) = call(
        attend,
        [shaped(length, heads * HEAD_DIM)],
        queries[0],
        held,
        segments_then,
        scratch=[
            pltpu.VMEM((span, HEAD_DIM), BF),
            pltpu.VMEM((span, 2 * HEAD_DIM), BF),
            pltpu.VMEM((length, span), F32),
            pltpu.VMEM((length, heads * HEAD_DIM), BF),
        ],
        semaphores=heads // batch,
        far_out=(0,),
    )
    own, other, attended = lax.optimization_barrier((own, other, attended))

    def add_parts(*refs):
        sums = []
        for part in (refs[:sides], refs[sides : 2 * sides]):
            total = part[0][...].astype(F32)
            for ref in part[1:]:
                total = total + ref[...].astype(F32)
            sums.append(total)
        for pieces, out in zip(plan.back[0], refs[2 * sides :]):
            out[...] = arranged(sums, pieces, out.shape[0]).astype(BF)

    keep, send = call(
        add_parts,
        [shaped(up_to(len(pieces) * CAP, 8), narrow) for pieces in plan.back[0]],
        *own,
        *other,
        flops=8 * padded * padded * quarter,
    )
    for bit, stage in zip(plan.bits[::-1], plan.back[1:]):
        keep, send = sort(stage, keep, swapped(send, "blk", bit))
    received = swapped(send, "blk", plan.bits[0])

    def mix(run):
        def kernel(share_ref, rows_ref, *refs):
            out_ref, here, sems = refs[-3:]
            copies = []
            for at in range(4):
                cut, within = at * cuts // 4, at % (4 // cuts)
                rows = rows_ref[:, within * (quarter // 4) : (within + 1) * (quarter // 4)]
                here[at] = dot(share_ref[cut], rows).astype(BF)
                target = out_ref.at[:, columns_of(run, at, 4)]
                copies.append(pltpu.make_async_copy(here.at[at], target, sems.at[at]))
                copies[-1].start()
            for copy in copies:
                copy.wait()

        return kernel

    moe_out = None
    for run, rows in ((0, keep), (1, received)):
        ins = [share, rows] + ([] if moe_out is None else [moe_out])
        (moe_out,) = call(
            mix(run),
            [shaped(length, wide)],
            *ins,
            scratch=[pltpu.VMEM((4, length, quarter // 4), BF)],
            semaphores=4,
            far_in=(2,),
            far_out=(0,),
            aliases={2: 0} if run else None,
            flops=4 * length * first_rows * quarter,
        )
    return attended[None], moe_out[None]


def solution(mesh):
    rows = P(("groups", "side"), "blk", "tp")
    placed = (
        rows,
        rows,
        rows,
        P(("groups", "side"), "blk"),
        rows,
        P(("groups", "side"), "blk", None),
        P(("groups", "side"), "blk", None),
        P("blk", "tp", "side"),
        P("blk", "tp", "side"),
        P("blk", "side", "tp"),
    )
    return jax.shard_map(body, mesh=mesh, in_specs=placed, out_specs=(rows, rows), check_vma=False)
```
